128 devices in a mesh: gx: 4 (over x), gy: 4 (over y), gz: 8 (over z, core).
Axes of the slice: x: 4, y: 4, z: 4, core: 2. Of those that a mesh axis runs over, the one named last changes fastest.
Arguments:
- source: float32 [128, 128, 512], P('gz', 'gx', 'gy'), may hold values from -24 to 24
- conductivity: float32 [128, 128, 512], P('gz', 'gx', 'gy'), may hold values from 1 to 10
- cell_kind: int32 [128, 128, 512], P('gz', 'gx', 'gy'), may hold values from 0 to 2
Outputs:
- potential: float32 [128, 128, 512], P('gz', 'gx', 'gy')
- residual: float32 [128, 128, 512], P('gz', 'gx', 'gy')
The draws below stay inside these ranges and needn't reach their ends.
All inputs are finite; a program needn't handle non-finite values.
Results may differ from the reference program's by a relative error of at most 0.0003.
Values sent between devices are 32-bit elements; how exact they have to be, the bound alone decides.
No kernel may reach another device: no remote copies, remote signals or barrier semaphores. Data moves between devices by JAX's collectives and lax.ppermute only.
A program may use at most 128 MiB of HBM per device.

```python
import math
import jax
import jax.numpy as jnp
from jax import lax

LEVELS = 4
PRE = 4
POST = 4
CSWEEPS = 32
NZ = 128
NX = 128
NY = 512


def smooth_field(phase):
    height = jnp.arange(NZ, dtype=jnp.float32)[:, None, None] / NZ
    across = jnp.arange(NX, dtype=jnp.float32)[None, :, None] / NX
    along = jnp.arange(NY, dtype=jnp.float32)[None, None, :] / NY
    wave = jnp.sin(6.2831853 * across + phase) * jnp.cos(6.2831853 * along - 0.5 * phase)
    return 3.0 * wave + 2.0 * jnp.cos(3.1415927 * height) + 1.0


def draw_source(key, part):
    key = jax.random.fold_in(key, 11)
    phase_key, rough_key = jax.random.split(key)
    phase = jax.random.uniform(phase_key, (), jnp.float32, 0.0, 6.2831853)
    rough = jnp.clip(jax.random.normal(rough_key, (NZ, NX, NY), jnp.float32), -4.0, 4.0)
    return 2.5 * rough + smooth_field(phase)


def draw_cell_kind(key, part):
    key = jax.random.fold_in(key, 5)
    drawn = jax.random.randint(key, (NZ, NX, NY), 0, 1024)
    return jnp.where(drawn < 128, 0, jnp.where(drawn == 128, 2, 1)).astype(jnp.int32)


def shard_levels(stream_key, shape, cuts, least, top_value):
    def one(axis_at, parts):
        steps = jax.random.uniform(jax.random.fold_in(jax.random.fold_in(stream_key, 6), axis_at), (parts,), jnp.float32, least / len(cuts), top_value / len(cuts))
        return jnp.repeat(jnp.exp(steps), shape[axis_at] // parts).reshape((-1,) + (1,) * (len(shape) - axis_at - 1))

    level = one(*cuts[0])
    for cut in cuts[1:]:
        level = level * one(*cut)
    return level


def setup_inputs(seed: int = 0) -> dict:
    streams_of = jax.random.split(jax.random.key(seed), 4)
    return {
        "source": draw_source(jax.random.fold_in(streams_of[3], 71), 0),
        "conductivity": jnp.clip(jnp.exp(math.log(10.0) - 2.3025851 * jax.random.uniform(streams_of[1], (NZ, NX, NY), jnp.float32) ** shard_levels(streams_of[1], (NZ, NX, NY), ((0, 8), (1, 4), (2, 4)), -0.2, 0.2)), 1.0, 10.0),
        "cell_kind": draw_cell_kind(jax.random.fold_in(streams_of[3], 71), 0),
    }


damping_factor = 0.8
vertical_weight = 4.0
shift_term = 0.005
surface_term = 8.0
dry_term = 0.02
face_weights = (vertical_weight, vertical_weight, 1.0, 1.0, 1.0, 1.0)


def fold_cells(values):
    height, across, along = values.shape
    return values.reshape(height // 2, 2, across // 2, 2, along // 2, 2).sum(axis=(1, 3, 5))


def spread_cells(values):
    height, across, along = values.shape
    spread_out = jnp.broadcast_to(values[:, None, :, None, :, None], (height, 2, across, 2, along, 2))
    return spread_out.reshape(height * 2, across * 2, along * 2)


def neighbours(padded):
    return [padded[:-2, 1:-1, 1:-1], padded[2:, 1:-1, 1:-1],
            padded[1:-1, :-2, 1:-1], padded[1:-1, 2:, 1:-1],
            padded[1:-1, 1:-1, :-2], padded[1:-1, 1:-1, 2:]]


def couplings_of(stiffness, padded_stiffness):
    return [weight * jnp.minimum(stiffness, beside) for weight, beside in zip(face_weights, neighbours(padded_stiffness))]


def diagonal_of(mass, couplings):
    diagonal = mass
    for coupling in couplings:
        diagonal = diagonal + coupling
    return diagonal


def apply_operator(potential, padded_potential, couplings, diagonal):
    applied = diagonal * potential
    for coupling, beside in zip(couplings, neighbours(padded_potential)):
        applied = applied - coupling * beside
    return applied


def operator_apply(potential, operator):
    stiffness, padded_stiffness, diagonal = operator
    couplings = couplings_of(stiffness, padded_stiffness)
    return apply_operator(potential, jnp.pad(potential, 1), couplings, diagonal)


def relax(potential, forcing, operator):
    applied = operator_apply(potential, operator)
    return potential + damping_factor * (forcing - applied) / operator[2]


def cycle(level_index, forcing, operators):
    operator = operators[level_index]
    potential = jnp.zeros_like(forcing)
    if level_index == len(operators) - 1:
        def sweep(step_index, current):
            return relax(current, forcing, operator)
        return lax.fori_loop(0, CSWEEPS, sweep, potential)
    for sweep_index in range(PRE):
        potential = relax(potential, forcing, operator)
    remainder = forcing - operator_apply(potential, operator)
    correction = cycle(level_index + 1, fold_cells(remainder), operators)
    potential = potential + spread_cells(correction)
    for sweep_index in range(POST):
        potential = relax(potential, forcing, operator)
    return potential


def reference(source, conductivity, cell_kind):
    wet = jnp.where(cell_kind > 0, 1.0, 0.0).astype(source.dtype)
    surface = jnp.where(cell_kind == 2, 1.0, 0.0).astype(source.dtype)
    stiffness = conductivity * wet
    mass = shift_term * stiffness + surface_term * stiffness * surface + dry_term * (1.0 - wet)
    forcing = source * wet
    operators = []
    for level_index in range(LEVELS + 1):
        padded_stiffness = jnp.pad(stiffness, 1)
        diagonal = diagonal_of(mass, couplings_of(stiffness, padded_stiffness))
        operators.append((stiffness, padded_stiffness, diagonal))
        if level_index < LEVELS:
            stiffness = 0.25 * fold_cells(stiffness)
            mass = fold_cells(mass)
    potential = cycle(0, forcing, operators)
    residual = forcing - operator_apply(potential, operators[0])
    return potential, residual
```

```python
import math

import jax
import jax.numpy as jnp
from jax import lax
from jax.experimental import pallas as pl
from jax.experimental.pallas import tpu as pltpu
from jax.sharding import PartitionSpec as P

CSWEEPS = 32
DAMP = 0.8
KEEP = 1.0 - DAMP
W0 = 5
W1 = 7
G1 = 6
S1, F1 = 11, 10
Z0, X0, Y0 = 16, 32, 128
Z1, X1, Y1 = 8, 16, 64
ZT0, XT0 = Z0 + 2 * W0, 48
ZT1, XT1 = Z1 + 2 * W1, 40
LANES = 128
MIB = 1024 * 1024
F32 = jnp.float32


def lane_of(shape):
    return lax.broadcasted_iota(jnp.int32, shape, len(shape) - 1)


def row_of(shape):
    return lax.broadcasted_iota(jnp.int32, shape, len(shape) - 2)


def roll(x, shift, axis):
    size = x.shape[axis]
    shift = shift % size
    return x if shift == 0 else pltpu.roll(x, shift, axis)


def loop(first, last, body, step):
    chunks = (last - first) // step

    def chunk(c, carry):
        for k in range(step):
            body(first + c * step + k)
        return carry

    if chunks > 1:
        lax.fori_loop(0, chunks, chunk, 0)
    elif chunks:
        chunk(0, 0)
    for z in range(first + chunks * step, last):
        body(z)


def pick(x, index):
    return jnp.take_along_axis(x, index, axis=1)


def fold_lanes(x, first, count, target):
    to = lane_of(x.shape) - target
    index = (first + 2 * to) % LANES
    pairs = pick(x, index) + pick(x, (index + 1) % LANES)
    return jnp.where((to >= 0) & (to < count // 2), pairs, 0.0)


def spread_lanes(x, first=0):
    return pick(x, first + lane_of(x.shape) // 2)


class Far:
    def __init__(self, ins, outs, late):
        self.ins = {k: pltpu.make_async_copy(*pair) for k, pair in ins.items()}
        self.outs = {k: pltpu.make_async_copy(*pair) for k, pair in outs.items()}
        self.started = []
        self.start(*[k for k in self.ins if k not in late])

    def start(self, *keys):
        for k in keys:
            self.ins[k].start()

    def wait(self, *keys):
        for k in keys or tuple(self.ins):
            self.ins.pop(k).wait()

    def flush(self, *keys):
        for k in keys:
            self.outs[k].start()
            self.started.append(k)

    def finish(self):
        self.flush(*[k for k in self.outs if k not in self.started])
        for copy in self.outs.values():
            copy.wait()


def padded(shape):
    plane = 4 * math.prod(shape[1:])
    return (max(shape[0], -(-7 * MIB // plane)), *shape[1:])


def call(body, outs, scratch, *args, place=None, far_in={}, far_out=(), late=(), grant=48):
    shapes = [
        jax.ShapeDtypeStruct(padded(shape) if k in far_out else shape, F32)
        for k, shape in enumerate(outs)
    ]
    vmem = pl.BlockSpec(memory_space=pltpu.VMEM)
    hbm = pl.BlockSpec(memory_space=pltpu.HBM)
    specs = [hbm if k in far_in else vmem for k in range(len(args))]
    out_specs = [hbm if k in far_out else vmem for k in range(len(outs))]
    held = [pltpu.VMEM(shape, F32) for shape in far_in.values()]
    held += [pltpu.VMEM(outs[k], F32) for k in far_out]
    extra = len(far_in) + len(far_out)
    if extra:
        held.append(pltpu.SemaphoreType.DMA((extra,)))
    placed = place is not None
    count = len(args)

    def wrapped(*refs):
        refs = list(refs)
        head = [refs.pop(0)] if placed else []
        ins, results = refs[:count], refs[count : count + len(outs)]
        rest = refs[count + len(outs) :]
        mine, rest = rest[: len(scratch)], rest[len(scratch) :]
        copies_in, copies_out = {}, {}
        for j, k in enumerate(far_in):
            copies_in[k] = (ins[k].at[0 : far_in[k][0]], rest[j], rest[extra].at[j])
            ins[k] = rest[j]
        for j, k in enumerate(far_out, len(far_in)):
            copies_out[k] = (rest[j], results[k].at[0 : outs[k][0]], rest[extra].at[j])
            results[k] = rest[j]
        far = Far(copies_in, copies_out, late)
        body(far, *head, *ins, *results, *mine)
        far.finish()

    if placed:
        specs = [pl.BlockSpec(memory_space=pltpu.SMEM)] + specs
        args = (place,) + args
    return pl.pallas_call(
        wrapped,
        out_shape=shapes,
        in_specs=specs,
        out_specs=out_specs,
        scratch_shapes=[pltpu.VMEM(shape, F32) for shape in scratch] + held,
        compiler_params=pltpu.CompilerParams(vmem_limit_bytes=grant * MIB),
    )(*args)


class Item:
    def __init__(self, fields, planes, rows, rows_out, width, kind, trim=False, width_z=None, edge=0):
        self.n, self.z, self.x, self.xt, self.w, self.kind = fields, planes, rows, rows_out, width, kind
        self.wz = width if width_z is None else width_z
        self.zt = planes + 2 * self.wz
        self.edge = edge
        self.trim = trim
        self.tall = rows + 8 if trim else rows_out
        self.virtual = 2 * fields if kind == "pair" else fields
        self.own = LANES if kind == "full" else LANES // 2
        self.slots = LANES // width
        self.groups = -(-self.virtual * (self.zt - 2 * edge) // self.slots)
        self.rows_x = fields * planes * width
        self.rows_z = fields * self.wz * self.tall
        self.rows_y = self.groups * self.tall

    def narrow(self, plane):
        if not self.trim:
            return plane
        upper, lower = plane[self.x : self.x + 8], plane[self.xt - 8 : self.xt]
        rim = jnp.where(row_of(upper.shape) < 4, upper, lower)
        return jnp.concatenate([plane[: self.x], rim], axis=0)

    def widen(self, plane):
        if not self.trim:
            return plane
        rim = plane[self.x :]
        upper = jnp.where(row_of(rim.shape) < 4, rim, 0.0)
        return jnp.concatenate([plane[: self.x], upper, rim - upper], axis=0)


def total(counts):
    count = sum(counts)
    return -(-count // 8) * 8


def pack_x(items, refs, low, high):
    at = 0
    for item, ref in zip(items, refs):
        for n in range(item.n):
            for z in range(item.z):
                low[at : at + item.w, :] = ref[n, z, 0 : item.w, :]
                high[at : at + item.w, :] = ref[n, z, item.x - item.w : item.x, :]
                at += item.w


def unpack_x(items, refs, from_low, from_high, outs):
    at = 0
    for item, ref, out in zip(items, refs, outs):
        out[:, :, item.x :, :] = jnp.zeros((item.n, item.z, item.xt - item.x, LANES), F32)
        for n in range(item.n):
            for z in range(item.z):
                out[n, z, 0 : item.x, :] = ref[n, z]
                out[n, z, item.x : item.x + item.w, :] = from_high[at : at + item.w, :]
                out[n, z, item.xt - item.w :, :] = from_low[at : at + item.w, :]
                at += item.w


def pack_z(items, refs, low, high):
    at = 0
    for item, ref in zip(items, refs):
        for n in range(item.n):
            for w in range(item.wz):
                low[at : at + item.tall, :] = item.narrow(ref[n, w])
                high[at : at + item.tall, :] = item.narrow(ref[n, item.z - item.wz + w])
                at += item.tall


def unpack_z(items, refs, from_low, from_high, outs):
    at = 0
    for item, ref, out in zip(items, refs, outs):
        for n in range(item.n):
            for w in range(item.wz):
                out[n, w] = item.widen(from_low[at : at + item.tall, :])
                out[n, item.wz + item.z + w] = item.widen(from_high[at : at + item.tall, :])
                at += item.tall
            for z in range(item.z):
                out[n, item.wz + z] = ref[n, z]


def pack_y(items, refs, low, high):
    at = 0
    for item, ref in zip(items, refs):
        lane = lane_of((item.tall, LANES))
        pairs = [(v, z) for v in range(item.virtual) for z in range(item.edge, item.zt - item.edge)]
        for g in range(item.groups):
            lows = jnp.zeros((item.tall, LANES), F32)
            highs = lows
            for k, (v, z) in enumerate(pairs[g * item.slots : (g + 1) * item.slots]):
                n, first = (v // 2, (v % 2) * item.own) if item.kind == "pair" else (v, 0)
                plane = item.narrow(ref[n, z])
                place = k * item.w
                mask = (lane >= place) & (lane < place + item.w)
                lows = jnp.where(mask, roll(plane, place - first, 1), lows)
                highs = jnp.where(mask, roll(plane, place - first - item.own + item.w, 1), highs)
            low[at : at + item.tall, :] = lows
            high[at : at + item.tall, :] = highs
            at += item.tall


def unpack_y(items, refs, from_low, from_high, outs):
    at = 0
    for item, ref, fields in zip(items, refs, outs):
        lane = lane_of((item.tall, LANES))
        for v in range(item.virtual if item.edge else 0):
            for z in [*range(item.edge), *range(item.zt - item.edge, item.zt)]:
                fields[v][z, :, 0:LANES] = ref[v, z]
                fields[v][z, :, LANES:] = jnp.zeros((item.xt, LANES), F32)
        pairs = [(v, z) for v in range(item.virtual) for z in range(item.edge, item.zt - item.edge)]
        for g in range(item.groups):
            lows = from_low[at : at + item.tall, :]
            highs = from_high[at : at + item.tall, :]
            at += item.tall
            for k, (v, z) in enumerate(pairs[g * item.slots : (g + 1) * item.slots]):
                place = k * item.w
                start = item.own % LANES
                upper = roll(highs, start - place, 1)
                lower = roll(lows, LANES - item.w - place, 1)
                rim = jnp.where(
                    lane < start + item.w, upper, jnp.where(lane >= LANES - item.w, lower, 0.0)
                )
                if item.kind == "full":
                    fields[v][z, :, 0:LANES] = ref[v, z]
                    fields[v][z, :, LANES:] = item.widen(rim)
                else:
                    plane = ref[v // 2, z] if item.kind == "pair" else ref[v, z]
                    if item.kind == "pair" and v % 2:
                        plane = roll(plane, item.own, 1)
                    fields[v][z] = jnp.where(lane < item.own, plane, rim)


def shift(low, high, axis):
    count = lax.axis_size(axis)
    forward = [(i, i + 1) for i in range(count - 1)]
    backward = [(target, source) for source, target in forward]
    return lax.ppermute(high, axis, forward), lax.ppermute(low, axis, backward)


def exchange(items, arrays, low, high):
    count = len(items)
    from_low, from_high = shift(low, high, "gx")
    shapes = [(item.n, item.z, item.xt, LANES) for item in items]
    message = (total(item.rows_z for item in items), LANES)

    def after_x(far, *refs):
        ins, (a, b), outs, (c, d) = refs[:count], refs[count : count + 2], refs[count + 2 : 2 * count + 2], refs[2 * count + 2 :]
        unpack_x(items, ins, a, b, outs)
        pack_z(items, outs, c, d)

    *arrays, low, high = call(after_x, shapes + [message] * 2, [], *arrays, from_low, from_high)
    from_low, from_high = shift(low, high, "gz")
    shapes = [(item.n, item.zt, item.xt, LANES) for item in items]
    message = (total(item.rows_y for item in items), LANES)

    def after_z(far, *refs):
        ins, (a, b), outs, (c, d) = refs[:count], refs[count : count + 2], refs[count + 2 : 2 * count + 2], refs[2 * count + 2 :]
        unpack_z(items, ins, a, b, outs)
        pack_y(items, outs, c, d)

    *arrays, low, high = call(after_z, shapes + [message] * 2, [], *arrays, from_low, from_high)
    from_low, from_high = shift(low, high, "gy")
    return arrays, from_low, from_high


STIFFNESS = Item(1, Z0, X0, XT0, W0, "full", True, edge=1)
INNER = Item(1, Z0, X0, XT0, W0 - 1, "full", True)
COARSE = Item(1, Z1, X1, XT1, S1, "pair", False, W1)
FORCING1 = Item(1, Z1, X1, XT1, F1, "half", False, G1)
POTENTIAL0 = Item(1, Z0, X0, XT0, W0, "full", False, 0)
FIRST, SECOND = (STIFFNESS, INNER, INNER, COARSE), (FORCING1, POTENTIAL0)


def x_message(items):
    return (total(item.rows_x for item in items), LANES)


def couple(s, m, r, cx, cy, cz, first, last, step, edges=False, start=None):
    planes, rows, lanes = s.shape

    def vertical(z):
        return 4.0 * jnp.minimum(s[z], s[z + 1])

    def one(z, below, above):
        here = s[z]
        x_face = jnp.minimum(here, roll(here, -1, 0))
        y_face = jnp.minimum(here, roll(here, -1, 1))
        if edges:
            x_face = jnp.where(row_of(here.shape) < rows - 1, x_face, 0.0)
            y_face = jnp.where(lane_of(here.shape) < lanes - 1, y_face, 0.0)
        cx[z] = x_face
        cy[z] = y_face
        cz[z] = above
        d = m[z] + below + above + x_face + roll(x_face, 1, 0) + y_face + roll(y_face, 1, 1)
        scale = DAMP / jnp.where(d > 0.0, d, 1.0)
        r[z] = scale
        if start:
            start[1][z] = scale * start[0][z]

    if edges:
        zero = jnp.zeros((rows, lanes), F32)
        one(0, zero, vertical(0))
        one(planes - 1, vertical(planes - 2), zero)
    else:
        cz[first - 1] = vertical(first - 1)
    loop(first + edges, last - edges, lambda z: one(z, vertical(z - 1), vertical(z)), step)


def gathered(v, f, cx, cy, cz, z, low=True, high=True):
    here = v[z]
    x_face, y_face = cx[z], cy[z]
    out = f[z]
    if high:
        out = out + cz[z] * v[z + 1]
    if low:
        out = out + cz[z - 1] * v[z - 1]
    out = out + x_face * roll(here, -1, 0) + roll(x_face * here, 1, 0)
    return here, out + y_face * roll(here, -1, 1) + roll(y_face * here, 1, 1)


def sweep(v, into, op, first, last, unroll, edges=False):
    r, f, cx, cy, cz = op

    def step(z, low=True, high=True):
        here, out = gathered(v, f, cx, cy, cz, z, low, high)
        into[z] = KEEP * here + r[z] * out

    if edges:
        step(first, low=False)
        step(last - 1, high=False)
        loop(first + 1, last - 1, step, unroll)
    else:
        loop(first, last, step, unroll)


def remain(v, op, z, low=True, high=True):
    r, f, cx, cy, cz = op
    here, out = gathered(v, f, cx, cy, cz, z, low, high)
    return out - here * (DAMP / r[z])


def first_sweep(v, op, first, last):
    r, f = op[:2]

    def step(z):
        v[z] = r[z] * f[z]

    loop(first, last, step, 4)


def prepare(far, stiffness, forcing, mass, coarse, low, high, tall):
    out = None
    for ref, scale, target in ((stiffness, 0.25, 0), (mass, 1.0, Y1)):
        for z in range(Z1):
            tall[z * X0 : (z + 1) * X0, :] = ref[0, 2 * z] + ref[0, 2 * z + 1]
        rows = tall[pl.ds(0, Z1 * X1, stride=2), :] + tall[pl.ds(1, Z1 * X1, stride=2), :]
        part = scale * fold_lanes(rows, 0, LANES, target)
        out = part if out is None else out + part
    for z in range(Z1):
        coarse[0, z] = out[z * X1 : (z + 1) * X1, :]
    pack_x(FIRST, (stiffness, forcing, mass, coarse), low, high)


def prepare_coarse(far, coarse, packed2, tall):
    for part, scale in ((0, 0.25), (1, 1.0)):
        packed2[part * 8 : part * 8 + 8, :] = scale * pack_coarse(
            lambda z: coarse[0, z], part * Y1, tall
        )


def pack_coarse(plane, first, tall):
    for z in range(Z1 // 2):
        tall[z * X1 : (z + 1) * X1, :] = plane(2 * z) + plane(2 * z + 1)
    count = Z1 // 2 * X1 // 2
    rows = tall[pl.ds(0, count, stride=2), :] + tall[pl.ds(1, count, stride=2), :]
    out = jnp.zeros((X1 // 2, LANES), F32)
    for z in range(Z1 // 2):
        part = rows[z * X1 // 2 : (z + 1) * X1 // 2, :]
        out = out + fold_lanes(part, first, Y1, z * Y1 // 2)
    return out


def parts(ref, planes, count=5):
    return [ref.at[k * planes : (k + 1) * planes] for k in range(count)]


def presmooth0(
    far, zx_s, zx_f, zx_m, zx_coarse, from_low, from_high,
    v_own, g_own, op, s1, m1, low, high,
    s, m, va, vb, tall,
):
    r, f, cx, cy, cz = parts(op, ZT0)
    inner = slice(1, ZT0 - 1)
    unpack_y(
        FIRST, (zx_s, zx_f, zx_m, zx_coarse), from_low, from_high,
        ([s], [f.at[inner]], [m.at[inner]], [s1, m1]),
    )
    couple(s, m, r, cx, cy, cz, 1, ZT0 - 1, 4, start=(f, va))
    far.flush(2)
    op = (r, f, cx, cy, cz)
    sweep(va, vb, op, 2, ZT0 - 2, 4)
    sweep(vb, va, op, 3, ZT0 - 3, 4)
    sweep(va, vb, op, 4, ZT0 - 4, 4)
    for z in range(Z1):
        a, b = W0 + 2 * z, W0 + 2 * z + 1
        plane = remain(vb, op, a) + remain(vb, op, b)
        tall[z * X0 : (z + 1) * X0, :] = plane[0:X0, 0:Y0]
    rows = tall[pl.ds(0, Z1 * X1, stride=2), :] + tall[pl.ds(1, Z1 * X1, stride=2), :]
    out = fold_lanes(rows, 0, LANES, 0)
    for z in range(Z1):
        g_own[0, z] = out[z * X1 : (z + 1) * X1, :]
    for z in range(Z0):
        v_own[0, z] = vb[W0 + z, 0:X0, 0:Y0]
    pack_x(SECOND, (g_own, v_own), low, high)


def presmooth1(
    far, g_zx, v0_zx, s, m, from_low, from_high,
    v_own, v0, copies, op, low, high,
    va, vb, tall,
):
    r, g, cx, cy, cz = parts(op, ZT1)
    for k in range(W1 - G1):
        g[k] = jnp.zeros((XT1, LANES), F32)
        g[ZT1 - 1 - k] = jnp.zeros((XT1, LANES), F32)
    inner = g.at[W1 - G1 : ZT1 - (W1 - G1)]
    unpack_y(SECOND, (g_zx, v0_zx), from_low, from_high, ([inner], [v0]))
    couple(s, m, r, cx, cy, cz, 1, ZT1 - 1, 10, start=(g, va))
    far.flush(3)
    op = (r, g, cx, cy, cz)
    sweep(va, vb, op, 4, ZT1 - 4, 10)
    sweep(vb, va, op, 5, ZT1 - 5, 10)
    sweep(va, vb, op, 6, ZT1 - 6, 10)
    packed = pack_coarse(lambda z: remain(vb, op, W1 + z)[0:X1, :], 0, tall)
    for d in range(copies.shape[0]):
        copies[d] = packed
    for z in range(Z1):
        v_own[z] = vb[W1 + z]
    lane = lane_of((XT0, LANES))
    base = (W0 + 1) * XT0
    for message, first0, first1 in ((low, 0, 0), (high, Z0 - W0, Z1 - W1)):
        rims = jnp.zeros((XT0, LANES), F32)
        for w in range(W0):
            message[w * XT0 : (w + 1) * XT0, :] = v0[first0 + w, :, 0:LANES]
            here = (lane >= 2 * W0 * w) & (lane < 2 * W0 * (w + 1))
            rims = jnp.where(here, roll(v0[first0 + w, :, LANES:], W0 + 2 * W0 * w, 1), rims)
        message[W0 * XT0 : base, :] = rims
        for w in range(W1):
            message[base + w * XT1 : base + (w + 1) * XT1, :] = v_own[first1 + w]


def unpack_whole(blocks, first, out):
    group = lane_of((8, LANES)) // 32

    def body(step):
        gz, gx = step // 4, step % 4
        for z in range(4):
            plane = None
            for gy in range(4):
                block = blocks[step * 4 + gy, first : first + 8, :]
                moved = roll(block, (gy - z) * 32, 1)
                plane = moved if plane is None else jnp.where(group == gy, moved, plane)
            out[gz * 4 + z, pl.ds(pl.multiple_of(gx * 8, 8), 8), :] = plane

    loop(0, 32, body, 4)


def fold_whole(plane, planes, rows, scale, tall, out):
    half = rows // 2
    for z in range(planes // 2):
        tall[z * rows : (z + 1) * rows, :] = plane(2 * z) + plane(2 * z + 1)
    count = planes // 2 * half
    folded = tall[pl.ds(0, count, stride=2), :] + tall[pl.ds(1, count, stride=2), :]
    folded = scale * fold_lanes(folded, 0, LANES, 0)
    for z in range(planes // 2):
        out[z] = folded[z * half : (z + 1) * half, :]


def spread_whole(v, planes, rows, tall, add):
    count = planes * rows
    flat = spread_lanes(jnp.concatenate([v[z] for z in range(planes)], axis=0))
    tall[pl.ds(0, count, stride=2), :] = flat
    tall[pl.ds(1, count, stride=2), :] = flat
    for z in range(planes):
        spread = tall[z * 2 * rows : (z + 1) * 2 * rows, :]
        add[2 * z] = add[2 * z] + spread
        add[2 * z + 1] = add[2 * z + 1] + spread


def coarsest(out, op):
    r, f, cx, cy, cz = op
    forced, upper, lower = [], [], []
    for z in range(8):
        scale = r[z]
        forced.append(scale * f[z])
        above = scale * cz[z]
        below = scale * cz[z - 1] if z else None
        upper.append((above, scale * cx[z], scale * cy[z]))
        lower.append((below, scale * roll(cx[z], 1, 0), scale * roll(cy[z], 1, 1)))

    def step(k, v):
        new = []
        for z in range(8):
            here = v[z]
            east = upper[z][2] * roll(here, -1, 1) + lower[z][2] * roll(here, 1, 1)
            north = upper[z][1] * roll(here, -1, 0) + lower[z][1] * roll(here, 1, 0)
            base = KEEP * here + forced[z]
            if z < 7:
                base = base + upper[z][0] * v[z + 1]
            if z:
                base = base + lower[z][0] * v[z - 1]
            new.append((base + north) + east)
        return tuple(new)

    v = lax.fori_loop(0, CSWEEPS - 1, step, tuple(forced), unroll=True)
    for z in range(8):
        out[z] = v[z]


def levels(stacked):
    level3 = [stacked.at[128 + 16 * (k // 2) : 144 + 16 * (k // 2), 16 * (k % 2) : 16 * (k % 2) + 16, :] for k in range(4)]
    level4 = [stacked.at[160:168, 8 * k : 8 * k + 8, :] for k in range(4)]
    return parts(stacked, 32, 4), level3, level4


def coarse_operators(
    far, operators,
    stacked,
    s2, m2, s3, m3, s4, m4, tall,
):
    (r2, cx2, cy2, cz2), (r3, cx3, cy3, cz3), (r4, cx4, cy4, cz4) = levels(stacked)
    far.wait()
    unpack_whole(operators, 0, s2)
    unpack_whole(operators, 8, m2)
    couple(s2, m2, r2, cx2, cy2, cz2, 0, 32, 10, True)
    fold_whole(lambda z: s2[z], 32, 32, 0.25, tall, s3)
    fold_whole(lambda z: m2[z], 32, 32, 1.0, tall, m3)
    couple(s3, m3, r3, cx3, cy3, cz3, 0, 16, 14, True)
    fold_whole(lambda z: s3[z], 16, 16, 0.25, tall, s4)
    fold_whole(lambda z: m3[z], 16, 16, 1.0, tall, m4)
    couple(s4, m4, r4, cx4, cy4, cz4, 0, 8, 6, True)


def coarse_cycle(
    far, forcing, stacked, out,
    f2, vb2, f3, va3, vb3, f4, vb4, tall,
):
    unpack_whole(forcing, 0, f2)
    far.wait()
    (r2, cx2, cy2, cz2), (r3, cx3, cy3, cz3), (r4, cx4, cy4, cz4) = levels(stacked)
    op2 = (r2, f2, cx2, cy2, cz2)
    op3 = (r3, f3, cx3, cy3, cz3)
    op4 = (r4, f4, cx4, cy4, cz4)
    va2 = out

    def four(va, vb, op, planes):
        sweep(va, vb, op, 0, planes, 15, True)
        sweep(vb, va, op, 0, planes, 15, True)

    def residue(v, op, planes):
        return lambda z: remain(v, op, z, z > 0, z < planes - 1)

    first_sweep(vb2, op2, 0, 32)
    sweep(vb2, va2, op2, 0, 32, 15, True)
    four(va2, vb2, op2, 32)
    fold_whole(residue(va2, op2, 32), 32, 32, 1.0, tall, f3)
    first_sweep(vb3, op3, 0, 16)
    sweep(vb3, va3, op3, 0, 16, 15, True)
    four(va3, vb3, op3, 16)
    fold_whole(residue(va3, op3, 16), 16, 16, 1.0, tall, f4)
    coarsest(vb4, op4)
    spread_whole(vb4, 8, 8, tall, va3)
    four(va3, vb3, op3, 16)
    four(va3, vb3, op3, 16)
    spread_whole(va3, 16, 16, tall, va2)
    four(va2, vb2, op2, 32)
    four(va2, vb2, op2, 32)


def postsmooth(
    far, place, v1, v0_zx, from_low, from_high, stacked1, stacked0, correction,
    potential, residual,
    va1, vb1, v0, vb0, tall,
):
    base = (W0 + 1) * XT0
    for message, first0, first1 in ((from_low, 0, 0), (from_high, W0 + Z0, W1 + Z1)):
        rims = message[W0 * XT0 : base, :]
        for w in range(W0):
            v0[first0 + w, :, 0:LANES] = message[w * XT0 : (w + 1) * XT0, :]
            v0[first0 + w, :, LANES:] = roll(rims, -W0 - 2 * W0 * w, 1)
        for w in range(W1):
            va1[first1 + w] = message[base + w * XT1 : base + (w + 1) * XT1, :]
    for z in range(Z0):
        v0[W0 + z] = v0_zx[z]
    for z in range(Z1):
        va1[W1 + z] = v1[z]
    gz, gx, gy = place[0], place[1], place[2]
    planes = []
    for k in range(12):
        plane = correction[(gz * 4 + 28 + k) % 32]
        plane = pltpu.roll(plane, (32 - gx * 8) % 32, 0)
        plane = pltpu.roll(plane, (LANES - gy * 32) % LANES, 1)
        planes += [plane[0:14], plane[26:32]]
    flat = jnp.concatenate(planes, axis=0)
    fine = lane_of(flat.shape)
    flat = pick(flat, fine // 2 + jnp.where(fine < 96, 0, 64))
    count = 12 * 20
    tall[pl.ds(0, count, stride=2), :] = flat
    tall[pl.ds(1, count, stride=2), :] = flat
    for z in range(ZT1):
        k = (z + 1) // 2
        va1[z] = va1[z] + tall[k * XT1 : (k + 1) * XT1, :]
    far.wait(4)
    far.start(5)
    op1 = parts(stacked1, ZT1)
    sweep(va1, vb1, op1, 1, ZT1 - 1, 10)
    sweep(vb1, va1, op1, 2, ZT1 - 2, 10)
    sweep(va1, vb1, op1, 3, ZT1 - 3, 10)
    sweep(vb1, va1, op1, 4, ZT1 - 4, 10)
    planes = []
    for k in range(14):
        planes += [va1[4 + k, 0:20, :], va1[4 + k, XT1 - 4 : XT1, :]]
    flat = jnp.concatenate(planes, axis=0)
    count = 14 * 24
    for half in range(2):
        part = spread_lanes(flat, 64 * half)
        tall[pl.ds(0, count, stride=2), :] = part
        tall[pl.ds(1, count, stride=2), :] = part
        for z in range(ZT0):
            k = (z + 1) // 2
            at = slice(half * LANES, (half + 1) * LANES)
            v0[z, :, at] = v0[z, :, at] + tall[k * XT0 : (k + 1) * XT0, :]
    far.wait(5)
    op0 = parts(stacked0, ZT0)
    sweep(v0, vb0, op0, 1, ZT0 - 1, 4)
    sweep(vb0, v0, op0, 2, ZT0 - 2, 4)
    sweep(v0, vb0, op0, 3, ZT0 - 3, 4)
    sweep(vb0, v0, op0, 4, ZT0 - 4, 4)
    for z in range(Z0):
        potential[z] = v0[W0 + z, 0:X0, 0:Y0]
    for z in range(Z0):
        residual[z] = remain(v0, op0, W0 + z)[0:X0, 0:Y0]


def shards(source, conductivity, cell_kind):
    own0, own1 = (1, Z0, X0, Y0), (1, Z1, X1, LANES)
    ext0, ext1 = (ZT0, XT0, 2 * LANES), (ZT1, XT1, LANES)
    everywhere = ("gz", "gx", "gy")
    devices = math.prod(lax.axis_size(axis) for axis in everywhere)
    place = jnp.stack([lax.axis_index(axis) for axis in everywhere]).astype(jnp.int32)
    wet = jnp.where(cell_kind > 0, 1.0, 0.0).astype(F32)
    surface = jnp.where(cell_kind == 2, 1.0, 0.0).astype(F32)
    stiffness = conductivity * wet
    mass = 0.005 * stiffness + 8.0 * stiffness * surface + 0.02 * (1.0 - wet)
    fields = [array.reshape(own0) for array in (stiffness, source * wet, mass)]
    coarse, low, high = call(
        prepare, [own1] + [x_message(FIRST)] * 2, [(Z1 * X0, LANES)], *fields
    )
    (packed2,) = call(prepare_coarse, [(16, LANES)], [(Z1 // 2 * X1, LANES)], coarse)
    operators2 = lax.all_gather(packed2, everywhere, axis=0)
    arrays, from_low, from_high = exchange(FIRST, (*fields, coarse), low, high)
    v0, g1, op0, s1, m1, low, high = call(
        presmooth0,
        [own0, own1, (5 * ZT0, XT0, 2 * LANES)] + [ext1] * 2 + [x_message(SECOND)] * 2,
        [ext0] * 4 + [(Z1 * X0, LANES)],
        *arrays, from_low, from_high, far_out=(2,),
    )
    arrays, from_low, from_high = exchange(SECOND, (g1, v0), low, high)
    stack0, stack1, stack2 = (5 * ZT0, XT0, 2 * LANES), (5 * ZT1, XT1, LANES), (168, 32, LANES)
    message = ((W0 + 1) * XT0 + W1 * XT1, LANES)
    v1, v0, copies, op1, low, high = call(
        presmooth1,
        [(Z1, XT1, LANES), (Z0, XT0, 2 * LANES), (devices, 8, LANES), stack1] + [message] * 2,
        [ext1] * 2 + [(Z1 // 2 * X1, LANES)],
        arrays[0], arrays[1], s1, m1, from_low, from_high, far_out=(3,),
    )
    copies, operators2 = lax.optimization_barrier((copies, operators2))
    forcing2 = lax.all_to_all(copies, everywhere, 0, 0)
    from_low, from_high = shift(low, high, "gz")
    level2, level3, level4 = (32, 32, LANES), (16, 16, LANES), (8, 8, LANES)
    (operators,) = call(
        coarse_operators,
        [stack2],
        [level2] * 2 + [level3] * 2 + [level4] * 2 + [(512, LANES)],
        operators2, far_in={0: operators2.shape}, far_out=(0,),
    )
    (correction,) = call(
        coarse_cycle,
        [level2],
        [level2] * 2 + [level3] * 3 + [level4] * 2 + [(512, LANES)],
        forcing2, operators, far_in={1: stack2},
    )
    return call(
        postsmooth,
        [(Z0, X0, Y0)] * 2,
        [ext1, ext1, ext0, ext0, (14 * XT0, LANES)],
        v1, v0, from_low, from_high, op1, op0, correction,
        place=place, far_in={4: stack1, 5: stack0}, late=(5,),
    )


def solution(mesh):
    spec = P("gz", "gx", "gy")
    return jax.shard_map(
        shards, mesh=mesh, in_specs=(spec,) * 3, out_specs=(spec,) * 2, check_vma=False
    )
```

```python
import math

import jax
import jax.numpy as jnp
from jax import lax
from jax.experimental import pallas as pl
from jax.experimental.pallas import tpu as pltpu
from jax.sharding import PartitionSpec as P

CSWEEPS = 32
DAMP = 0.8
KEEP = 1.0 - DAMP
W0 = 5
W1 = 7
G1 = 6
S1, F1 = 11, 10
Z0, X0, Y0 = 16, 32, 128
Z1, X1, Y1 = 8, 16, 64
ZT0, XT0 = Z0 + 2 * W0, 48
ZT1, XT1 = Z1 + 2 * W1, 40
LANES = 128
MIB = 1024 * 1024
F32 = jnp.float32


def lane_of(shape):
    return lax.broadcasted_iota(jnp.int32, shape, len(shape) - 1)


def row_of(shape):
    return lax.broadcasted_iota(jnp.int32, shape, len(shape) - 2)


def roll(x, shift, axis):
    size = x.shape[axis]
    shift = shift % size
    return x if shift == 0 else pltpu.roll(x, shift, axis)


def loop(first, last, body, step):
    chunks = (last - first) // step

    def chunk(c, carry):
        for k in range(step):
            body(first + c * step + k)
        return carry

    if chunks > 1:
        lax.fori_loop(0, chunks, chunk, 0)
    elif chunks:
        chunk(0, 0)
    for z in range(first + chunks * step, last):
        body(z)


def pick(x, index):
    return jnp.take_along_axis(x, index, axis=1)


def fold_lanes(x, first, count, target):
    to = lane_of(x.shape) - target
    index = (first + 2 * to) % LANES
    pairs = pick(x, index) + pick(x, (index + 1) % LANES)
    return jnp.where((to >= 0) & (to < count // 2), pairs, 0.0)


def spread_lanes(x, first=0):
    return pick(x, first + lane_of(x.shape) // 2)


class Far:
    def __init__(self, ins, outs):
        self.ins = {k: pltpu.make_async_copy(*pair) for k, pair in ins.items()}
        self.outs = {k: pltpu.make_async_copy(*pair) for k, pair in outs.items()}
        self.started = []
        for copy in self.ins.values():
            copy.start()

    def wait(self, *keys):
        for k in keys or tuple(self.ins):
            self.ins.pop(k).wait()

    def flush(self, *keys):
        for k in keys:
            self.outs[k].start()
            self.started.append(k)

    def finish(self):
        self.flush(*[k for k in self.outs if k not in self.started])
        for copy in self.outs.values():
            copy.wait()


def padded(shape):
    plane = 4 * math.prod(shape[1:])
    return (max(shape[0], -(-7 * MIB // plane)), *shape[1:])


def call(body, outs, scratch, *args, place=None, far_in={}, far_out=(), grant=48):
    shapes = [
        jax.ShapeDtypeStruct(padded(shape) if k in far_out else shape, F32)
        for k, shape in enumerate(outs)
    ]
    vmem = pl.BlockSpec(memory_space=pltpu.VMEM)
    hbm = pl.BlockSpec(memory_space=pltpu.HBM)
    specs = [hbm if k in far_in else vmem for k in range(len(args))]
    out_specs = [hbm if k in far_out else vmem for k in range(len(outs))]
    held = [pltpu.VMEM(shape, F32) for shape in far_in.values()]
    held += [pltpu.VMEM(outs[k], F32) for k in far_out]
    extra = len(far_in) + len(far_out)
    if extra:
        held.append(pltpu.SemaphoreType.DMA((extra,)))
    placed = place is not None
    count = len(args)

    def wrapped(*refs):
        refs = list(refs)
        head = [refs.pop(0)] if placed else []
        ins, results = refs[:count], refs[count : count + len(outs)]
        rest = refs[count + len(outs) :]
        mine, rest = rest[: len(scratch)], rest[len(scratch) :]
        copies_in, copies_out = {}, {}
        for j, k in enumerate(far_in):
            copies_in[k] = (ins[k].at[0 : far_in[k][0]], rest[j], rest[extra].at[j])
            ins[k] = rest[j]
        for j, k in enumerate(far_out, len(far_in)):
            copies_out[k] = (rest[j], results[k].at[0 : outs[k][0]], rest[extra].at[j])
            results[k] = rest[j]
        far = Far(copies_in, copies_out)
        body(far, *head, *ins, *results, *mine)
        far.finish()

    if placed:
        specs = [pl.BlockSpec(memory_space=pltpu.SMEM)] + specs
        args = (place,) + args
    return pl.pallas_call(
        wrapped,
        out_shape=shapes,
        in_specs=specs,
        out_specs=out_specs,
        scratch_shapes=[pltpu.VMEM(shape, F32) for shape in scratch] + held,
        compiler_params=pltpu.CompilerParams(vmem_limit_bytes=grant * MIB),
    )(*args)


class Item:
    def __init__(self, fields, planes, rows, rows_out, width, kind, trim=False, width_z=None, edge=0):
        self.n, self.z, self.x, self.xt, self.w, self.kind = fields, planes, rows, rows_out, width, kind
        self.wz = width if width_z is None else width_z
        self.zt = planes + 2 * self.wz
        self.edge = edge
        self.trim = trim
        self.tall = rows + 8 if trim else rows_out
        self.virtual = 2 * fields if kind == "pair" else fields
        self.own = LANES if kind == "full" else LANES // 2
        self.slots = LANES // width
        self.groups = -(-self.virtual * (self.zt - 2 * edge) // self.slots)
        self.rows_x = fields * planes * width
        self.rows_z = fields * self.wz * self.tall
        self.rows_y = self.groups * self.tall

    def narrow(self, plane):
        if not self.trim:
            return plane
        upper, lower = plane[self.x : self.x + 8], plane[self.xt - 8 : self.xt]
        rim = jnp.where(row_of(upper.shape) < 4, upper, lower)
        return jnp.concatenate([plane[: self.x], rim], axis=0)

    def widen(self, plane):
        if not self.trim:
            return plane
        rim = plane[self.x :]
        upper = jnp.where(row_of(rim.shape) < 4, rim, 0.0)
        return jnp.concatenate([plane[: self.x], upper, rim - upper], axis=0)


def total(counts):
    count = sum(counts)
    return -(-count // 8) * 8


def pack_x(items, refs, low, high):
    at = 0
    for item, ref in zip(items, refs):
        for n in range(item.n):
            for z in range(item.z):
                low[at : at + item.w, :] = ref[n, z, 0 : item.w, :]
                high[at : at + item.w, :] = ref[n, z, item.x - item.w : item.x, :]
                at += item.w


def unpack_x(items, refs, from_low, from_high, outs):
    at = 0
    for item, ref, out in zip(items, refs, outs):
        out[:, :, item.x :, :] = jnp.zeros((item.n, item.z, item.xt - item.x, LANES), F32)
        for n in range(item.n):
            for z in range(item.z):
                out[n, z, 0 : item.x, :] = ref[n, z]
                out[n, z, item.x : item.x + item.w, :] = from_high[at : at + item.w, :]
                out[n, z, item.xt - item.w :, :] = from_low[at : at + item.w, :]
                at += item.w


def pack_z(items, refs, low, high):
    at = 0
    for item, ref in zip(items, refs):
        for n in range(item.n):
            for w in range(item.wz):
                low[at : at + item.tall, :] = item.narrow(ref[n, w])
                high[at : at + item.tall, :] = item.narrow(ref[n, item.z - item.wz + w])
                at += item.tall


def unpack_z(items, refs, from_low, from_high, outs):
    at = 0
    for item, ref, out in zip(items, refs, outs):
        for n in range(item.n):
            for w in range(item.wz):
                out[n, w] = item.widen(from_low[at : at + item.tall, :])
                out[n, item.wz + item.z + w] = item.widen(from_high[at : at + item.tall, :])
                at += item.tall
            for z in range(item.z):
                out[n, item.wz + z] = ref[n, z]


def pack_y(items, refs, low, high):
    at = 0
    for item, ref in zip(items, refs):
        lane = lane_of((item.tall, LANES))
        pairs = [(v, z) for v in range(item.virtual) for z in range(item.edge, item.zt - item.edge)]
        for g in range(item.groups):
            lows = jnp.zeros((item.tall, LANES), F32)
            highs = lows
            for k, (v, z) in enumerate(pairs[g * item.slots : (g + 1) * item.slots]):
                n, first = (v // 2, (v % 2) * item.own) if item.kind == "pair" else (v, 0)
                plane = item.narrow(ref[n, z])
                place = k * item.w
                mask = (lane >= place) & (lane < place + item.w)
                lows = jnp.where(mask, roll(plane, place - first, 1), lows)
                highs = jnp.where(mask, roll(plane, place - first - item.own + item.w, 1), highs)
            low[at : at + item.tall, :] = lows
            high[at : at + item.tall, :] = highs
            at += item.tall


def unpack_y(items, refs, from_low, from_high, outs):
    at = 0
    for item, ref, fields in zip(items, refs, outs):
        lane = lane_of((item.tall, LANES))
        for v in range(item.virtual if item.edge else 0):
            for z in [*range(item.edge), *range(item.zt - item.edge, item.zt)]:
                fields[v][z, :, 0:LANES] = ref[v, z]
                fields[v][z, :, LANES:] = jnp.zeros((item.xt, LANES), F32)
        pairs = [(v, z) for v in range(item.virtual) for z in range(item.edge, item.zt - item.edge)]
        for g in range(item.groups):
            lows = from_low[at : at + item.tall, :]
            highs = from_high[at : at + item.tall, :]
            at += item.tall
            for k, (v, z) in enumerate(pairs[g * item.slots : (g + 1) * item.slots]):
                place = k * item.w
                start = item.own % LANES
                upper = roll(highs, start - place, 1)
                lower = roll(lows, LANES - item.w - place, 1)
                rim = jnp.where(
                    lane < start + item.w, upper, jnp.where(lane >= LANES - item.w, lower, 0.0)
                )
                if item.kind == "full":
                    fields[v][z, :, 0:LANES] = ref[v, z]
                    fields[v][z, :, LANES:] = item.widen(rim)
                else:
                    plane = ref[v // 2, z] if item.kind == "pair" else ref[v, z]
                    if item.kind == "pair" and v % 2:
                        plane = roll(plane, item.own, 1)
                    fields[v][z] = jnp.where(lane < item.own, plane, rim)


def shift(low, high, axis):
    count = lax.axis_size(axis)
    forward = [(i, i + 1) for i in range(count - 1)]
    backward = [(target, source) for source, target in forward]
    return lax.ppermute(high, axis, forward), lax.ppermute(low, axis, backward)


def exchange(items, arrays, low, high, beside=None):
    count = len(items)
    from_low, from_high = shift(low, high, "gx")
    shapes = [(item.n, item.z, item.xt, LANES) for item in items]
    message = (total(item.rows_z for item in items), LANES)

    def after_x(far, *refs):
        ins, (a, b), outs, (c, d) = refs[:count], refs[count : count + 2], refs[count + 2 : 2 * count + 2], refs[2 * count + 2 :]
        unpack_x(items, ins, a, b, outs)
        pack_z(items, outs, c, d)

    *arrays, low, high = call(after_x, shapes + [message] * 2, [], *arrays, from_low, from_high)
    extra = beside(low) if beside else None
    from_low, from_high = shift(low, high, "gz")
    shapes = [(item.n, item.zt, item.xt, LANES) for item in items]
    message = (total(item.rows_y for item in items), LANES)

    def after_z(far, *refs):
        ins, (a, b), outs, (c, d) = refs[:count], refs[count : count + 2], refs[count + 2 : 2 * count + 2], refs[2 * count + 2 :]
        unpack_z(items, ins, a, b, outs)
        pack_y(items, outs, c, d)

    *arrays, low, high = call(after_z, shapes + [message] * 2, [], *arrays, from_low, from_high)
    from_low, from_high = shift(low, high, "gy")
    return (arrays, from_low, from_high, extra) if beside else (arrays, from_low, from_high)


STIFFNESS = Item(1, Z0, X0, XT0, W0, "full", True, edge=1)
INNER = Item(1, Z0, X0, XT0, W0 - 1, "full", True)
COARSE = Item(1, Z1, X1, XT1, S1, "pair", False, W1)
FORCING1 = Item(1, Z1, X1, XT1, F1, "half", False, G1)
POTENTIAL0 = Item(1, Z0, X0, XT0, W0, "full", False, 0)
FIRST, SECOND = (STIFFNESS, INNER, INNER, COARSE), (FORCING1, POTENTIAL0)


def x_message(items):
    return (total(item.rows_x for item in items), LANES)


def couple(s, m, r, cx, cy, cz, first, last, step, edges=False, start=None):
    planes, rows, lanes = s.shape

    def vertical(z):
        return 4.0 * jnp.minimum(s[z], s[z + 1])

    def one(z, below, above):
        here = s[z]
        x_face = jnp.minimum(here, roll(here, -1, 0))
        y_face = jnp.minimum(here, roll(here, -1, 1))
        if edges:
            x_face = jnp.where(row_of(here.shape) < rows - 1, x_face, 0.0)
            y_face = jnp.where(lane_of(here.shape) < lanes - 1, y_face, 0.0)
        cx[z] = x_face
        cy[z] = y_face
        cz[z] = above
        d = m[z] + below + above + x_face + roll(x_face, 1, 0) + y_face + roll(y_face, 1, 1)
        scale = DAMP / jnp.where(d > 0.0, d, 1.0)
        r[z] = scale
        if start:
            start[1][z] = scale * start[0][z]

    if edges:
        zero = jnp.zeros((rows, lanes), F32)
        one(0, zero, vertical(0))
        one(planes - 1, vertical(planes - 2), zero)
    else:
        cz[first - 1] = vertical(first - 1)
    loop(first + edges, last - edges, lambda z: one(z, vertical(z - 1), vertical(z)), step)


def gathered(v, f, cx, cy, cz, z, low=True, high=True):
    here = v[z]
    x_face, y_face = cx[z], cy[z]
    out = f[z]
    if high:
        out = out + cz[z] * v[z + 1]
    if low:
        out = out + cz[z - 1] * v[z - 1]
    out = out + x_face * roll(here, -1, 0) + roll(x_face * here, 1, 0)
    return here, out + y_face * roll(here, -1, 1) + roll(y_face * here, 1, 1)


def sweep(v, into, op, first, last, unroll, edges=False):
    r, f, cx, cy, cz = op

    def step(z, low=True, high=True):
        here, out = gathered(v, f, cx, cy, cz, z, low, high)
        into[z] = KEEP * here + r[z] * out

    if edges:
        step(first, low=False)
        step(last - 1, high=False)
        loop(first + 1, last - 1, step, unroll)
    else:
        loop(first, last, step, unroll)


def remain(v, op, z, low=True, high=True):
    r, f, cx, cy, cz = op
    here, out = gathered(v, f, cx, cy, cz, z, low, high)
    return out - here * (DAMP / r[z])


def first_sweep(v, op, first, last):
    r, f = op[:2]

    def step(z):
        v[z] = r[z] * f[z]

    loop(first, last, step, 4)


def prepare(far, stiffness, forcing, mass, coarse, low, high, tall):
    out = None
    for ref, scale, target in ((stiffness, 0.25, 0), (mass, 1.0, Y1)):
        for z in range(Z1):
            tall[z * X0 : (z + 1) * X0, :] = ref[0, 2 * z] + ref[0, 2 * z + 1]
        rows = tall[pl.ds(0, Z1 * X1, stride=2), :] + tall[pl.ds(1, Z1 * X1, stride=2), :]
        part = scale * fold_lanes(rows, 0, LANES, target)
        out = part if out is None else out + part
    for z in range(Z1):
        coarse[0, z] = out[z * X1 : (z + 1) * X1, :]
    pack_x(FIRST, (stiffness, forcing, mass, coarse), low, high)


def prepare_coarse(far, coarse, packed2, tall):
    for part, scale in ((0, 0.25), (1, 1.0)):
        packed2[part * 8 : part * 8 + 8, :] = scale * pack_coarse(
            lambda z: coarse[0, z], part * Y1, tall
        )


def pack_coarse(plane, first, tall):
    for z in range(Z1 // 2):
        tall[z * X1 : (z + 1) * X1, :] = plane(2 * z) + plane(2 * z + 1)
    count = Z1 // 2 * X1 // 2
    rows = tall[pl.ds(0, count, stride=2), :] + tall[pl.ds(1, count, stride=2), :]
    out = jnp.zeros((X1 // 2, LANES), F32)
    for z in range(Z1 // 2):
        part = rows[z * X1 // 2 : (z + 1) * X1 // 2, :]
        out = out + fold_lanes(part, first, Y1, z * Y1 // 2)
    return out


def parts(ref, planes, count=5):
    return [ref.at[k * planes : (k + 1) * planes] for k in range(count)]


def presmooth0(
    far, zx_s, zx_f, zx_m, zx_coarse, from_low, from_high,
    v_own, g_own, op, s1, m1, low, high,
    s, m, va, vb, tall,
):
    r, f, cx, cy, cz = parts(op, ZT0)
    inner = slice(1, ZT0 - 1)
    unpack_y(
        FIRST, (zx_s, zx_f, zx_m, zx_coarse), from_low, from_high,
        ([s], [f.at[inner]], [m.at[inner]], [s1, m1]),
    )
    couple(s, m, r, cx, cy, cz, 1, ZT0 - 1, 8, start=(f, va))
    far.flush(2)
    op = (r, f, cx, cy, cz)
    sweep(va, vb, op, 2, ZT0 - 2, 11)
    sweep(vb, va, op, 3, ZT0 - 3, 10)
    sweep(va, vb, op, 4, ZT0 - 4, 9)
    for z in range(Z1):
        a, b = W0 + 2 * z, W0 + 2 * z + 1
        plane = remain(vb, op, a) + remain(vb, op, b)
        tall[z * X0 : (z + 1) * X0, :] = plane[0:X0, 0:Y0]
    rows = tall[pl.ds(0, Z1 * X1, stride=2), :] + tall[pl.ds(1, Z1 * X1, stride=2), :]
    out = fold_lanes(rows, 0, LANES, 0)
    for z in range(Z1):
        g_own[0, z] = out[z * X1 : (z + 1) * X1, :]
    for z in range(Z0):
        v_own[0, z] = vb[W0 + z, 0:X0, 0:Y0]
    pack_x(SECOND, (g_own, v_own), low, high)


def presmooth1(
    far, g_zx, v0_zx, s, m, from_low, from_high,
    v_own, v0, copies, op, low, high,
    va, vb, tall,
):
    r, g, cx, cy, cz = parts(op, ZT1)
    for k in range(W1 - G1):
        g[k] = jnp.zeros((XT1, LANES), F32)
        g[ZT1 - 1 - k] = jnp.zeros((XT1, LANES), F32)
    inner = g.at[W1 - G1 : ZT1 - (W1 - G1)]
    unpack_y(SECOND, (g_zx, v0_zx), from_low, from_high, ([inner], [v0]))
    couple(s, m, r, cx, cy, cz, 1, ZT1 - 1, 20, start=(g, va))
    far.flush(3)
    op = (r, g, cx, cy, cz)
    sweep(va, vb, op, 4, ZT1 - 4, 14)
    sweep(vb, va, op, 5, ZT1 - 5, 12)
    sweep(va, vb, op, 6, ZT1 - 6, 10)
    packed = pack_coarse(lambda z: remain(vb, op, W1 + z)[0:X1, :], 0, tall)
    for d in range(copies.shape[0]):
        copies[d] = packed
    for z in range(Z1):
        v_own[z] = vb[W1 + z]
    lane = lane_of((XT0, LANES))
    base = (W0 + 1) * XT0
    for message, first0, first1 in ((low, 0, 0), (high, Z0 - W0, Z1 - W1)):
        rims = jnp.zeros((XT0, LANES), F32)
        for w in range(W0):
            message[w * XT0 : (w + 1) * XT0, :] = v0[first0 + w, :, 0:LANES]
            here = (lane >= 2 * W0 * w) & (lane < 2 * W0 * (w + 1))
            rims = jnp.where(here, roll(v0[first0 + w, :, LANES:], W0 + 2 * W0 * w, 1), rims)
        message[W0 * XT0 : base, :] = rims
        for w in range(W1):
            message[base + w * XT1 : base + (w + 1) * XT1, :] = v_own[first1 + w]


def unpack_whole(blocks, first, out):
    group = lane_of((8, LANES)) // 32

    def body(step):
        gz, gx = step // 4, step % 4
        for z in range(4):
            plane = None
            for gy in range(4):
                block = blocks[step * 4 + gy, first : first + 8, :]
                moved = roll(block, (gy - z) * 32, 1)
                plane = moved if plane is None else jnp.where(group == gy, moved, plane)
            out[gz * 4 + z, pl.ds(pl.multiple_of(gx * 8, 8), 8), :] = plane

    loop(0, 32, body, 4)


def fold_whole(plane, planes, rows, scale, tall, out):
    half = rows // 2
    for z in range(planes // 2):
        tall[z * rows : (z + 1) * rows, :] = plane(2 * z) + plane(2 * z + 1)
    count = planes // 2 * half
    folded = tall[pl.ds(0, count, stride=2), :] + tall[pl.ds(1, count, stride=2), :]
    folded = scale * fold_lanes(folded, 0, LANES, 0)
    for z in range(planes // 2):
        out[z] = folded[z * half : (z + 1) * half, :]


def spread_whole(v, planes, rows, tall, add):
    count = planes * rows
    flat = spread_lanes(jnp.concatenate([v[z] for z in range(planes)], axis=0))
    tall[pl.ds(0, count, stride=2), :] = flat
    tall[pl.ds(1, count, stride=2), :] = flat
    for z in range(planes):
        spread = tall[z * 2 * rows : (z + 1) * 2 * rows, :]
        add[2 * z] = add[2 * z] + spread
        add[2 * z + 1] = add[2 * z + 1] + spread


def coarsest(out, op):
    r, f, cx, cy, cz = op
    forced, upper, lower = [], [], []
    for z in range(8):
        scale = r[z]
        forced.append(scale * f[z])
        above = scale * cz[z]
        below = scale * cz[z - 1] if z else None
        upper.append((above, scale * cx[z], scale * cy[z]))
        lower.append((below, scale * roll(cx[z], 1, 0), scale * roll(cy[z], 1, 1)))

    def step(k, v):
        new = []
        for z in range(8):
            here = v[z]
            east = upper[z][2] * roll(here, -1, 1) + lower[z][2] * roll(here, 1, 1)
            north = upper[z][1] * roll(here, -1, 0) + lower[z][1] * roll(here, 1, 0)
            base = KEEP * here + forced[z]
            if z < 7:
                base = base + upper[z][0] * v[z + 1]
            if z:
                base = base + lower[z][0] * v[z - 1]
            new.append((base + north) + east)
        return tuple(new)

    v = lax.fori_loop(0, CSWEEPS - 1, step, tuple(forced), unroll=True)
    for z in range(8):
        out[z] = v[z]


def levels(stacked):
    level3 = [stacked.at[128 + 16 * (k // 2) : 144 + 16 * (k // 2), 16 * (k % 2) : 16 * (k % 2) + 16, :] for k in range(4)]
    level4 = [stacked.at[160:168, 8 * k : 8 * k + 8, :] for k in range(4)]
    return parts(stacked, 32, 4), level3, level4


def coarse_operators(
    far, operators,
    stacked,
    s2, m2, s3, m3, s4, m4, tall,
):
    (r2, cx2, cy2, cz2), (r3, cx3, cy3, cz3), (r4, cx4, cy4, cz4) = levels(stacked)
    far.wait()
    unpack_whole(operators, 0, s2)
    unpack_whole(operators, 8, m2)
    couple(s2, m2, r2, cx2, cy2, cz2, 0, 32, 10, True)
    fold_whole(lambda z: s2[z], 32, 32, 0.25, tall, s3)
    fold_whole(lambda z: m2[z], 32, 32, 1.0, tall, m3)
    couple(s3, m3, r3, cx3, cy3, cz3, 0, 16, 14, True)
    fold_whole(lambda z: s3[z], 16, 16, 0.25, tall, s4)
    fold_whole(lambda z: m3[z], 16, 16, 1.0, tall, m4)
    couple(s4, m4, r4, cx4, cy4, cz4, 0, 8, 6, True)


def coarse_cycle(
    far, forcing, stacked, out,
    f2, vb2, f3, va3, vb3, f4, vb4, tall, meanwhile,
):
    unpack_whole(forcing, 0, f2)
    far.wait(0)
    (r2, cx2, cy2, cz2), (r3, cx3, cy3, cz3), (r4, cx4, cy4, cz4) = levels(stacked)
    op2 = (r2, f2, cx2, cy2, cz2)
    op3 = (r3, f3, cx3, cy3, cz3)
    op4 = (r4, f4, cx4, cy4, cz4)
    va2 = out

    def four(va, vb, op, planes):
        sweep(va, vb, op, 0, planes, 30, True)
        sweep(vb, va, op, 0, planes, 30, True)

    def residue(v, op, planes):
        return lambda z: remain(v, op, z, z > 0, z < planes - 1)

    first_sweep(vb2, op2, 0, 32)
    sweep(vb2, va2, op2, 0, 32, 30, True)
    four(va2, vb2, op2, 32)
    fold_whole(residue(va2, op2, 32), 32, 32, 1.0, tall, f3)
    first_sweep(vb3, op3, 0, 16)
    sweep(vb3, va3, op3, 0, 16, 15, True)
    four(va3, vb3, op3, 16)
    fold_whole(residue(va3, op3, 16), 16, 16, 1.0, tall, f4)
    meanwhile()
    coarsest(vb4, op4)
    spread_whole(vb4, 8, 8, tall, va3)
    four(va3, vb3, op3, 16)
    four(va3, vb3, op3, 16)
    spread_whole(va3, 16, 16, tall, va2)
    four(va2, vb2, op2, 32)
    four(va2, vb2, op2, 32)


def finish(
    far, place, stacked2, stacked1, stacked0, forcing, v1, v0_zx, from_low, from_high,
    potential, residual,
    va1, vb1, v0, vb0, correction, f2, vb2, f3, va3, vb3, f4, vb4, tall,
):
    def meanwhile():
        base = (W0 + 1) * XT0
        for message, first0, first1 in ((from_low, 0, 0), (from_high, W0 + Z0, W1 + Z1)):
            rims = message[W0 * XT0 : base, :]
            for w in range(W0):
                v0[first0 + w, :, 0:LANES] = message[w * XT0 : (w + 1) * XT0, :]
                v0[first0 + w, :, LANES:] = roll(rims, -W0 - 2 * W0 * w, 1)
            for w in range(W1):
                va1[first1 + w] = message[base + w * XT1 : base + (w + 1) * XT1, :]
        for z in range(Z0):
            v0[W0 + z] = v0_zx[z]
        for z in range(Z1):
            va1[W1 + z] = v1[z]

    coarse_cycle(far, forcing, stacked2, correction, f2, vb2, f3, va3, vb3, f4, vb4, tall, meanwhile)
    gz, gx, gy = place[0], place[1], place[2]
    planes = []
    for k in range(12):
        plane = correction[(gz * 4 + 28 + k) % 32]
        plane = pltpu.roll(plane, (32 - gx * 8) % 32, 0)
        plane = pltpu.roll(plane, (LANES - gy * 32) % LANES, 1)
        planes += [plane[0:14], plane[26:32]]
    flat = jnp.concatenate(planes, axis=0)
    fine = lane_of(flat.shape)
    flat = pick(flat, fine // 2 + jnp.where(fine < 96, 0, 64))
    count = 12 * 20
    tall[pl.ds(0, count, stride=2), :] = flat
    tall[pl.ds(1, count, stride=2), :] = flat
    for z in range(ZT1):
        k = (z + 1) // 2
        va1[z] = va1[z] + tall[k * XT1 : (k + 1) * XT1, :]
    far.wait(1)
    op1 = parts(stacked1, ZT1)
    sweep(va1, vb1, op1, 1, ZT1 - 1, 20)
    sweep(vb1, va1, op1, 2, ZT1 - 2, 18)
    sweep(va1, vb1, op1, 3, ZT1 - 3, 16)
    sweep(vb1, va1, op1, 4, ZT1 - 4, 14)
    planes = []
    for k in range(14):
        planes += [va1[4 + k, 0:20, :], va1[4 + k, XT1 - 4 : XT1, :]]
    flat = jnp.concatenate(planes, axis=0)
    count = 14 * 24
    for half in range(2):
        part = spread_lanes(flat, 64 * half)
        tall[pl.ds(0, count, stride=2), :] = part
        tall[pl.ds(1, count, stride=2), :] = part
        for z in range(ZT0):
            k = (z + 1) // 2
            at = slice(half * LANES, (half + 1) * LANES)
            v0[z, :, at] = v0[z, :, at] + tall[k * XT0 : (k + 1) * XT0, :]
    far.wait(2)
    op0 = parts(stacked0, ZT0)
    sweep(v0, vb0, op0, 1, ZT0 - 1, 12)
    sweep(vb0, v0, op0, 2, ZT0 - 2, 11)
    sweep(v0, vb0, op0, 3, ZT0 - 3, 10)
    sweep(vb0, v0, op0, 4, ZT0 - 4, 9)
    for z in range(Z0):
        potential[z] = v0[W0 + z, 0:X0, 0:Y0]
    for z in range(Z0):
        residual[z] = remain(v0, op0, W0 + z)[0:X0, 0:Y0]


def shards(source, conductivity, cell_kind):
    own0, own1 = (1, Z0, X0, Y0), (1, Z1, X1, LANES)
    ext0, ext1 = (ZT0, XT0, 2 * LANES), (ZT1, XT1, LANES)
    everywhere = ("gz", "gx", "gy")
    devices = math.prod(lax.axis_size(axis) for axis in everywhere)
    place = jnp.stack([lax.axis_index(axis) for axis in everywhere]).astype(jnp.int32)
    wet = jnp.where(cell_kind > 0, 1.0, 0.0).astype(F32)
    surface = jnp.where(cell_kind == 2, 1.0, 0.0).astype(F32)
    stiffness = conductivity * wet
    mass = 0.005 * stiffness + 8.0 * stiffness * surface + 0.02 * (1.0 - wet)
    fields = [array.reshape(own0) for array in (stiffness, source * wet, mass)]
    coarse, low, high = call(
        prepare, [own1] + [x_message(FIRST)] * 2, [(Z1 * X0, LANES)], *fields
    )

    def gather_coarse(message):
        block, _ = lax.optimization_barrier((coarse, message))
        (packed2,) = call(prepare_coarse, [(16, LANES)], [(Z1 // 2 * X1, LANES)], block)
        return lax.all_gather(packed2, everywhere, axis=0)

    arrays, from_low, from_high, operators2 = exchange(FIRST, (*fields, coarse), low, high, gather_coarse)
    v0, g1, op0, s1, m1, low, high = call(
        presmooth0,
        [own0, own1, (5 * ZT0, XT0, 2 * LANES)] + [ext1] * 2 + [x_message(SECOND)] * 2,
        [ext0] * 4 + [(Z1 * X0, LANES)],
        *arrays, from_low, from_high, far_out=(2,),
    )
    arrays, from_low, from_high = exchange(SECOND, (g1, v0), low, high)
    stack0, stack1, stack2 = (5 * ZT0, XT0, 2 * LANES), (5 * ZT1, XT1, LANES), (168, 32, LANES)
    message = ((W0 + 1) * XT0 + W1 * XT1, LANES)
    v1, v0, copies, op1, low, high = call(
        presmooth1,
        [(Z1, XT1, LANES), (Z0, XT0, 2 * LANES), (devices, 8, LANES), stack1] + [message] * 2,
        [ext1] * 2 + [(Z1 // 2 * X1, LANES)],
        arrays[0], arrays[1], s1, m1, from_low, from_high, far_out=(3,),
    )
    _, operators2 = lax.optimization_barrier((copies, operators2))
    forcing2 = lax.all_to_all(copies, everywhere, 0, 0)
    from_low, from_high = shift(low, high, "gz")
    level2, level3, level4 = (32, 32, LANES), (16, 16, LANES), (8, 8, LANES)
    (operators,) = call(
        coarse_operators,
        [stack2],
        [level2] * 2 + [level3] * 2 + [level4] * 2 + [(512, LANES)],
        operators2, far_in={0: operators2.shape}, far_out=(0,),
    )
    return call(
        finish,
        [(Z0, X0, Y0)] * 2,
        [ext1, ext1, ext0, ext0] + [level2] * 3 + [level3] * 3 + [level4] * 2 + [(14 * XT0, LANES)],
        operators, op1, op0, forcing2, v1, v0, from_low, from_high,
        place=place, far_in={0: stack2, 1: stack1, 2: stack0},
    )


def solution(mesh):
    spec = P("gz", "gx", "gy")
    return jax.shard_map(
        shards, mesh=mesh, in_specs=(spec,) * 3, out_specs=(spec,) * 2, check_vma=False
    )
```

```python
import math

import jax
import jax.numpy as jnp
from jax import lax
from jax.experimental import pallas as pl
from jax.experimental.pallas import tpu as pltpu
from jax.sharding import PartitionSpec as P

CSWEEPS = 32
DAMP = 0.8
KEEP = 1.0 - DAMP
W0 = 5
W1 = 7
G1 = 6
S1, F1 = 11, 10
Z0, X0, Y0 = 16, 32, 128
Z1, X1, Y1 = 8, 16, 64
ZT0, XT0 = Z0 + 2 * W0, 48
ZT1, XT1 = Z1 + 2 * W1, 40
LANES = 128
MIB = 1024 * 1024
F32 = jnp.float32


def lane_of(shape):
    return lax.broadcasted_iota(jnp.int32, shape, len(shape) - 1)


def row_of(shape):
    return lax.broadcasted_iota(jnp.int32, shape, len(shape) - 2)


def roll(x, shift, axis):
    size = x.shape[axis]
    shift = shift % size
    return x if shift == 0 else pltpu.roll(x, shift, axis)


def loop(first, last, body, step):
    chunks = (last - first) // step

    def chunk(c, carry):
        for k in range(step):
            body(first + c * step + k)
        return carry

    if chunks > 1:
        lax.fori_loop(0, chunks, chunk, 0)
    elif chunks:
        chunk(0, 0)
    for z in range(first + chunks * step, last):
        body(z)


def pick(x, index):
    return jnp.take_along_axis(x, index, axis=1)


def fold_lanes(x, first, count, target):
    to = lane_of(x.shape) - target
    index = (first + 2 * to) % LANES
    pairs = pick(x, index) + pick(x, (index + 1) % LANES)
    return jnp.where((to >= 0) & (to < count // 2), pairs, 0.0)


def spread_lanes(x, first=0):
    return pick(x, first + lane_of(x.shape) // 2)


class Far:
    def __init__(self, ins, outs, late):
        self.ins = {k: pltpu.make_async_copy(*pair) for k, pair in ins.items()}
        self.outs = {k: pltpu.make_async_copy(*pair) for k, pair in outs.items()}
        self.started = []
        self.start(*[k for k in self.ins if k not in late])

    def start(self, *keys):
        for k in keys:
            self.ins[k].start()

    def wait(self, *keys):
        for k in keys or tuple(self.ins):
            self.ins.pop(k).wait()

    def flush(self, *keys):
        for k in keys:
            self.outs[k].start()
            self.started.append(k)

    def finish(self):
        self.flush(*[k for k in self.outs if k not in self.started])
        for copy in self.outs.values():
            copy.wait()


def padded(shape):
    plane = 4 * math.prod(shape[1:])
    return (max(shape[0], -(-7 * MIB // plane)), *shape[1:])


def call(body, outs, scratch, *args, place=None, far_in={}, far_out=(), late=(), grant=48):
    shapes = [
        jax.ShapeDtypeStruct(padded(shape) if k in far_out else shape, F32)
        for k, shape in enumerate(outs)
    ]
    vmem = pl.BlockSpec(memory_space=pltpu.VMEM)
    hbm = pl.BlockSpec(memory_space=pltpu.HBM)
    specs = [hbm if k in far_in else vmem for k in range(len(args))]
    out_specs = [hbm if k in far_out else vmem for k in range(len(outs))]
    held = [pltpu.VMEM(shape, F32) for shape in far_in.values()]
    held += [pltpu.VMEM(outs[k], F32) for k in far_out]
    extra = len(far_in) + len(far_out)
    if extra:
        held.append(pltpu.SemaphoreType.DMA((extra,)))
    placed = place is not None
    count = len(args)

    def wrapped(*refs):
        refs = list(refs)
        head = [refs.pop(0)] if placed else []
        ins, results = refs[:count], refs[count : count + len(outs)]
        rest = refs[count + len(outs) :]
        mine, rest = rest[: len(scratch)], rest[len(scratch) :]
        copies_in, copies_out = {}, {}
        for j, k in enumerate(far_in):
            copies_in[k] = (ins[k].at[0 : far_in[k][0]], rest[j], rest[extra].at[j])
            ins[k] = rest[j]
        for j, k in enumerate(far_out, len(far_in)):
            copies_out[k] = (rest[j], results[k].at[0 : outs[k][0]], rest[extra].at[j])
            results[k] = rest[j]
        far = Far(copies_in, copies_out, late)
        body(far, *head, *ins, *results, *mine)
        far.finish()

    if placed:
        specs = [pl.BlockSpec(memory_space=pltpu.SMEM)] + specs
        args = (place,) + args
    return pl.pallas_call(
        wrapped,
        out_shape=shapes,
        in_specs=specs,
        out_specs=out_specs,
        scratch_shapes=[pltpu.VMEM(shape, F32) for shape in scratch] + held,
        compiler_params=pltpu.CompilerParams(vmem_limit_bytes=grant * MIB),
    )(*args)


class Item:
    def __init__(self, fields, planes, rows, rows_out, width, kind, trim=False, width_z=None, edge=0):
        self.n, self.z, self.x, self.xt, self.w, self.kind = fields, planes, rows, rows_out, width, kind
        self.wz = width if width_z is None else width_z
        self.zt = planes + 2 * self.wz
        self.edge = edge
        self.trim = trim
        self.tall = rows + 8 if trim else rows_out
        self.virtual = 2 * fields if kind == "pair" else fields
        self.own = LANES if kind == "full" else LANES // 2
        self.slots = LANES // width
        self.groups = -(-self.virtual * (self.zt - 2 * edge) // self.slots)
        self.rows_x = fields * planes * width
        self.rows_z = fields * self.wz * self.tall
        self.rows_y = self.groups * self.tall

    def narrow(self, plane):
        if not self.trim:
            return plane
        upper, lower = plane[self.x : self.x + 8], plane[self.xt - 8 : self.xt]
        rim = jnp.where(row_of(upper.shape) < 4, upper, lower)
        return jnp.concatenate([plane[: self.x], rim], axis=0)

    def widen(self, plane):
        if not self.trim:
            return plane
        rim = plane[self.x :]
        upper = jnp.where(row_of(rim.shape) < 4, rim, 0.0)
        return jnp.concatenate([plane[: self.x], upper, rim - upper], axis=0)


def total(counts):
    count = sum(counts)
    return -(-count // 8) * 8


def pack_x(items, refs, low, high):
    at = 0
    for item, ref in zip(items, refs):
        for n in range(item.n):
            for z in range(item.z):
                low[at : at + item.w, :] = ref[n, z, 0 : item.w, :]
                high[at : at + item.w, :] = ref[n, z, item.x - item.w : item.x, :]
                at += item.w


def unpack_x(items, refs, from_low, from_high, outs):
    at = 0
    for item, ref, out in zip(items, refs, outs):
        out[:, :, item.x :, :] = jnp.zeros((item.n, item.z, item.xt - item.x, LANES), F32)
        for n in range(item.n):
            for z in range(item.z):
                out[n, z, 0 : item.x, :] = ref[n, z]
                out[n, z, item.x : item.x + item.w, :] = from_high[at : at + item.w, :]
                out[n, z, item.xt - item.w :, :] = from_low[at : at + item.w, :]
                at += item.w


def pack_z(items, refs, low, high):
    at = 0
    for item, ref in zip(items, refs):
        for n in range(item.n):
            for w in range(item.wz):
                low[at : at + item.tall, :] = item.narrow(ref[n, w])
                high[at : at + item.tall, :] = item.narrow(ref[n, item.z - item.wz + w])
                at += item.tall


def unpack_z(items, refs, from_low, from_high, outs):
    at = 0
    for item, ref, out in zip(items, refs, outs):
        for n in range(item.n):
            for w in range(item.wz):
                out[n, w] = item.widen(from_low[at : at + item.tall, :])
                out[n, item.wz + item.z + w] = item.widen(from_high[at : at + item.tall, :])
                at += item.tall
            for z in range(item.z):
                out[n, item.wz + z] = ref[n, z]


def pack_y(items, refs, low, high):
    at = 0
    for item, ref in zip(items, refs):
        lane = lane_of((item.tall, LANES))
        pairs = [(v, z) for v in range(item.virtual) for z in range(item.edge, item.zt - item.edge)]
        for g in range(item.groups):
            lows = jnp.zeros((item.tall, LANES), F32)
            highs = lows
            for k, (v, z) in enumerate(pairs[g * item.slots : (g + 1) * item.slots]):
                n, first = (v // 2, (v % 2) * item.own) if item.kind == "pair" else (v, 0)
                plane = item.narrow(ref[n, z])
                place = k * item.w
                mask = (lane >= place) & (lane < place + item.w)
                lows = jnp.where(mask, roll(plane, place - first, 1), lows)
                highs = jnp.where(mask, roll(plane, place - first - item.own + item.w, 1), highs)
            low[at : at + item.tall, :] = lows
            high[at : at + item.tall, :] = highs
            at += item.tall


def unpack_y(items, refs, from_low, from_high, outs):
    at = 0
    for item, ref, fields in zip(items, refs, outs):
        lane = lane_of((item.tall, LANES))
        for v in range(item.virtual if item.edge else 0):
            for z in [*range(item.edge), *range(item.zt - item.edge, item.zt)]:
                fields[v][z, :, 0:LANES] = ref[v, z]
                fields[v][z, :, LANES:] = jnp.zeros((item.xt, LANES), F32)
        pairs = [(v, z) for v in range(item.virtual) for z in range(item.edge, item.zt - item.edge)]
        for g in range(item.groups):
            lows = from_low[at : at + item.tall, :]
            highs = from_high[at : at + item.tall, :]
            at += item.tall
            for k, (v, z) in enumerate(pairs[g * item.slots : (g + 1) * item.slots]):
                place = k * item.w
                start = item.own % LANES
                upper = roll(highs, start - place, 1)
                lower = roll(lows, LANES - item.w - place, 1)
                rim = jnp.where(
                    lane < start + item.w, upper, jnp.where(lane >= LANES - item.w, lower, 0.0)
                )
                if item.kind == "full":
                    fields[v][z, :, 0:LANES] = ref[v, z]
                    fields[v][z, :, LANES:] = item.widen(rim)
                else:
                    plane = ref[v // 2, z] if item.kind == "pair" else ref[v, z]
                    if item.kind == "pair" and v % 2:
                        plane = roll(plane, item.own, 1)
                    fields[v][z] = jnp.where(lane < item.own, plane, rim)


def shift(low, high, axis):
    count = lax.axis_size(axis)
    forward = [(i, i + 1) for i in range(count - 1)]
    backward = [(target, source) for source, target in forward]
    return lax.ppermute(high, axis, forward), lax.ppermute(low, axis, backward)


def exchange(items, arrays, low, high, beside=None):
    count = len(items)
    from_low, from_high = shift(low, high, "gx")
    shapes = [(item.n, item.z, item.xt, LANES) for item in items]
    message = (total(item.rows_z for item in items), LANES)

    def after_x(far, *refs):
        ins, (a, b), outs, (c, d) = refs[:count], refs[count : count + 2], refs[count + 2 : 2 * count + 2], refs[2 * count + 2 :]
        unpack_x(items, ins, a, b, outs)
        pack_z(items, outs, c, d)

    *arrays, low, high = call(after_x, shapes + [message] * 2, [], *arrays, from_low, from_high)
    extra = beside(low) if beside else None
    from_low, from_high = shift(low, high, "gz")
    shapes = [(item.n, item.zt, item.xt, LANES) for item in items]
    message = (total(item.rows_y for item in items), LANES)

    def after_z(far, *refs):
        ins, (a, b), outs, (c, d) = refs[:count], refs[count : count + 2], refs[count + 2 : 2 * count + 2], refs[2 * count + 2 :]
        unpack_z(items, ins, a, b, outs)
        pack_y(items, outs, c, d)

    *arrays, low, high = call(after_z, shapes + [message] * 2, [], *arrays, from_low, from_high)
    from_low, from_high = shift(low, high, "gy")
    return (arrays, from_low, from_high, extra) if beside else (arrays, from_low, from_high)


STIFFNESS = Item(1, Z0, X0, XT0, W0, "full", True, edge=1)
INNER = Item(1, Z0, X0, XT0, W0 - 1, "full", True)
COARSE = Item(1, Z1, X1, XT1, S1, "pair", False, W1)
FORCING1 = Item(1, Z1, X1, XT1, F1, "half", False, G1)
POTENTIAL0 = Item(1, Z0, X0, XT0, W0, "full", False, 0)
FIRST, SECOND = (STIFFNESS, INNER, INNER, COARSE), (FORCING1, POTENTIAL0)


def x_message(items):
    return (total(item.rows_x for item in items), LANES)


def couple(s, m, r, cx, cy, cz, first, last, step, edges=False, start=None):
    planes, rows, lanes = s.shape

    def vertical(z):
        return 4.0 * jnp.minimum(s[z], s[z + 1])

    def one(z, below, above):
        here = s[z]
        x_face = jnp.minimum(here, roll(here, -1, 0))
        y_face = jnp.minimum(here, roll(here, -1, 1))
        if edges:
            x_face = jnp.where(row_of(here.shape) < rows - 1, x_face, 0.0)
            y_face = jnp.where(lane_of(here.shape) < lanes - 1, y_face, 0.0)
        cx[z] = x_face
        cy[z] = y_face
        cz[z] = above
        d = m[z] + below + above + x_face + roll(x_face, 1, 0) + y_face + roll(y_face, 1, 1)
        scale = DAMP / jnp.where(d > 0.0, d, 1.0)
        r[z] = scale
        if start:
            start[1][z] = scale * start[0][z]

    if edges:
        zero = jnp.zeros((rows, lanes), F32)
        one(0, zero, vertical(0))
        one(planes - 1, vertical(planes - 2), zero)
    else:
        cz[first - 1] = vertical(first - 1)
    loop(first + edges, last - edges, lambda z: one(z, vertical(z - 1), vertical(z)), step)


def gathered(v, f, cx, cy, cz, z, low=True, high=True):
    here = v[z]
    x_face, y_face = cx[z], cy[z]
    out = f[z]
    if high:
        out = out + cz[z] * v[z + 1]
    if low:
        out = out + cz[z - 1] * v[z - 1]
    out = out + x_face * roll(here, -1, 0) + roll(x_face * here, 1, 0)
    return here, out + y_face * roll(here, -1, 1) + roll(y_face * here, 1, 1)


def sweep(v, into, op, first, last, unroll, edges=False):
    r, f, cx, cy, cz = op

    def step(z, low=True, high=True):
        here, out = gathered(v, f, cx, cy, cz, z, low, high)
        into[z] = KEEP * here + r[z] * out

    if edges:
        step(first, low=False)
        step(last - 1, high=False)
        loop(first + 1, last - 1, step, unroll)
    else:
        loop(first, last, step, unroll)


def remain(v, op, z, low=True, high=True):
    r, f, cx, cy, cz = op
    here, out = gathered(v, f, cx, cy, cz, z, low, high)
    return out - here * (DAMP / r[z])


def first_sweep(v, op, first, last):
    r, f = op[:2]

    def step(z):
        v[z] = r[z] * f[z]

    loop(first, last, step, 4)


def prepare(far, stiffness, forcing, mass, coarse, low, high, tall):
    out = None
    for ref, scale, target in ((stiffness, 0.25, 0), (mass, 1.0, Y1)):
        for z in range(Z1):
            tall[z * X0 : (z + 1) * X0, :] = ref[0, 2 * z] + ref[0, 2 * z + 1]
        rows = tall[pl.ds(0, Z1 * X1, stride=2), :] + tall[pl.ds(1, Z1 * X1, stride=2), :]
        part = scale * fold_lanes(rows, 0, LANES, target)
        out = part if out is None else out + part
    for z in range(Z1):
        coarse[0, z] = out[z * X1 : (z + 1) * X1, :]
    pack_x(FIRST, (stiffness, forcing, mass, coarse), low, high)


def prepare_coarse(far, coarse, packed2, tall):
    for part, scale in ((0, 0.25), (1, 1.0)):
        packed2[part * 8 : part * 8 + 8, :] = scale * pack_coarse(
            lambda z: coarse[0, z], part * Y1, tall
        )


def pack_coarse(plane, first, tall):
    for z in range(Z1 // 2):
        tall[z * X1 : (z + 1) * X1, :] = plane(2 * z) + plane(2 * z + 1)
    count = Z1 // 2 * X1 // 2
    rows = tall[pl.ds(0, count, stride=2), :] + tall[pl.ds(1, count, stride=2), :]
    out = jnp.zeros((X1 // 2, LANES), F32)
    for z in range(Z1 // 2):
        part = rows[z * X1 // 2 : (z + 1) * X1 // 2, :]
        out = out + fold_lanes(part, first, Y1, z * Y1 // 2)
    return out


def parts(ref, planes, count=5):
    return [ref.at[k * planes : (k + 1) * planes] for k in range(count)]


def presmooth0(
    far, zx_s, zx_f, zx_m, zx_coarse, from_low, from_high,
    v_own, g_own, op, s1, m1, low, high,
    s, m, va, vb, tall,
):
    r, f, cx, cy, cz = parts(op, ZT0)
    inner = slice(1, ZT0 - 1)
    unpack_y(
        FIRST, (zx_s, zx_f, zx_m, zx_coarse), from_low, from_high,
        ([s], [f.at[inner]], [m.at[inner]], [s1, m1]),
    )
    couple(s, m, r, cx, cy, cz, 1, ZT0 - 1, 8, start=(f, va))
    far.flush(2)
    op = (r, f, cx, cy, cz)
    sweep(va, vb, op, 2, ZT0 - 2, 11)
    sweep(vb, va, op, 3, ZT0 - 3, 10)
    sweep(va, vb, op, 4, ZT0 - 4, 9)
    for z in range(Z1):
        a, b = W0 + 2 * z, W0 + 2 * z + 1
        plane = remain(vb, op, a) + remain(vb, op, b)
        tall[z * X0 : (z + 1) * X0, :] = plane[0:X0, 0:Y0]
    rows = tall[pl.ds(0, Z1 * X1, stride=2), :] + tall[pl.ds(1, Z1 * X1, stride=2), :]
    out = fold_lanes(rows, 0, LANES, 0)
    for z in range(Z1):
        g_own[0, z] = out[z * X1 : (z + 1) * X1, :]
    for z in range(Z0):
        v_own[0, z] = vb[W0 + z, 0:X0, 0:Y0]
    pack_x(SECOND, (g_own, v_own), low, high)


def presmooth1(
    far, g_zx, v0_zx, s, m, from_low, from_high,
    v_own, v0, copies, op, low, high,
    va, vb, tall,
):
    r, g, cx, cy, cz = parts(op, ZT1)
    for k in range(W1 - G1):
        g[k] = jnp.zeros((XT1, LANES), F32)
        g[ZT1 - 1 - k] = jnp.zeros((XT1, LANES), F32)
    inner = g.at[W1 - G1 : ZT1 - (W1 - G1)]
    unpack_y(SECOND, (g_zx, v0_zx), from_low, from_high, ([inner], [v0]))
    couple(s, m, r, cx, cy, cz, 1, ZT1 - 1, 10, start=(g, va))
    far.flush(3)
    op = (r, g, cx, cy, cz)
    sweep(va, vb, op, 4, ZT1 - 4, 10)
    sweep(vb, va, op, 5, ZT1 - 5, 10)
    sweep(va, vb, op, 6, ZT1 - 6, 10)
    packed = pack_coarse(lambda z: remain(vb, op, W1 + z)[0:X1, :], 0, tall)
    for d in range(copies.shape[0]):
        copies[d] = packed
    for z in range(Z1):
        v_own[z] = vb[W1 + z]
    lane = lane_of((XT0, LANES))
    base = (W0 + 1) * XT0
    for message, first0, first1 in ((low, 0, 0), (high, Z0 - W0, Z1 - W1)):
        rims = jnp.zeros((XT0, LANES), F32)
        for w in range(W0):
            message[w * XT0 : (w + 1) * XT0, :] = v0[first0 + w, :, 0:LANES]
            here = (lane >= 2 * W0 * w) & (lane < 2 * W0 * (w + 1))
            rims = jnp.where(here, roll(v0[first0 + w, :, LANES:], W0 + 2 * W0 * w, 1), rims)
        message[W0 * XT0 : base, :] = rims
        for w in range(W1):
            message[base + w * XT1 : base + (w + 1) * XT1, :] = v_own[first1 + w]


def unpack_whole(blocks, first, out):
    group = lane_of((8, LANES)) // 32

    def body(step):
        gz, gx = step // 4, step % 4
        for z in range(4):
            plane = None
            for gy in range(4):
                block = blocks[step * 4 + gy, first : first + 8, :]
                moved = roll(block, (gy - z) * 32, 1)
                plane = moved if plane is None else jnp.where(group == gy, moved, plane)
            out[gz * 4 + z, pl.ds(pl.multiple_of(gx * 8, 8), 8), :] = plane

    loop(0, 32, body, 4)


def fold_whole(plane, planes, rows, scale, tall, out):
    half = rows // 2
    for z in range(planes // 2):
        tall[z * rows : (z + 1) * rows, :] = plane(2 * z) + plane(2 * z + 1)
    count = planes // 2 * half
    folded = tall[pl.ds(0, count, stride=2), :] + tall[pl.ds(1, count, stride=2), :]
    folded = scale * fold_lanes(folded, 0, LANES, 0)
    for z in range(planes // 2):
        out[z] = folded[z * half : (z + 1) * half, :]


def spread_whole(v, planes, rows, tall, add):
    count = planes * rows
    flat = spread_lanes(jnp.concatenate([v[z] for z in range(planes)], axis=0))
    tall[pl.ds(0, count, stride=2), :] = flat
    tall[pl.ds(1, count, stride=2), :] = flat
    for z in range(planes):
        spread = tall[z * 2 * rows : (z + 1) * 2 * rows, :]
        add[2 * z] = add[2 * z] + spread
        add[2 * z + 1] = add[2 * z + 1] + spread


def coarsest(out, op):
    r, f, cx, cy, cz = op
    forced, upper, lower = [], [], []
    for z in range(8):
        scale = r[z]
        forced.append(scale * f[z])
        above = scale * cz[z]
        below = scale * cz[z - 1] if z else None
        upper.append((above, scale * cx[z], scale * cy[z]))
        lower.append((below, scale * roll(cx[z], 1, 0), scale * roll(cy[z], 1, 1)))

    def step(k, v):
        new = []
        for z in range(8):
            here = v[z]
            east = upper[z][2] * roll(here, -1, 1) + lower[z][2] * roll(here, 1, 1)
            north = upper[z][1] * roll(here, -1, 0) + lower[z][1] * roll(here, 1, 0)
            base = KEEP * here + forced[z]
            if z < 7:
                base = base + upper[z][0] * v[z + 1]
            if z:
                base = base + lower[z][0] * v[z - 1]
            new.append((base + north) + east)
        return tuple(new)

    v = lax.fori_loop(0, CSWEEPS - 1, step, tuple(forced), unroll=True)
    for z in range(8):
        out[z] = v[z]


def levels(stacked2, stacked34):
    level3 = [stacked34.at[16 * (k // 2) : 16 * (k // 2) + 16, 16 * (k % 2) : 16 * (k % 2) + 16, :] for k in range(4)]
    level4 = [stacked34.at[32:40, 8 * k : 8 * k + 8, :] for k in range(4)]
    return parts(stacked2, 32, 4), level3, level4


def coarse_operators(
    far, operators,
    stacked2, stacked34,
    s2, m2, s3, m3, s4, m4, tall,
):
    (r2, cx2, cy2, cz2), (r3, cx3, cy3, cz3), (r4, cx4, cy4, cz4) = levels(stacked2, stacked34)
    far.wait()
    unpack_whole(operators, 0, s2)
    unpack_whole(operators, 8, m2)
    couple(s2, m2, r2, cx2, cy2, cz2, 0, 32, 10, True)
    far.flush(0)
    fold_whole(lambda z: s2[z], 32, 32, 0.25, tall, s3)
    fold_whole(lambda z: m2[z], 32, 32, 1.0, tall, m3)
    couple(s3, m3, r3, cx3, cy3, cz3, 0, 16, 14, True)
    fold_whole(lambda z: s3[z], 16, 16, 0.25, tall, s4)
    fold_whole(lambda z: m3[z], 16, 16, 1.0, tall, m4)
    couple(s4, m4, r4, cx4, cy4, cz4, 0, 8, 6, True)


def coarse_cycle(
    far, forcing, stacked2, stacked34, out,
    f2, vb2, f3, va3, vb3, f4, vb4, tall, meanwhile,
):
    unpack_whole(forcing, 0, f2)
    far.wait(0, 3)
    far.start(1, 2)
    (r2, cx2, cy2, cz2), (r3, cx3, cy3, cz3), (r4, cx4, cy4, cz4) = levels(stacked2, stacked34)
    op2 = (r2, f2, cx2, cy2, cz2)
    op3 = (r3, f3, cx3, cy3, cz3)
    op4 = (r4, f4, cx4, cy4, cz4)
    va2 = out

    def four(va, vb, op, planes):
        sweep(va, vb, op, 0, planes, 30, True)
        sweep(vb, va, op, 0, planes, 30, True)

    def residue(v, op, planes):
        return lambda z: remain(v, op, z, z > 0, z < planes - 1)

    first_sweep(vb2, op2, 0, 32)
    sweep(vb2, va2, op2, 0, 32, 30, True)
    four(va2, vb2, op2, 32)
    fold_whole(residue(va2, op2, 32), 32, 32, 1.0, tall, f3)
    first_sweep(vb3, op3, 0, 16)
    sweep(vb3, va3, op3, 0, 16, 15, True)
    four(va3, vb3, op3, 16)
    fold_whole(residue(va3, op3, 16), 16, 16, 1.0, tall, f4)
    meanwhile()
    coarsest(vb4, op4)
    spread_whole(vb4, 8, 8, tall, va3)
    four(va3, vb3, op3, 16)
    four(va3, vb3, op3, 16)
    spread_whole(va3, 16, 16, tall, va2)
    four(va2, vb2, op2, 32)
    four(va2, vb2, op2, 32)


def finish(
    far, place, stacked2, stacked1, stacked0, stacked34, forcing, v1, v0_zx, from_low, from_high,
    potential, residual,
    va1, vb1, v0, vb0, correction, f2, vb2, f3, va3, vb3, f4, vb4, tall,
):
    def meanwhile():
        base = (W0 + 1) * XT0
        for message, first0, first1 in ((from_low, 0, 0), (from_high, W0 + Z0, W1 + Z1)):
            rims = message[W0 * XT0 : base, :]
            for w in range(W0):
                v0[first0 + w, :, 0:LANES] = message[w * XT0 : (w + 1) * XT0, :]
                v0[first0 + w, :, LANES:] = roll(rims, -W0 - 2 * W0 * w, 1)
            for w in range(W1):
                va1[first1 + w] = message[base + w * XT1 : base + (w + 1) * XT1, :]
        for z in range(Z0):
            v0[W0 + z] = v0_zx[z]
        for z in range(Z1):
            va1[W1 + z] = v1[z]

    coarse_cycle(far, forcing, stacked2, stacked34, correction, f2, vb2, f3, va3, vb3, f4, vb4, tall, meanwhile)
    gz, gx, gy = place[0], place[1], place[2]
    planes = []
    for k in range(12):
        plane = correction[(gz * 4 + 28 + k) % 32]
        plane = pltpu.roll(plane, (32 - gx * 8) % 32, 0)
        plane = pltpu.roll(plane, (LANES - gy * 32) % LANES, 1)
        planes += [plane[0:14], plane[26:32]]
    flat = jnp.concatenate(planes, axis=0)
    fine = lane_of(flat.shape)
    flat = pick(flat, fine // 2 + jnp.where(fine < 96, 0, 64))
    count = 12 * 20
    tall[pl.ds(0, count, stride=2), :] = flat
    tall[pl.ds(1, count, stride=2), :] = flat
    for z in range(ZT1):
        k = (z + 1) // 2
        va1[z] = va1[z] + tall[k * XT1 : (k + 1) * XT1, :]
    far.wait(1)
    op1 = parts(stacked1, ZT1)
    sweep(va1, vb1, op1, 1, ZT1 - 1, 10)
    sweep(vb1, va1, op1, 2, ZT1 - 2, 10)
    sweep(va1, vb1, op1, 3, ZT1 - 3, 10)
    sweep(vb1, va1, op1, 4, ZT1 - 4, 10)
    planes = []
    for k in range(14):
        planes += [va1[4 + k, 0:20, :], va1[4 + k, XT1 - 4 : XT1, :]]
    flat = jnp.concatenate(planes, axis=0)
    count = 14 * 24
    for half in range(2):
        part = spread_lanes(flat, 64 * half)
        tall[pl.ds(0, count, stride=2), :] = part
        tall[pl.ds(1, count, stride=2), :] = part
        for z in range(ZT0):
            k = (z + 1) // 2
            at = slice(half * LANES, (half + 1) * LANES)
            v0[z, :, at] = v0[z, :, at] + tall[k * XT0 : (k + 1) * XT0, :]
    far.wait(2)
    op0 = parts(stacked0, ZT0)
    sweep(v0, vb0, op0, 1, ZT0 - 1, 12)
    sweep(vb0, v0, op0, 2, ZT0 - 2, 11)
    sweep(v0, vb0, op0, 3, ZT0 - 3, 10)
    sweep(vb0, v0, op0, 4, ZT0 - 4, 9)
    for z in range(Z0):
        potential[z] = v0[W0 + z, 0:X0, 0:Y0]
    for z in range(Z0):
        residual[z] = remain(v0, op0, W0 + z)[0:X0, 0:Y0]


def shards(source, conductivity, cell_kind):
    own0, own1 = (1, Z0, X0, Y0), (1, Z1, X1, LANES)
    ext0, ext1 = (ZT0, XT0, 2 * LANES), (ZT1, XT1, LANES)
    everywhere = ("gz", "gx", "gy")
    devices = math.prod(lax.axis_size(axis) for axis in everywhere)
    place = jnp.stack([lax.axis_index(axis) for axis in everywhere]).astype(jnp.int32)
    wet = jnp.where(cell_kind > 0, 1.0, 0.0).astype(F32)
    surface = jnp.where(cell_kind == 2, 1.0, 0.0).astype(F32)
    stiffness = conductivity * wet
    mass = 0.005 * stiffness + 8.0 * stiffness * surface + 0.02 * (1.0 - wet)
    fields = [array.reshape(own0) for array in (stiffness, source * wet, mass)]
    coarse, low, high = call(
        prepare, [own1] + [x_message(FIRST)] * 2, [(Z1 * X0, LANES)], *fields
    )

    def gather_coarse(message):
        block, _ = lax.optimization_barrier((coarse, message))
        (packed2,) = call(prepare_coarse, [(16, LANES)], [(Z1 // 2 * X1, LANES)], block)
        return lax.all_gather(packed2, everywhere, axis=0)

    arrays, from_low, from_high, operators2 = exchange(FIRST, (*fields, coarse), low, high, gather_coarse)
    v0, g1, op0, s1, m1, low, high = call(
        presmooth0,
        [own0, own1, (5 * ZT0, XT0, 2 * LANES)] + [ext1] * 2 + [x_message(SECOND)] * 2,
        [ext0] * 4 + [(Z1 * X0, LANES)],
        *arrays, from_low, from_high, far_out=(2,),
    )
    arrays, from_low, from_high = exchange(SECOND, (g1, v0), low, high)
    stack0, stack1 = (5 * ZT0, XT0, 2 * LANES), (5 * ZT1, XT1, LANES)
    stack2, stack34 = (128, 32, LANES), (40, 32, LANES)
    message = ((W0 + 1) * XT0 + W1 * XT1, LANES)
    v1, v0, copies, op1, low, high = call(
        presmooth1,
        [(Z1, XT1, LANES), (Z0, XT0, 2 * LANES), (devices, 8, LANES), stack1] + [message] * 2,
        [ext1] * 2 + [(Z1 // 2 * X1, LANES)],
        arrays[0], arrays[1], s1, m1, from_low, from_high, far_out=(3,),
    )
    _, operators2 = lax.optimization_barrier((copies, operators2))
    forcing2 = lax.all_to_all(copies, everywhere, 0, 0)
    from_low, from_high = shift(low, high, "gz")
    level2, level3, level4 = (32, 32, LANES), (16, 16, LANES), (8, 8, LANES)
    operators, operators34 = call(
        coarse_operators,
        [stack2, stack34],
        [level2] * 2 + [level3] * 2 + [level4] * 2 + [(512, LANES)],
        operators2, far_in={0: operators2.shape}, far_out=(0, 1),
    )
    return call(
        finish,
        [(Z0, X0, Y0)] * 2,
        [ext1, ext1, ext0, ext0] + [level2] * 3 + [level3] * 3 + [level4] * 2 + [(14 * XT0, LANES)],
        operators, op1, op0, operators34, forcing2, v1, v0, from_low, from_high,
        place=place, far_in={0: stack2, 1: stack1, 2: stack0, 3: stack34}, late=(1, 2),
    )


def solution(mesh):
    spec = P("gz", "gx", "gy")
    return jax.shard_map(
        shards, mesh=mesh, in_specs=(spec,) * 3, out_specs=(spec,) * 2, check_vma=False
    )
```

```python
import math

import jax
import jax.numpy as jnp
from jax import lax
from jax.experimental import pallas as pl
from jax.experimental.pallas import tpu as pltpu
from jax.sharding import PartitionSpec as P

CSWEEPS = 32
DAMP = 0.8
KEEP = 1.0 - DAMP
W0 = 5
W1 = 7
G1 = 6
S1, F1 = 11, 10
Z0, X0, Y0 = 16, 32, 128
Z1, X1, Y1 = 8, 16, 64
ZT0, XT0 = Z0 + 2 * W0, 48
ZT1, XT1 = Z1 + 2 * W1, 40
LANES = 128
MIB = 1024 * 1024
F32 = jnp.float32


def lane_of(shape):
    return lax.broadcasted_iota(jnp.int32, shape, len(shape) - 1)


def row_of(shape):
    return lax.broadcasted_iota(jnp.int32, shape, len(shape) - 2)


def roll(x, shift, axis):
    size = x.shape[axis]
    shift = shift % size
    return x if shift == 0 else pltpu.roll(x, shift, axis)


def loop(first, last, body, step):
    chunks = (last - first) // step

    def chunk(c, carry):
        for k in range(step):
            body(first + c * step + k)
        return carry

    if chunks > 1:
        lax.fori_loop(0, chunks, chunk, 0)
    elif chunks:
        chunk(0, 0)
    for z in range(first + chunks * step, last):
        body(z)


def pick(x, index):
    return jnp.take_along_axis(x, index, axis=1)


def fold_lanes(x, first, count, target):
    to = lane_of(x.shape) - target
    index = (first + 2 * to) % LANES
    pairs = pick(x, index) + pick(x, (index + 1) % LANES)
    return jnp.where((to >= 0) & (to < count // 2), pairs, 0.0)


def spread_lanes(x, first=0):
    return pick(x, first + lane_of(x.shape) // 2)


class Far:
    def __init__(self, ins, outs, late):
        self.ins = {k: pltpu.make_async_copy(*pair) for k, pair in ins.items()}
        self.outs = {k: pltpu.make_async_copy(*pair) for k, pair in outs.items()}
        self.started = []
        self.start(*[k for k in self.ins if k not in late])

    def start(self, *keys):
        for k in keys:
            self.ins[k].start()

    def wait(self, *keys):
        for k in keys or tuple(self.ins):
            self.ins.pop(k).wait()

    def flush(self, *keys):
        for k in keys:
            self.outs[k].start()
            self.started.append(k)

    def finish(self):
        self.flush(*[k for k in self.outs if k not in self.started])
        for copy in self.outs.values():
            copy.wait()


def padded(shape):
    plane = 4 * math.prod(shape[1:])
    return (max(shape[0], -(-7 * MIB // plane)), *shape[1:])


def call(body, outs, scratch, *args, place=None, far_in={}, far_out=(), late=(), grant=48, pad=True):
    shapes = [
        jax.ShapeDtypeStruct(padded(shape) if pad and k in far_out else shape, F32)
        for k, shape in enumerate(outs)
    ]
    vmem = pl.BlockSpec(memory_space=pltpu.VMEM)
    hbm = pl.BlockSpec(memory_space=pltpu.HBM)
    specs = [hbm if k in far_in else vmem for k in range(len(args))]
    out_specs = [hbm if k in far_out else vmem for k in range(len(outs))]
    held = [pltpu.VMEM(shape, F32) for shape in far_in.values()]
    held += [pltpu.VMEM(outs[k], F32) for k in far_out]
    extra = len(far_in) + len(far_out)
    if extra:
        held.append(pltpu.SemaphoreType.DMA((extra,)))
    placed = place is not None
    count = len(args)

    def wrapped(*refs):
        refs = list(refs)
        head = [refs.pop(0)] if placed else []
        ins, results = refs[:count], refs[count : count + len(outs)]
        rest = refs[count + len(outs) :]
        mine, rest = rest[: len(scratch)], rest[len(scratch) :]
        copies_in, copies_out = {}, {}
        for j, k in enumerate(far_in):
            copies_in[k] = (ins[k].at[0 : far_in[k][0]], rest[j], rest[extra].at[j])
            ins[k] = rest[j]
        for j, k in enumerate(far_out, len(far_in)):
            copies_out[k] = (rest[j], results[k].at[0 : outs[k][0]], rest[extra].at[j])
            results[k] = rest[j]
        far = Far(copies_in, copies_out, late)
        body(far, *head, *ins, *results, *mine)
        far.finish()

    if placed:
        specs = [pl.BlockSpec(memory_space=pltpu.SMEM)] + specs
        args = (place,) + args
    return pl.pallas_call(
        wrapped,
        out_shape=shapes,
        in_specs=specs,
        out_specs=out_specs,
        scratch_shapes=[pltpu.VMEM(shape, F32) for shape in scratch] + held,
        compiler_params=pltpu.CompilerParams(vmem_limit_bytes=grant * MIB),
    )(*args)


class Item:
    def __init__(self, fields, planes, rows, rows_out, width, kind, trim=False, width_z=None, edge=0):
        self.n, self.z, self.x, self.xt, self.w, self.kind = fields, planes, rows, rows_out, width, kind
        self.wz = width if width_z is None else width_z
        self.zt = planes + 2 * self.wz
        self.edge = edge
        self.trim = trim
        self.tall = rows + 8 if trim else rows_out
        self.virtual = 2 * fields if kind == "pair" else fields
        self.own = LANES if kind == "full" else LANES // 2
        self.slots = LANES // width
        self.groups = -(-self.virtual * (self.zt - 2 * edge) // self.slots)
        self.rows_x = fields * planes * width
        self.rows_z = fields * self.wz * self.tall
        self.rows_y = self.groups * self.tall

    def narrow(self, plane):
        if not self.trim:
            return plane
        upper, lower = plane[self.x : self.x + 8], plane[self.xt - 8 : self.xt]
        rim = jnp.where(row_of(upper.shape) < 4, upper, lower)
        return jnp.concatenate([plane[: self.x], rim], axis=0)

    def widen(self, plane):
        if not self.trim:
            return plane
        rim = plane[self.x :]
        upper = jnp.where(row_of(rim.shape) < 4, rim, 0.0)
        return jnp.concatenate([plane[: self.x], upper, rim - upper], axis=0)


def total(counts):
    count = sum(counts)
    return -(-count // 8) * 8


def pack_x(items, refs, low, high):
    at = 0
    for item, ref in zip(items, refs):
        for n in range(item.n):
            for z in range(item.z):
                low[at : at + item.w, :] = ref[n, z, 0 : item.w, :]
                high[at : at + item.w, :] = ref[n, z, item.x - item.w : item.x, :]
                at += item.w


def unpack_x(items, refs, from_low, from_high, outs):
    at = 0
    for item, ref, out in zip(items, refs, outs):
        out[:, :, item.x :, :] = jnp.zeros((item.n, item.z, item.xt - item.x, LANES), F32)
        for n in range(item.n):
            for z in range(item.z):
                out[n, z, 0 : item.x, :] = ref[n, z]
                out[n, z, item.x : item.x + item.w, :] = from_high[at : at + item.w, :]
                out[n, z, item.xt - item.w :, :] = from_low[at : at + item.w, :]
                at += item.w


def pack_z(items, refs, low, high):
    at = 0
    for item, ref in zip(items, refs):
        for n in range(item.n):
            for w in range(item.wz):
                low[at : at + item.tall, :] = item.narrow(ref[n, w])
                high[at : at + item.tall, :] = item.narrow(ref[n, item.z - item.wz + w])
                at += item.tall


class Planes:
    def __init__(self, item, ref, from_low, from_high, base):
        self.item, self.ref, self.low, self.high, self.base = item, ref, from_low, from_high, base

    def received(self, n, z):
        item = self.item
        if item.wz <= z < item.wz + item.z:
            return None
        message, w = (self.low, z) if z < item.wz else (self.high, z - item.wz - item.z)
        at = self.base + (n * item.wz + w) * item.tall
        return message[at : at + item.tall, :]

    def whole(self, n, z):
        plane = self.received(n, z)
        return self.ref[n, z - self.item.wz] if plane is None else self.item.widen(plane)

    def narrow(self, n, z):
        plane = self.received(n, z)
        return self.item.narrow(self.ref[n, z - self.item.wz]) if plane is None else plane


def planes_of(items, refs, from_low, from_high):
    planes, base = [], 0
    for item, ref in zip(items, refs):
        planes.append(Planes(item, ref, from_low, from_high, base))
        base += item.rows_z
    return planes


def pack_y(items, sources, low, high):
    at = 0
    for item, source in zip(items, sources):
        lane = lane_of((item.tall, LANES))
        pairs = [(v, z) for v in range(item.virtual) for z in range(item.edge, item.zt - item.edge)]
        for g in range(item.groups):
            lows = jnp.zeros((item.tall, LANES), F32)
            highs = lows
            for k, (v, z) in enumerate(pairs[g * item.slots : (g + 1) * item.slots]):
                n, first = (v // 2, (v % 2) * item.own) if item.kind == "pair" else (v, 0)
                plane = source.narrow(n, z)
                place = k * item.w
                mask = (lane >= place) & (lane < place + item.w)
                lows = jnp.where(mask, roll(plane, place - first, 1), lows)
                highs = jnp.where(mask, roll(plane, place - first - item.own + item.w, 1), highs)
            low[at : at + item.tall, :] = lows
            high[at : at + item.tall, :] = highs
            at += item.tall


def unpack_y(items, sources, from_low, from_high, outs):
    at = 0
    for item, source, fields in zip(items, sources, outs):
        lane = lane_of((item.tall, LANES))
        for v in range(item.virtual if item.edge else 0):
            for z in [*range(item.edge), *range(item.zt - item.edge, item.zt)]:
                fields[v][z, :, 0:LANES] = source.whole(v, z)
                fields[v][z, :, LANES:] = jnp.zeros((item.xt, LANES), F32)
        pairs = [(v, z) for v in range(item.virtual) for z in range(item.edge, item.zt - item.edge)]
        for g in range(item.groups):
            lows = from_low[at : at + item.tall, :]
            highs = from_high[at : at + item.tall, :]
            at += item.tall
            for k, (v, z) in enumerate(pairs[g * item.slots : (g + 1) * item.slots]):
                place = k * item.w
                start = item.own % LANES
                upper = roll(highs, start - place, 1)
                lower = roll(lows, LANES - item.w - place, 1)
                rim = jnp.where(
                    lane < start + item.w, upper, jnp.where(lane >= LANES - item.w, lower, 0.0)
                )
                if item.kind == "full":
                    fields[v][z, :, 0:LANES] = source.whole(v, z)
                    fields[v][z, :, LANES:] = item.widen(rim)
                else:
                    plane = source.whole(v // 2 if item.kind == "pair" else v, z)
                    if item.kind == "pair" and v % 2:
                        plane = roll(plane, item.own, 1)
                    fields[v][z] = jnp.where(lane < item.own, plane, rim)


def shift(low, high, axis):
    count = lax.axis_size(axis)
    forward = [(i, i + 1) for i in range(count - 1)]
    backward = [(target, source) for source, target in forward]
    return lax.ppermute(high, axis, forward), lax.ppermute(low, axis, backward)


def exchange(items, arrays, low, high, beside=None):
    count = len(items)
    from_low, from_high = shift(low, high, "gx")
    shapes = [(item.n, item.z, item.xt, LANES) for item in items]
    message = (total(item.rows_z for item in items), LANES)

    def after_x(far, *refs):
        ins, (a, b), outs, (c, d) = refs[:count], refs[count : count + 2], refs[count + 2 : 2 * count + 2], refs[2 * count + 2 :]
        unpack_x(items, ins, a, b, outs)
        pack_z(items, outs, c, d)

    *arrays, low, high = call(after_x, shapes + [message] * 2, [], *arrays, from_low, from_high)
    extra = beside(low) if beside else None
    z_low, z_high = shift(low, high, "gz")
    message = (total(item.rows_y for item in items), LANES)

    def after_z(far, *refs):
        pack_y(items, planes_of(items, refs[:count], *refs[count : count + 2]), *refs[count + 2 :])

    low, high = call(after_z, [message] * 2, [], *arrays, z_low, z_high)
    received = (*arrays, z_low, z_high, *shift(low, high, "gy"))
    return (received, extra) if beside else received


STIFFNESS = Item(1, Z0, X0, XT0, W0, "full", True, edge=1)
INNER = Item(1, Z0, X0, XT0, W0 - 1, "full", True)
COARSE = Item(1, Z1, X1, XT1, S1, "pair", False, W1)
FORCING1 = Item(1, Z1, X1, XT1, F1, "half", False, G1)
POTENTIAL0 = Item(1, Z0, X0, XT0, W0, "full", False, 0)
FIRST, SECOND = (STIFFNESS, INNER, INNER, COARSE), (FORCING1, POTENTIAL0)


def x_message(items):
    return (total(item.rows_x for item in items), LANES)


def couple(s, m, r, cx, cy, cz, first, last, step, edges=False, start=None):
    planes, rows, lanes = s.shape

    def vertical(z):
        return 4.0 * jnp.minimum(s[z], s[z + 1])

    def one(z, below, above):
        here = s[z]
        x_face = jnp.minimum(here, roll(here, -1, 0))
        y_face = jnp.minimum(here, roll(here, -1, 1))
        if edges:
            x_face = jnp.where(row_of(here.shape) < rows - 1, x_face, 0.0)
            y_face = jnp.where(lane_of(here.shape) < lanes - 1, y_face, 0.0)
        cx[z] = x_face
        cy[z] = y_face
        cz[z] = above
        d = m[z] + below + above + x_face + roll(x_face, 1, 0) + y_face + roll(y_face, 1, 1)
        scale = DAMP / jnp.where(d > 0.0, d, 1.0)
        r[z] = scale
        if start:
            start[1][z] = scale * start[0][z]

    if edges:
        zero = jnp.zeros((rows, lanes), F32)
        one(0, zero, vertical(0))
        one(planes - 1, vertical(planes - 2), zero)
    else:
        cz[first - 1] = vertical(first - 1)
    loop(first + edges, last - edges, lambda z: one(z, vertical(z - 1), vertical(z)), step)


def gathered(v, f, cx, cy, cz, z, low=True, high=True):
    here = v[z]
    x_face, y_face = cx[z], cy[z]
    out = f[z]
    if high:
        out = out + cz[z] * v[z + 1]
    if low:
        out = out + cz[z - 1] * v[z - 1]
    out = out + x_face * roll(here, -1, 0) + roll(x_face * here, 1, 0)
    return here, out + y_face * roll(here, -1, 1) + roll(y_face * here, 1, 1)


def sweep(v, into, op, first, last, unroll, edges=False):
    r, f, cx, cy, cz = op

    def step(z, low=True, high=True):
        here, out = gathered(v, f, cx, cy, cz, z, low, high)
        into[z] = KEEP * here + r[z] * out

    if edges:
        step(first, low=False)
        step(last - 1, high=False)
        loop(first + 1, last - 1, step, unroll)
    else:
        loop(first, last, step, unroll)


def remain(v, op, z, low=True, high=True):
    r, f, cx, cy, cz = op
    here, out = gathered(v, f, cx, cy, cz, z, low, high)
    return out - here * (DAMP / r[z])


def first_sweep(v, op, first, last):
    r, f = op[:2]

    def step(z):
        v[z] = r[z] * f[z]

    loop(first, last, step, 4)


def prepare(far, stiffness, forcing, mass, coarse, low, high, tall):
    out = None
    for ref, scale, target in ((stiffness, 0.25, 0), (mass, 1.0, Y1)):
        for z in range(Z1):
            tall[z * X0 : (z + 1) * X0, :] = ref[0, 2 * z] + ref[0, 2 * z + 1]
        rows = tall[pl.ds(0, Z1 * X1, stride=2), :] + tall[pl.ds(1, Z1 * X1, stride=2), :]
        part = scale * fold_lanes(rows, 0, LANES, target)
        out = part if out is None else out + part
    for z in range(Z1):
        coarse[0, z] = out[z * X1 : (z + 1) * X1, :]
    pack_x(FIRST, (stiffness, forcing, mass, coarse), low, high)


def prepare_coarse(far, coarse, packed2, tall):
    for part, scale in ((0, 0.25), (1, 1.0)):
        packed2[part * 8 : part * 8 + 8, :] = scale * pack_coarse(
            lambda z: coarse[0, z], part * Y1, tall
        )


def pack_coarse(plane, first, tall):
    for z in range(Z1 // 2):
        tall[z * X1 : (z + 1) * X1, :] = plane(2 * z) + plane(2 * z + 1)
    count = Z1 // 2 * X1 // 2
    rows = tall[pl.ds(0, count, stride=2), :] + tall[pl.ds(1, count, stride=2), :]
    out = jnp.zeros((X1 // 2, LANES), F32)
    for z in range(Z1 // 2):
        part = rows[z * X1 // 2 : (z + 1) * X1 // 2, :]
        out = out + fold_lanes(part, first, Y1, z * Y1 // 2)
    return out


def parts(ref, planes, count=5):
    return [ref.at[k * planes : (k + 1) * planes] for k in range(count)]


def presmooth0(
    far, x_s, x_f, x_m, x_coarse, z_low, z_high, from_low, from_high,
    v_own, g_own, op, s1, m1, low, high,
    s, m, va, vb, tall,
):
    r, f, cx, cy, cz = parts(op, ZT0)
    inner = slice(1, ZT0 - 1)
    unpack_y(
        FIRST, planes_of(FIRST, (x_s, x_f, x_m, x_coarse), z_low, z_high), from_low, from_high,
        ([s], [f.at[inner]], [m.at[inner]], [s1, m1]),
    )
    couple(s, m, r, cx, cy, cz, 1, ZT0 - 1, 8, start=(f, va))
    far.flush(2)
    op = (r, f, cx, cy, cz)
    sweep(va, vb, op, 2, ZT0 - 2, 11)
    sweep(vb, va, op, 3, ZT0 - 3, 10)
    sweep(va, vb, op, 4, ZT0 - 4, 9)
    for z in range(Z1):
        a, b = W0 + 2 * z, W0 + 2 * z + 1
        plane = remain(vb, op, a) + remain(vb, op, b)
        tall[z * X0 : (z + 1) * X0, :] = plane[0:X0, 0:Y0]
    rows = tall[pl.ds(0, Z1 * X1, stride=2), :] + tall[pl.ds(1, Z1 * X1, stride=2), :]
    out = fold_lanes(rows, 0, LANES, 0)
    for z in range(Z1):
        g_own[0, z] = out[z * X1 : (z + 1) * X1, :]
    for z in range(Z0):
        v_own[0, z] = vb[W0 + z, 0:X0, 0:Y0]
    pack_x(SECOND, (g_own, v_own), low, high)


def presmooth1(
    far, g_x, v0_x, z_low, z_high, from_low, from_high, s, m,
    v_own, v0, copies, op, low, high,
    va, vb, tall,
):
    r, g, cx, cy, cz = parts(op, ZT1)
    for k in range(W1 - G1):
        g[k] = jnp.zeros((XT1, LANES), F32)
        g[ZT1 - 1 - k] = jnp.zeros((XT1, LANES), F32)
    inner = g.at[W1 - G1 : ZT1 - (W1 - G1)]
    unpack_y(SECOND, planes_of(SECOND, (g_x, v0_x), z_low, z_high), from_low, from_high, ([inner], [v0]))
    couple(s, m, r, cx, cy, cz, 1, ZT1 - 1, 10, start=(g, va))
    far.flush(3)
    op = (r, g, cx, cy, cz)
    sweep(va, vb, op, 4, ZT1 - 4, 10)
    sweep(vb, va, op, 5, ZT1 - 5, 10)
    sweep(va, vb, op, 6, ZT1 - 6, 10)
    packed = pack_coarse(lambda z: remain(vb, op, W1 + z)[0:X1, :], 0, tall)
    for d in range(copies.shape[0]):
        copies[d] = packed
    for z in range(Z1):
        v_own[z] = vb[W1 + z]
    lane = lane_of((XT0, LANES))
    base = (W0 + 1) * XT0
    for message, first0, first1 in ((low, 0, 0), (high, Z0 - W0, Z1 - W1)):
        rims = jnp.zeros((XT0, LANES), F32)
        for w in range(W0):
            message[w * XT0 : (w + 1) * XT0, :] = v0[first0 + w, :, 0:LANES]
            here = (lane >= 2 * W0 * w) & (lane < 2 * W0 * (w + 1))
            rims = jnp.where(here, roll(v0[first0 + w, :, LANES:], W0 + 2 * W0 * w, 1), rims)
        message[W0 * XT0 : base, :] = rims
        for w in range(W1):
            message[base + w * XT1 : base + (w + 1) * XT1, :] = v_own[first1 + w]


def unpack_whole(blocks, first, out):
    group = lane_of((8, LANES)) // 32

    def body(step):
        gz, gx = step // 4, step % 4
        for z in range(4):
            plane = None
            for gy in range(4):
                block = blocks[step * 4 + gy, first : first + 8, :]
                moved = roll(block, (gy - z) * 32, 1)
                plane = moved if plane is None else jnp.where(group == gy, moved, plane)
            out[gz * 4 + z, pl.ds(pl.multiple_of(gx * 8, 8), 8), :] = plane

    loop(0, 32, body, 4)


def fold_whole(plane, planes, rows, scale, tall, out):
    half = rows // 2
    for z in range(planes // 2):
        tall[z * rows : (z + 1) * rows, :] = plane(2 * z) + plane(2 * z + 1)
    count = planes // 2 * half
    folded = tall[pl.ds(0, count, stride=2), :] + tall[pl.ds(1, count, stride=2), :]
    folded = scale * fold_lanes(folded, 0, LANES, 0)
    for z in range(planes // 2):
        out[z] = folded[z * half : (z + 1) * half, :]


def spread_whole(v, planes, rows, tall, add):
    count = planes * rows
    flat = spread_lanes(jnp.concatenate([v[z] for z in range(planes)], axis=0))
    tall[pl.ds(0, count, stride=2), :] = flat
    tall[pl.ds(1, count, stride=2), :] = flat
    for z in range(planes):
        spread = tall[z * 2 * rows : (z + 1) * 2 * rows, :]
        add[2 * z] = add[2 * z] + spread
        add[2 * z + 1] = add[2 * z + 1] + spread


def coarsest(out, op):
    r, f, cx, cy, cz = op
    forced, upper, lower = [], [], []
    for z in range(8):
        scale = r[z]
        forced.append(scale * f[z])
        above = scale * cz[z]
        below = scale * cz[z - 1] if z else None
        upper.append((above, scale * cx[z], scale * cy[z]))
        lower.append((below, scale * roll(cx[z], 1, 0), scale * roll(cy[z], 1, 1)))

    def step(k, v):
        new = []
        for z in range(8):
            here = v[z]
            east = upper[z][2] * roll(here, -1, 1) + lower[z][2] * roll(here, 1, 1)
            north = upper[z][1] * roll(here, -1, 0) + lower[z][1] * roll(here, 1, 0)
            base = KEEP * here + forced[z]
            if z < 7:
                base = base + upper[z][0] * v[z + 1]
            if z:
                base = base + lower[z][0] * v[z - 1]
            new.append((base + north) + east)
        return tuple(new)

    v = lax.fori_loop(0, CSWEEPS - 1, step, tuple(forced), unroll=True)
    for z in range(8):
        out[z] = v[z]


def levels(stacked2, stacked34):
    level3 = [stacked34.at[16 * (k // 2) : 16 * (k // 2) + 16, 16 * (k % 2) : 16 * (k % 2) + 16, :] for k in range(4)]
    level4 = [stacked34.at[32:40, 8 * k : 8 * k + 8, :] for k in range(4)]
    return parts(stacked2, 32, 4), level3, level4


def coarse_operators(
    far, operators,
    stacked2, stacked34,
    s2, m2, s3, m3, s4, m4, tall,
):
    (r2, cx2, cy2, cz2), (r3, cx3, cy3, cz3), (r4, cx4, cy4, cz4) = levels(stacked2, stacked34)
    far.wait()
    unpack_whole(operators, 0, s2)
    unpack_whole(operators, 8, m2)
    couple(s2, m2, r2, cx2, cy2, cz2, 0, 32, 10, True)
    far.flush(0)
    fold_whole(lambda z: s2[z], 32, 32, 0.25, tall, s3)
    fold_whole(lambda z: m2[z], 32, 32, 1.0, tall, m3)
    couple(s3, m3, r3, cx3, cy3, cz3, 0, 16, 14, True)
    fold_whole(lambda z: s3[z], 16, 16, 0.25, tall, s4)
    fold_whole(lambda z: m3[z], 16, 16, 1.0, tall, m4)
    couple(s4, m4, r4, cx4, cy4, cz4, 0, 8, 6, True)


def coarse_cycle(
    far, forcing, stacked2, stacked34, out,
    f2, vb2, f3, va3, vb3, f4, vb4, tall, meanwhile,
):
    unpack_whole(forcing, 0, f2)
    far.wait(0, 3)
    far.start(1, 2)
    (r2, cx2, cy2, cz2), (r3, cx3, cy3, cz3), (r4, cx4, cy4, cz4) = levels(stacked2, stacked34)
    op2 = (r2, f2, cx2, cy2, cz2)
    op3 = (r3, f3, cx3, cy3, cz3)
    op4 = (r4, f4, cx4, cy4, cz4)
    va2 = out

    def four(va, vb, op, planes):
        sweep(va, vb, op, 0, planes, 30, True)
        sweep(vb, va, op, 0, planes, 30, True)

    def residue(v, op, planes):
        return lambda z: remain(v, op, z, z > 0, z < planes - 1)

    first_sweep(vb2, op2, 0, 32)
    sweep(vb2, va2, op2, 0, 32, 30, True)
    four(va2, vb2, op2, 32)
    fold_whole(residue(va2, op2, 32), 32, 32, 1.0, tall, f3)
    first_sweep(vb3, op3, 0, 16)
    sweep(vb3, va3, op3, 0, 16, 15, True)
    four(va3, vb3, op3, 16)
    fold_whole(residue(va3, op3, 16), 16, 16, 1.0, tall, f4)
    meanwhile()
    coarsest(vb4, op4)
    spread_whole(vb4, 8, 8, tall, va3)
    four(va3, vb3, op3, 16)
    four(va3, vb3, op3, 16)
    spread_whole(va3, 16, 16, tall, va2)
    four(va2, vb2, op2, 32)
    four(va2, vb2, op2, 32)


def finish(
    far, place, stacked2, stacked1, stacked0, stacked34, forcing, v1, v0_zx, from_low, from_high,
    potential, residual,
    va1, vb1, v0, vb0, correction, f2, vb2, f3, va3, vb3, f4, vb4, tall,
):
    def meanwhile():
        base = (W0 + 1) * XT0
        for message, first0, first1 in ((from_low, 0, 0), (from_high, W0 + Z0, W1 + Z1)):
            rims = message[W0 * XT0 : base, :]
            for w in range(W0):
                v0[first0 + w, :, 0:LANES] = message[w * XT0 : (w + 1) * XT0, :]
                v0[first0 + w, :, LANES:] = roll(rims, -W0 - 2 * W0 * w, 1)
            for w in range(W1):
                va1[first1 + w] = message[base + w * XT1 : base + (w + 1) * XT1, :]
        for z in range(Z0):
            v0[W0 + z] = v0_zx[z]
        for z in range(Z1):
            va1[W1 + z] = v1[z]

    coarse_cycle(far, forcing, stacked2, stacked34, correction, f2, vb2, f3, va3, vb3, f4, vb4, tall, meanwhile)
    gz, gx, gy = place[0], place[1], place[2]
    planes = []
    for k in range(12):
        plane = correction[(gz * 4 + 28 + k) % 32]
        plane = pltpu.roll(plane, (32 - gx * 8) % 32, 0)
        plane = pltpu.roll(plane, (LANES - gy * 32) % LANES, 1)
        planes += [plane[0:14], plane[26:32]]
    flat = jnp.concatenate(planes, axis=0)
    fine = lane_of(flat.shape)
    flat = pick(flat, fine // 2 + jnp.where(fine < 96, 0, 64))
    count = 12 * 20
    tall[pl.ds(0, count, stride=2), :] = flat
    tall[pl.ds(1, count, stride=2), :] = flat
    for z in range(ZT1):
        k = (z + 1) // 2
        va1[z] = va1[z] + tall[k * XT1 : (k + 1) * XT1, :]
    far.wait(1)
    op1 = parts(stacked1, ZT1)
    sweep(va1, vb1, op1, 1, ZT1 - 1, 20)
    sweep(vb1, va1, op1, 2, ZT1 - 2, 18)
    sweep(va1, vb1, op1, 3, ZT1 - 3, 16)
    sweep(vb1, va1, op1, 4, ZT1 - 4, 14)
    planes = []
    for k in range(14):
        planes += [va1[4 + k, 0:20, :], va1[4 + k, XT1 - 4 : XT1, :]]
    flat = jnp.concatenate(planes, axis=0)
    count = 14 * 24
    for half in range(2):
        part = spread_lanes(flat, 64 * half)
        tall[pl.ds(0, count, stride=2), :] = part
        tall[pl.ds(1, count, stride=2), :] = part
        for z in range(ZT0):
            k = (z + 1) // 2
            at = slice(half * LANES, (half + 1) * LANES)
            v0[z, :, at] = v0[z, :, at] + tall[k * XT0 : (k + 1) * XT0, :]
    far.wait(2)
    op0 = parts(stacked0, ZT0)
    sweep(v0, vb0, op0, 1, ZT0 - 1, 12)
    sweep(vb0, v0, op0, 2, ZT0 - 2, 11)
    sweep(v0, vb0, op0, 3, ZT0 - 3, 10)
    sweep(vb0, v0, op0, 4, ZT0 - 4, 9)
    for z in range(Z0):
        potential[z] = v0[W0 + z, 0:X0, 0:Y0]
    far.flush(0)
    for z in range(Z0):
        residual[z] = remain(v0, op0, W0 + z)[0:X0, 0:Y0]


def shards(source, conductivity, cell_kind):
    own0, own1 = (1, Z0, X0, Y0), (1, Z1, X1, LANES)
    ext0, ext1 = (ZT0, XT0, 2 * LANES), (ZT1, XT1, LANES)
    everywhere = ("gz", "gx", "gy")
    devices = math.prod(lax.axis_size(axis) for axis in everywhere)
    place = jnp.stack([lax.axis_index(axis) for axis in everywhere]).astype(jnp.int32)
    wet = jnp.where(cell_kind > 0, 1.0, 0.0).astype(F32)
    surface = jnp.where(cell_kind == 2, 1.0, 0.0).astype(F32)
    stiffness = conductivity * wet
    mass = 0.005 * stiffness + 8.0 * stiffness * surface + 0.02 * (1.0 - wet)
    fields = [array.reshape(own0) for array in (stiffness, source * wet, mass)]
    coarse, low, high = call(
        prepare, [own1] + [x_message(FIRST)] * 2, [(Z1 * X0, LANES)], *fields
    )

    def gather_coarse(message):
        block, _ = lax.optimization_barrier((coarse, message))
        (packed2,) = call(prepare_coarse, [(16, LANES)], [(Z1 // 2 * X1, LANES)], block)
        return lax.all_gather(packed2, everywhere, axis=0)

    received, operators2 = exchange(FIRST, (*fields, coarse), low, high, gather_coarse)
    v0, g1, op0, s1, m1, low, high = call(
        presmooth0,
        [own0, own1, (5 * ZT0, XT0, 2 * LANES)] + [ext1] * 2 + [x_message(SECOND)] * 2,
        [ext0] * 4 + [(Z1 * X0, LANES)],
        *received, far_out=(2,),
    )
    received = exchange(SECOND, (g1, v0), low, high)
    stack0, stack1 = (5 * ZT0, XT0, 2 * LANES), (5 * ZT1, XT1, LANES)
    stack2, stack34 = (128, 32, LANES), (40, 32, LANES)
    message = ((W0 + 1) * XT0 + W1 * XT1, LANES)
    v1, v0, copies, op1, low, high = call(
        presmooth1,
        [(Z1, XT1, LANES), (Z0, XT0, 2 * LANES), (devices, 8, LANES), stack1] + [message] * 2,
        [ext1] * 2 + [(Z1 // 2 * X1, LANES)],
        *received, s1, m1, far_out=(3,),
    )
    _, operators2 = lax.optimization_barrier((copies, operators2))
    forcing2 = lax.all_to_all(copies, everywhere, 0, 0)
    from_low, from_high = shift(low, high, "gz")
    level2, level3, level4 = (32, 32, LANES), (16, 16, LANES), (8, 8, LANES)
    operators, operators34 = call(
        coarse_operators,
        [stack2, stack34],
        [level2] * 2 + [level3] * 2 + [level4] * 2 + [(512, LANES)],
        operators2, far_in={0: operators2.shape}, far_out=(0, 1),
    )
    return call(
        finish,
        [(Z0, X0, Y0)] * 2,
        [ext1, ext1, ext0, ext0] + [level2] * 3 + [level3] * 3 + [level4] * 2 + [(14 * XT0, LANES)],
        operators, op1, op0, operators34, forcing2, v1, v0, from_low, from_high,
        place=place, far_in={0: stack2, 1: stack1, 2: stack0, 3: stack34}, late=(1, 2),
        far_out=(0, 1), pad=False,
    )


def solution(mesh):
    spec = P("gz", "gx", "gy")
    return jax.shard_map(
        shards, mesh=mesh, in_specs=(spec,) * 3, out_specs=(spec,) * 2, check_vma=False
    )
```

```python
import math

import jax
import jax.numpy as jnp
from jax import lax
from jax.experimental import pallas as pl
from jax.experimental.pallas import tpu as pltpu
from jax.sharding import PartitionSpec as P

CSWEEPS = 32
DAMP = 0.8
KEEP = 1.0 - DAMP
W0 = 5
W1 = 7
G1 = 6
S1, F1 = 11, 10
Z0, X0, Y0 = 16, 32, 128
Z1, X1, Y1 = 8, 16, 64
ZT0, XT0, EVEN = Z0 + 2 * W0, 48, 24
ZT1, XT1 = Z1 + 2 * W1, 40
LANES = 128
MIB = 1024 * 1024
F32 = jnp.float32


def lane_of(shape):
    return lax.broadcasted_iota(jnp.int32, shape, len(shape) - 1)


def row_of(shape):
    return lax.broadcasted_iota(jnp.int32, shape, len(shape) - 2)


def roll(x, shift, axis):
    size = x.shape[axis]
    shift = shift % size
    return x if shift == 0 else pltpu.roll(x, shift, axis)


def loop(first, last, body, step):
    chunks = (last - first) // step

    def chunk(c, carry):
        for k in range(step):
            body(first + c * step + k)
        return carry

    if chunks > 1:
        lax.fori_loop(0, chunks, chunk, 0)
    elif chunks:
        chunk(0, 0)
    for z in range(first + chunks * step, last):
        body(z)


def pick(x, index):
    return jnp.take_along_axis(x, index, axis=1)


def fold_lanes(x, first, count, target):
    to = lane_of(x.shape) - target
    index = (first + 2 * to) % LANES
    pairs = pick(x, index) + pick(x, (index + 1) % LANES)
    return jnp.where((to >= 0) & (to < count // 2), pairs, 0.0)


def spread_lanes(x, first=0):
    return pick(x, first + lane_of(x.shape) // 2)


class Far:
    def __init__(self, ins, outs, late):
        self.ins = {k: pltpu.make_async_copy(*pair) for k, pair in ins.items()}
        self.outs = {k: pltpu.make_async_copy(*pair) for k, pair in outs.items()}
        self.started = []
        self.start(*[k for k in self.ins if k not in late])

    def start(self, *keys):
        for k in keys:
            self.ins[k].start()

    def wait(self, *keys):
        for k in keys or tuple(self.ins):
            self.ins.pop(k).wait()

    def flush(self, *keys):
        for k in keys:
            self.outs[k].start()
            self.started.append(k)

    def finish(self):
        self.flush(*[k for k in self.outs if k not in self.started])
        for copy in self.outs.values():
            copy.wait()


def padded(shape):
    plane = 4 * math.prod(shape[1:])
    return (max(shape[0], -(-7 * MIB // plane)), *shape[1:])


def call(body, outs, scratch, *args, place=None, far_in={}, far_out=(), late=(), grant=48, pad=True):
    shapes = [
        jax.ShapeDtypeStruct(padded(shape) if pad and k in far_out else shape, F32)
        for k, shape in enumerate(outs)
    ]
    vmem = pl.BlockSpec(memory_space=pltpu.VMEM)
    hbm = pl.BlockSpec(memory_space=pltpu.HBM)
    specs = [hbm if k in far_in else vmem for k in range(len(args))]
    out_specs = [hbm if k in far_out else vmem for k in range(len(outs))]
    held = [pltpu.VMEM(shape, F32) for shape in far_in.values()]
    held += [pltpu.VMEM(outs[k], F32) for k in far_out]
    extra = len(far_in) + len(far_out)
    if extra:
        held.append(pltpu.SemaphoreType.DMA((extra,)))
    placed = place is not None
    count = len(args)

    def wrapped(*refs):
        refs = list(refs)
        head = [refs.pop(0)] if placed else []
        ins, results = refs[:count], refs[count : count + len(outs)]
        rest = refs[count + len(outs) :]
        mine, rest = rest[: len(scratch)], rest[len(scratch) :]
        copies_in, copies_out = {}, {}
        for j, k in enumerate(far_in):
            copies_in[k] = (ins[k].at[0 : far_in[k][0]], rest[j], rest[extra].at[j])
            ins[k] = rest[j]
        for j, k in enumerate(far_out, len(far_in)):
            copies_out[k] = (rest[j], results[k].at[0 : outs[k][0]], rest[extra].at[j])
            results[k] = rest[j]
        far = Far(copies_in, copies_out, late)
        body(far, *head, *ins, *results, *mine)
        far.finish()

    if placed:
        specs = [pl.BlockSpec(memory_space=pltpu.SMEM)] + specs
        args = (place,) + args
    return pl.pallas_call(
        wrapped,
        out_shape=shapes,
        in_specs=specs,
        out_specs=out_specs,
        scratch_shapes=[pltpu.VMEM(shape, F32) for shape in scratch] + held,
        compiler_params=pltpu.CompilerParams(vmem_limit_bytes=grant * MIB),
    )(*args)


class Item:
    def __init__(self, fields, planes, rows, rows_out, width, kind, trim=False, width_z=None, edge=0):
        self.n, self.z, self.x, self.xt, self.w, self.kind = fields, planes, rows, rows_out, width, kind
        self.wz = width if width_z is None else width_z
        self.zt = planes + 2 * self.wz
        self.edge = edge
        self.trim = trim
        self.tall = rows + 8 if trim else rows_out
        self.virtual = 2 * fields if kind == "pair" else fields
        self.own = LANES if kind == "full" else LANES // 2
        self.slots = LANES // width
        self.groups = -(-self.virtual * (self.zt - 2 * edge) // self.slots)
        self.rows_x = fields * planes * width
        self.rows_z = fields * self.wz * self.tall
        self.rows_y = self.groups * self.tall

    def narrow(self, plane):
        if not self.trim:
            return plane
        even, odd = plane[16:24], plane[40:48]
        rim = jnp.where(reached(even), even, roll(odd, 4, 0))
        return jnp.concatenate([plane[0:16], plane[24:40], rim], axis=0)

    def widen(self, plane):
        if not self.trim:
            return plane
        rim = plane[32:40]
        even = jnp.where(reached(rim), rim, 0.0)
        odd = jnp.where(reached(rim), roll(rim, 4, 0), 0.0)
        return jnp.concatenate([plane[0:16], even, plane[16:32], odd], axis=0)


def reached(rim):
    return (row_of(rim.shape) < 2) | (row_of(rim.shape) >= 6)


def every_other(first, count):
    return pl.ds(first, count, stride=2)


def total(counts):
    count = sum(counts)
    return -(-count // 8) * 8


def pack_x(items, refs, low, high):
    at = 0
    for item, ref in zip(items, refs):
        for n in range(item.n):
            for z in range(item.z):
                low[at : at + item.w, :] = ref[n, z, 0 : item.w, :]
                high[at : at + item.w, :] = ref[n, z, item.x - item.w : item.x, :]
                at += item.w


def unpack_x(items, refs, from_low, from_high, outs):
    at = 0
    for item, ref, out in zip(items, refs, outs):
        w = item.w
        if item.kind == "full":
            for first in (16, 40):
                out[:, :, first : first + 8, :] = jnp.zeros((item.n, item.z, 8, LANES), F32)
        else:
            out[:, :, item.x :, :] = jnp.zeros((item.n, item.z, item.xt - item.x, LANES), F32)
        for n in range(item.n):
            for z in range(item.z):
                if item.kind == "full":
                    more, less = (w + 1) // 2, w // 2
                    out[n, z, 0:16, :] = ref[n, z, every_other(0, 16), :]
                    out[n, z, 24:40, :] = ref[n, z, every_other(1, 16), :]
                    out[n, z, 16 : 16 + more, :] = from_high[every_other(at, more), :]
                    out[n, z, 40 : 40 + less, :] = from_high[every_other(at + 1, less), :]
                    out[n, z, 24 - less : 24, :] = from_low[every_other(at + w % 2, less), :]
                    out[n, z, 48 - more : 48, :] = from_low[every_other(at + 1 - w % 2, more), :]
                else:
                    out[n, z, 0 : item.x, :] = ref[n, z]
                    out[n, z, item.x : item.x + w, :] = from_high[at : at + w, :]
                    out[n, z, item.xt - w :, :] = from_low[at : at + w, :]
                at += w


def pack_z(items, refs, low, high):
    at = 0
    for item, ref in zip(items, refs):
        for n in range(item.n):
            for w in range(item.wz):
                low[at : at + item.tall, :] = item.narrow(ref[n, w])
                high[at : at + item.tall, :] = item.narrow(ref[n, item.z - item.wz + w])
                at += item.tall


class Planes:
    def __init__(self, item, ref, from_low, from_high, base):
        self.item, self.ref, self.low, self.high, self.base = item, ref, from_low, from_high, base

    def received(self, n, z):
        item = self.item
        if item.wz <= z < item.wz + item.z:
            return None
        message, w = (self.low, z) if z < item.wz else (self.high, z - item.wz - item.z)
        at = self.base + (n * item.wz + w) * item.tall
        return message[at : at + item.tall, :]

    def whole(self, n, z):
        plane = self.received(n, z)
        return self.ref[n, z - self.item.wz] if plane is None else self.item.widen(plane)

    def narrow(self, n, z):
        plane = self.received(n, z)
        return self.item.narrow(self.ref[n, z - self.item.wz]) if plane is None else plane


def planes_of(items, refs, from_low, from_high):
    planes, base = [], 0
    for item, ref in zip(items, refs):
        planes.append(Planes(item, ref, from_low, from_high, base))
        base += item.rows_z
    return planes


def pack_y(items, sources, low, high):
    at = 0
    for item, source in zip(items, sources):
        lane = lane_of((item.tall, LANES))
        pairs = [(v, z) for v in range(item.virtual) for z in range(item.edge, item.zt - item.edge)]
        for g in range(item.groups):
            lows = jnp.zeros((item.tall, LANES), F32)
            highs = lows
            for k, (v, z) in enumerate(pairs[g * item.slots : (g + 1) * item.slots]):
                n, first = (v // 2, (v % 2) * item.own) if item.kind == "pair" else (v, 0)
                plane = source.narrow(n, z)
                place = k * item.w
                mask = (lane >= place) & (lane < place + item.w)
                lows = jnp.where(mask, roll(plane, place - first, 1), lows)
                highs = jnp.where(mask, roll(plane, place - first - item.own + item.w, 1), highs)
            low[at : at + item.tall, :] = lows
            high[at : at + item.tall, :] = highs
            at += item.tall


def unpack_y(items, sources, from_low, from_high, outs):
    at = 0
    for item, source, fields in zip(items, sources, outs):
        lane = lane_of((item.tall, LANES))
        for v in range(item.virtual if item.edge else 0):
            for z in [*range(item.edge), *range(item.zt - item.edge, item.zt)]:
                fields[v][z, :, 0:LANES] = source.whole(v, z)
                fields[v][z, :, LANES:] = jnp.zeros((item.xt, LANES), F32)
        pairs = [(v, z) for v in range(item.virtual) for z in range(item.edge, item.zt - item.edge)]
        for g in range(item.groups):
            lows = from_low[at : at + item.tall, :]
            highs = from_high[at : at + item.tall, :]
            at += item.tall
            for k, (v, z) in enumerate(pairs[g * item.slots : (g + 1) * item.slots]):
                place = k * item.w
                start = item.own % LANES
                upper = roll(highs, start - place, 1)
                lower = roll(lows, LANES - item.w - place, 1)
                rim = jnp.where(
                    lane < start + item.w, upper, jnp.where(lane >= LANES - item.w, lower, 0.0)
                )
                if item.kind == "full":
                    fields[v][z, :, 0:LANES] = source.whole(v, z)
                    fields[v][z, :, LANES:] = item.widen(rim)
                else:
                    plane = source.whole(v // 2 if item.kind == "pair" else v, z)
                    if item.kind == "pair" and v % 2:
                        plane = roll(plane, item.own, 1)
                    fields[v][z] = jnp.where(lane < item.own, plane, rim)


def shift(low, high, axis):
    count = lax.axis_size(axis)
    forward = [(i, i + 1) for i in range(count - 1)]
    backward = [(target, source) for source, target in forward]
    return lax.ppermute(high, axis, forward), lax.ppermute(low, axis, backward)


def exchange(items, arrays, low, high, beside=None):
    count = len(items)
    from_low, from_high = shift(low, high, "gx")
    shapes = [(item.n, item.z, item.xt, LANES) for item in items]
    message = (total(item.rows_z for item in items), LANES)

    def after_x(far, *refs):
        ins, (a, b), outs, (c, d) = refs[:count], refs[count : count + 2], refs[count + 2 : 2 * count + 2], refs[2 * count + 2 :]
        unpack_x(items, ins, a, b, outs)
        pack_z(items, outs, c, d)

    *arrays, low, high = call(after_x, shapes + [message] * 2, [], *arrays, from_low, from_high)
    extra = beside(low) if beside else None
    z_low, z_high = shift(low, high, "gz")
    message = (total(item.rows_y for item in items), LANES)

    def after_z(far, *refs):
        pack_y(items, planes_of(items, refs[:count], *refs[count : count + 2]), *refs[count + 2 :])

    low, high = call(after_z, [message] * 2, [], *arrays, z_low, z_high)
    received = (*arrays, z_low, z_high, *shift(low, high, "gy"))
    return (received, extra) if beside else received


STIFFNESS = Item(1, Z0, X0, XT0, W0, "full", True, edge=1)
INNER = Item(1, Z0, X0, XT0, W0 - 1, "full", True)
COARSE = Item(1, Z1, X1, XT1, S1, "pair", False, W1)
FORCING1 = Item(1, Z1, X1, XT1, F1, "half", False, G1)
POTENTIAL0 = Item(1, Z0, X0, XT0, W0, "full", False, 0)
FIRST, SECOND = (STIFFNESS, INNER, INNER, COARSE), (FORCING1, POTENTIAL0)


def x_message(items):
    return (total(item.rows_x for item in items), LANES)


def x_above(plane):
    if plane.shape[0] != XT0:
        return roll(plane, -1, 0)
    return jnp.concatenate([plane[EVEN:], roll(plane[:EVEN], -1, 0)], axis=0)


def x_below(plane):
    if plane.shape[0] != XT0:
        return roll(plane, 1, 0)
    return jnp.concatenate([roll(plane[EVEN:], 1, 0), plane[:EVEN]], axis=0)


def couple(s, m, r, cx, cy, cz, first, last, step, edges=False, start=None):
    planes, rows, lanes = s.shape

    def vertical(z):
        return 4.0 * jnp.minimum(s[z], s[z + 1])

    def one(z, below, above):
        here = s[z]
        x_face = jnp.minimum(here, x_above(here))
        y_face = jnp.minimum(here, roll(here, -1, 1))
        if edges:
            x_face = jnp.where(row_of(here.shape) < rows - 1, x_face, 0.0)
            y_face = jnp.where(lane_of(here.shape) < lanes - 1, y_face, 0.0)
        cx[z] = x_face
        cy[z] = y_face
        cz[z] = above
        d = m[z] + below + above + x_face + x_below(x_face) + y_face + roll(y_face, 1, 1)
        scale = DAMP / jnp.where(d > 0.0, d, 1.0)
        r[z] = scale
        if start:
            start[1][z] = scale * start[0][z]

    if edges:
        zero = jnp.zeros((rows, lanes), F32)
        one(0, zero, vertical(0))
        one(planes - 1, vertical(planes - 2), zero)
    else:
        cz[first - 1] = vertical(first - 1)
    loop(first + edges, last - edges, lambda z: one(z, vertical(z - 1), vertical(z)), step)


def gathered(v, f, cx, cy, cz, z, low=True, high=True):
    here = v[z]
    x_face, y_face = cx[z], cy[z]
    out = f[z]
    if high:
        out = out + cz[z] * v[z + 1]
    if low:
        out = out + cz[z - 1] * v[z - 1]
    out = out + x_face * x_above(here) + x_below(x_face * here)
    return here, out + y_face * roll(here, -1, 1) + roll(y_face * here, 1, 1)


def sweep(v, into, op, first, last, unroll, edges=False):
    r, f, cx, cy, cz = op

    def step(z, low=True, high=True):
        here, out = gathered(v, f, cx, cy, cz, z, low, high)
        into[z] = KEEP * here + r[z] * out

    if edges:
        step(first, low=False)
        step(last - 1, high=False)
        loop(first + 1, last - 1, step, unroll)
    else:
        loop(first, last, step, unroll)


def remain(v, op, z, low=True, high=True):
    r, f, cx, cy, cz = op
    here, out = gathered(v, f, cx, cy, cz, z, low, high)
    return out - here * (DAMP / r[z])


def first_sweep(v, op, first, last):
    r, f = op[:2]

    def step(z):
        v[z] = r[z] * f[z]

    loop(first, last, step, 4)


def prepare(far, stiffness, forcing, mass, coarse, low, high, tall):
    out = None
    for ref, scale, target in ((stiffness, 0.25, 0), (mass, 1.0, Y1)):
        for z in range(Z1):
            tall[z * X0 : (z + 1) * X0, :] = ref[0, 2 * z] + ref[0, 2 * z + 1]
        rows = tall[pl.ds(0, Z1 * X1, stride=2), :] + tall[pl.ds(1, Z1 * X1, stride=2), :]
        part = scale * fold_lanes(rows, 0, LANES, target)
        out = part if out is None else out + part
    for z in range(Z1):
        coarse[0, z] = out[z * X1 : (z + 1) * X1, :]
    pack_x(FIRST, (stiffness, forcing, mass, coarse), low, high)


def prepare_coarse(far, coarse, packed2, tall):
    for part, scale in ((0, 0.25), (1, 1.0)):
        packed2[part * 8 : part * 8 + 8, :] = scale * pack_coarse(
            lambda z: coarse[0, z], part * Y1, tall
        )


def pack_coarse(plane, first, tall):
    for z in range(Z1 // 2):
        tall[z * X1 : (z + 1) * X1, :] = plane(2 * z) + plane(2 * z + 1)
    count = Z1 // 2 * X1 // 2
    rows = tall[pl.ds(0, count, stride=2), :] + tall[pl.ds(1, count, stride=2), :]
    out = jnp.zeros((X1 // 2, LANES), F32)
    for z in range(Z1 // 2):
        part = rows[z * X1 // 2 : (z + 1) * X1 // 2, :]
        out = out + fold_lanes(part, first, Y1, z * Y1 // 2)
    return out


def parts(ref, planes, count=5):
    return [ref.at[k * planes : (k + 1) * planes] for k in range(count)]


def presmooth0(
    far, x_s, x_f, x_m, x_coarse, z_low, z_high, from_low, from_high,
    v_own, g_own, op, s1, m1, low, high,
    s, m, va, vb, tall,
):
    r, f, cx, cy, cz = parts(op, ZT0)
    inner = slice(1, ZT0 - 1)
    unpack_y(
        FIRST, planes_of(FIRST, (x_s, x_f, x_m, x_coarse), z_low, z_high), from_low, from_high,
        ([s], [f.at[inner]], [m.at[inner]], [s1, m1]),
    )
    couple(s, m, r, cx, cy, cz, 1, ZT0 - 1, 8, start=(f, va))
    far.flush(2)
    op = (r, f, cx, cy, cz)
    sweep(va, vb, op, 2, ZT0 - 2, 11)
    sweep(vb, va, op, 3, ZT0 - 3, 10)
    sweep(va, vb, op, 4, ZT0 - 4, 9)
    rows = []
    for z in range(Z1):
        plane = remain(vb, op, W0 + 2 * z) + remain(vb, op, W0 + 2 * z + 1)
        rows.append(plane[0:X1, 0:Y0] + plane[EVEN : EVEN + X1, 0:Y0])
    out = fold_lanes(jnp.concatenate(rows, axis=0), 0, LANES, 0)
    for z in range(Z1):
        g_own[0, z] = out[z * X1 : (z + 1) * X1, :]
    for z in range(Z0):
        v_own[0, z, every_other(0, X1), :] = vb[W0 + z, 0:X1, 0:Y0]
        v_own[0, z, every_other(1, X1), :] = vb[W0 + z, EVEN : EVEN + X1, 0:Y0]
    pack_x(SECOND, (g_own, v_own), low, high)


def presmooth1(
    far, g_x, v0_x, z_low, z_high, from_low, from_high, s, m,
    v_own, v0, copies, op, low, high,
    va, vb, tall,
):
    r, g, cx, cy, cz = parts(op, ZT1)
    for k in range(W1 - G1):
        g[k] = jnp.zeros((XT1, LANES), F32)
        g[ZT1 - 1 - k] = jnp.zeros((XT1, LANES), F32)
    inner = g.at[W1 - G1 : ZT1 - (W1 - G1)]
    unpack_y(SECOND, planes_of(SECOND, (g_x, v0_x), z_low, z_high), from_low, from_high, ([inner], [v0]))
    couple(s, m, r, cx, cy, cz, 1, ZT1 - 1, 10, start=(g, va))
    far.flush(3)
    op = (r, g, cx, cy, cz)
    sweep(va, vb, op, 4, ZT1 - 4, 10)
    sweep(vb, va, op, 5, ZT1 - 5, 10)
    sweep(va, vb, op, 6, ZT1 - 6, 10)
    packed = pack_coarse(lambda z: remain(vb, op, W1 + z)[0:X1, :], 0, tall)
    for d in range(copies.shape[0]):
        copies[d] = packed
    for z in range(Z1):
        v_own[z] = vb[W1 + z]
    lane = lane_of((XT0, LANES))
    base = (W0 + 1) * XT0
    for message, first0, first1 in ((low, 0, 0), (high, Z0 - W0, Z1 - W1)):
        rims = jnp.zeros((XT0, LANES), F32)
        for w in range(W0):
            message[w * XT0 : (w + 1) * XT0, :] = v0[first0 + w, :, 0:LANES]
            here = (lane >= 2 * W0 * w) & (lane < 2 * W0 * (w + 1))
            rims = jnp.where(here, roll(v0[first0 + w, :, LANES:], W0 + 2 * W0 * w, 1), rims)
        message[W0 * XT0 : base, :] = rims
        for w in range(W1):
            message[base + w * XT1 : base + (w + 1) * XT1, :] = v_own[first1 + w]


def unpack_whole(blocks, first, out):
    group = lane_of((8, LANES)) // 32

    def body(step):
        gz, gx = step // 4, step % 4
        for z in range(4):
            plane = None
            for gy in range(4):
                block = blocks[step * 4 + gy, first : first + 8, :]
                moved = roll(block, (gy - z) * 32, 1)
                plane = moved if plane is None else jnp.where(group == gy, moved, plane)
            out[gz * 4 + z, pl.ds(pl.multiple_of(gx * 8, 8), 8), :] = plane

    loop(0, 32, body, 4)


def fold_whole(plane, planes, rows, scale, tall, out):
    half = rows // 2
    for z in range(planes // 2):
        tall[z * rows : (z + 1) * rows, :] = plane(2 * z) + plane(2 * z + 1)
    count = planes // 2 * half
    folded = tall[pl.ds(0, count, stride=2), :] + tall[pl.ds(1, count, stride=2), :]
    folded = scale * fold_lanes(folded, 0, LANES, 0)
    for z in range(planes // 2):
        out[z] = folded[z * half : (z + 1) * half, :]


def spread_whole(v, planes, rows, tall, add):
    count = planes * rows
    flat = spread_lanes(jnp.concatenate([v[z] for z in range(planes)], axis=0))
    tall[pl.ds(0, count, stride=2), :] = flat
    tall[pl.ds(1, count, stride=2), :] = flat
    for z in range(planes):
        spread = tall[z * 2 * rows : (z + 1) * 2 * rows, :]
        add[2 * z] = add[2 * z] + spread
        add[2 * z + 1] = add[2 * z + 1] + spread


def coarsest(out, op):
    r, f, cx, cy, cz = op
    forced, upper, lower = [], [], []
    for z in range(8):
        scale = r[z]
        forced.append(scale * f[z])
        above = scale * cz[z]
        below = scale * cz[z - 1] if z else None
        upper.append((above, scale * cx[z], scale * cy[z]))
        lower.append((below, scale * roll(cx[z], 1, 0), scale * roll(cy[z], 1, 1)))

    def step(k, v):
        new = []
        for z in range(8):
            here = v[z]
            east = upper[z][2] * roll(here, -1, 1) + lower[z][2] * roll(here, 1, 1)
            north = upper[z][1] * roll(here, -1, 0) + lower[z][1] * roll(here, 1, 0)
            base = KEEP * here + forced[z]
            if z < 7:
                base = base + upper[z][0] * v[z + 1]
            if z:
                base = base + lower[z][0] * v[z - 1]
            new.append((base + north) + east)
        return tuple(new)

    v = lax.fori_loop(0, CSWEEPS - 1, step, tuple(forced), unroll=True)
    for z in range(8):
        out[z] = v[z]


def levels(stacked2, stacked34):
    level3 = [stacked34.at[16 * (k // 2) : 16 * (k // 2) + 16, 16 * (k % 2) : 16 * (k % 2) + 16, :] for k in range(4)]
    level4 = [stacked34.at[32:40, 8 * k : 8 * k + 8, :] for k in range(4)]
    return parts(stacked2, 32, 4), level3, level4


def coarse_operators(
    far, operators,
    stacked2, stacked34,
    s2, m2, s3, m3, s4, m4, tall,
):
    (r2, cx2, cy2, cz2), (r3, cx3, cy3, cz3), (r4, cx4, cy4, cz4) = levels(stacked2, stacked34)
    far.wait()
    unpack_whole(operators, 0, s2)
    unpack_whole(operators, 8, m2)
    couple(s2, m2, r2, cx2, cy2, cz2, 0, 32, 10, True)
    far.flush(0)
    fold_whole(lambda z: s2[z], 32, 32, 0.25, tall, s3)
    fold_whole(lambda z: m2[z], 32, 32, 1.0, tall, m3)
    couple(s3, m3, r3, cx3, cy3, cz3, 0, 16, 14, True)
    fold_whole(lambda z: s3[z], 16, 16, 0.25, tall, s4)
    fold_whole(lambda z: m3[z], 16, 16, 1.0, tall, m4)
    couple(s4, m4, r4, cx4, cy4, cz4, 0, 8, 6, True)


def coarse_cycle(
    far, forcing, stacked2, stacked34, out,
    f2, vb2, f3, va3, vb3, f4, vb4, tall, meanwhile,
):
    unpack_whole(forcing, 0, f2)
    far.wait(0, 3)
    far.start(1, 2)
    (r2, cx2, cy2, cz2), (r3, cx3, cy3, cz3), (r4, cx4, cy4, cz4) = levels(stacked2, stacked34)
    op2 = (r2, f2, cx2, cy2, cz2)
    op3 = (r3, f3, cx3, cy3, cz3)
    op4 = (r4, f4, cx4, cy4, cz4)
    va2 = out

    def four(va, vb, op, planes):
        sweep(va, vb, op, 0, planes, 30, True)
        sweep(vb, va, op, 0, planes, 30, True)

    def residue(v, op, planes):
        return lambda z: remain(v, op, z, z > 0, z < planes - 1)

    first_sweep(vb2, op2, 0, 32)
    sweep(vb2, va2, op2, 0, 32, 30, True)
    four(va2, vb2, op2, 32)
    fold_whole(residue(va2, op2, 32), 32, 32, 1.0, tall, f3)
    first_sweep(vb3, op3, 0, 16)
    sweep(vb3, va3, op3, 0, 16, 15, True)
    four(va3, vb3, op3, 16)
    fold_whole(residue(va3, op3, 16), 16, 16, 1.0, tall, f4)
    meanwhile()
    coarsest(vb4, op4)
    spread_whole(vb4, 8, 8, tall, va3)
    four(va3, vb3, op3, 16)
    four(va3, vb3, op3, 16)
    spread_whole(va3, 16, 16, tall, va2)
    four(va2, vb2, op2, 32)
    four(va2, vb2, op2, 32)


def finish(
    far, place, stacked2, stacked1, stacked0, stacked34, forcing, v1, v0_zx, from_low, from_high,
    potential, residual,
    va1, vb1, v0, vb0, correction, f2, vb2, f3, va3, vb3, f4, vb4, tall,
):
    def meanwhile():
        base = (W0 + 1) * XT0
        for message, first0, first1 in ((from_low, 0, 0), (from_high, W0 + Z0, W1 + Z1)):
            rims = message[W0 * XT0 : base, :]
            for w in range(W0):
                v0[first0 + w, :, 0:LANES] = message[w * XT0 : (w + 1) * XT0, :]
                v0[first0 + w, :, LANES:] = roll(rims, -W0 - 2 * W0 * w, 1)
            for w in range(W1):
                va1[first1 + w] = message[base + w * XT1 : base + (w + 1) * XT1, :]
        for z in range(Z0):
            v0[W0 + z] = v0_zx[z]
        for z in range(Z1):
            va1[W1 + z] = v1[z]

    coarse_cycle(far, forcing, stacked2, stacked34, correction, f2, vb2, f3, va3, vb3, f4, vb4, tall, meanwhile)
    gz, gx, gy = place[0], place[1], place[2]
    planes = []
    for k in range(12):
        plane = correction[(gz * 4 + 28 + k) % 32]
        plane = pltpu.roll(plane, (32 - gx * 8) % 32, 0)
        plane = pltpu.roll(plane, (LANES - gy * 32) % LANES, 1)
        planes += [plane[0:14], plane[26:32]]
    flat = jnp.concatenate(planes, axis=0)
    fine = lane_of(flat.shape)
    flat = pick(flat, fine // 2 + jnp.where(fine < 96, 0, 64))
    count = 12 * 20
    tall[pl.ds(0, count, stride=2), :] = flat
    tall[pl.ds(1, count, stride=2), :] = flat
    for z in range(ZT1):
        k = (z + 1) // 2
        va1[z] = va1[z] + tall[k * XT1 : (k + 1) * XT1, :]
    far.wait(1)
    op1 = parts(stacked1, ZT1)
    sweep(va1, vb1, op1, 1, ZT1 - 1, 20)
    sweep(vb1, va1, op1, 2, ZT1 - 2, 18)
    sweep(va1, vb1, op1, 3, ZT1 - 3, 16)
    sweep(vb1, va1, op1, 4, ZT1 - 4, 14)
    planes = []
    for k in range(14):
        planes += [va1[4 + k, 0:20, :], va1[4 + k, XT1 - 4 : XT1, :]]
    flat = jnp.concatenate(planes, axis=0)
    for half in range(2):
        part = spread_lanes(flat, 64 * half)
        at = slice(half * LANES, (half + 1) * LANES)
        for z in range(ZT0):
            k = (z + 1) // 2
            add = part[k * EVEN : (k + 1) * EVEN, :]
            v0[z, 0:EVEN, at] = v0[z, 0:EVEN, at] + add
            v0[z, EVEN:, at] = v0[z, EVEN:, at] + add
    far.wait(2)
    op0 = parts(stacked0, ZT0)
    sweep(v0, vb0, op0, 1, ZT0 - 1, 12)
    sweep(vb0, v0, op0, 2, ZT0 - 2, 11)
    sweep(v0, vb0, op0, 3, ZT0 - 3, 10)
    sweep(vb0, v0, op0, 4, ZT0 - 4, 9)
    for z in range(Z0):
        potential[z, every_other(0, X1), :] = v0[W0 + z, 0:X1, 0:Y0]
        potential[z, every_other(1, X1), :] = v0[W0 + z, EVEN : EVEN + X1, 0:Y0]
    far.flush(0)
    for z in range(Z0):
        plane = remain(v0, op0, W0 + z)
        residual[z, every_other(0, X1), :] = plane[0:X1, 0:Y0]
        residual[z, every_other(1, X1), :] = plane[EVEN : EVEN + X1, 0:Y0]


def shards(source, conductivity, cell_kind):
    own0, own1 = (1, Z0, X0, Y0), (1, Z1, X1, LANES)
    ext0, ext1 = (ZT0, XT0, 2 * LANES), (ZT1, XT1, LANES)
    everywhere = ("gz", "gx", "gy")
    devices = math.prod(lax.axis_size(axis) for axis in everywhere)
    place = jnp.stack([lax.axis_index(axis) for axis in everywhere]).astype(jnp.int32)
    wet = jnp.where(cell_kind > 0, 1.0, 0.0).astype(F32)
    surface = jnp.where(cell_kind == 2, 1.0, 0.0).astype(F32)
    stiffness = conductivity * wet
    mass = 0.005 * stiffness + 8.0 * stiffness * surface + 0.02 * (1.0 - wet)
    fields = [array.reshape(own0) for array in (stiffness, source * wet, mass)]
    coarse, low, high = call(
        prepare, [own1] + [x_message(FIRST)] * 2, [(Z1 * X0, LANES)], *fields
    )

    def gather_coarse(message):
        block, _ = lax.optimization_barrier((coarse, message))
        (packed2,) = call(prepare_coarse, [(16, LANES)], [(Z1 // 2 * X1, LANES)], block)
        return lax.all_gather(packed2, everywhere, axis=0)

    received, operators2 = exchange(FIRST, (*fields, coarse), low, high, gather_coarse)
    v0, g1, op0, s1, m1, low, high = call(
        presmooth0,
        [own0, own1, (5 * ZT0, XT0, 2 * LANES)] + [ext1] * 2 + [x_message(SECOND)] * 2,
        [ext0] * 4 + [(Z1 * X0, LANES)],
        *received, far_out=(2,),
    )
    received = exchange(SECOND, (g1, v0), low, high)
    stack0, stack1 = (5 * ZT0, XT0, 2 * LANES), (5 * ZT1, XT1, LANES)
    stack2, stack34 = (128, 32, LANES), (40, 32, LANES)
    message = ((W0 + 1) * XT0 + W1 * XT1, LANES)
    v1, v0, copies, op1, low, high = call(
        presmooth1,
        [(Z1, XT1, LANES), (Z0, XT0, 2 * LANES), (devices, 8, LANES), stack1] + [message] * 2,
        [ext1] * 2 + [(Z1 // 2 * X1, LANES)],
        *received, s1, m1, far_out=(3,),
    )
    _, operators2 = lax.optimization_barrier((copies, operators2))
    forcing2 = lax.all_to_all(copies, everywhere, 0, 0)
    from_low, from_high = shift(low, high, "gz")
    level2, level3, level4 = (32, 32, LANES), (16, 16, LANES), (8, 8, LANES)
    operators, operators34 = call(
        coarse_operators,
        [stack2, stack34],
        [level2] * 2 + [level3] * 2 + [level4] * 2 + [(512, LANES)],
        operators2, far_in={0: operators2.shape}, far_out=(0, 1),
    )
    return call(
        finish,
        [(Z0, X0, Y0)] * 2,
        [ext1, ext1, ext0, ext0] + [level2] * 3 + [level3] * 3 + [level4] * 2 + [(14 * XT0, LANES)],
        operators, op1, op0, operators34, forcing2, v1, v0, from_low, from_high,
        place=place, far_in={0: stack2, 1: stack1, 2: stack0, 3: stack34}, late=(1, 2),
        far_out=(0, 1), pad=False,
    )


def solution(mesh):
    spec = P("gz", "gx", "gy")
    return jax.shard_map(
        shards, mesh=mesh, in_specs=(spec,) * 3, out_specs=(spec,) * 2, check_vma=False
    )
```

```python
import math

import jax
import jax.numpy as jnp
from jax import lax
from jax.experimental import pallas as pl
from jax.experimental.pallas import tpu as pltpu
from jax.sharding import PartitionSpec as P

CSWEEPS = 32
DAMP = 0.8
KEEP = 1.0 - DAMP
W0 = 5
W1 = 7
G1 = 6
S1, F1 = 11, 10
Z0, X0, Y0 = 16, 32, 128
Z1, X1, Y1 = 8, 16, 64
ZT0, XT0, EVEN = Z0 + 2 * W0, 48, 24
ZT1, XT1 = Z1 + 2 * W1, 40
LANES = 128
MIB = 1024 * 1024
F32 = jnp.float32


def lane_of(shape):
    return lax.broadcasted_iota(jnp.int32, shape, len(shape) - 1)


def row_of(shape):
    return lax.broadcasted_iota(jnp.int32, shape, len(shape) - 2)


def roll(x, shift, axis):
    size = x.shape[axis]
    shift = shift % size
    return x if shift == 0 else pltpu.roll(x, shift, axis)


def loop(first, last, body, step):
    chunks = (last - first) // step

    def chunk(c, carry):
        for k in range(step):
            body(first + c * step + k)
        return carry

    if chunks > 1:
        lax.fori_loop(0, chunks, chunk, 0)
    elif chunks:
        chunk(0, 0)
    for z in range(first + chunks * step, last):
        body(z)


def pick(x, index):
    return jnp.take_along_axis(x, index, axis=1)


def fold_lanes(x, first, count, target):
    to = lane_of(x.shape) - target
    index = (first + 2 * to) % LANES
    pairs = pick(x, index) + pick(x, (index + 1) % LANES)
    return jnp.where((to >= 0) & (to < count // 2), pairs, 0.0)


def spread_lanes(x, first=0):
    return pick(x, first + lane_of(x.shape) // 2)


class Far:
    def __init__(self, ins, outs, late):
        self.ins = {k: pltpu.make_async_copy(*pair) for k, pair in ins.items()}
        self.outs = {k: pltpu.make_async_copy(*pair) for k, pair in outs.items()}
        self.started = []
        self.start(*[k for k in self.ins if k not in late])

    def start(self, *keys):
        for k in keys:
            self.ins[k].start()

    def wait(self, *keys):
        for k in keys or tuple(self.ins):
            self.ins.pop(k).wait()

    def flush(self, *keys):
        for k in keys:
            self.outs[k].start()
            self.started.append(k)

    def finish(self):
        self.flush(*[k for k in self.outs if k not in self.started])
        for copy in self.outs.values():
            copy.wait()


def padded(shape):
    plane = 4 * math.prod(shape[1:])
    return (max(shape[0], -(-7 * MIB // plane)), *shape[1:])


def call(body, outs, scratch, *args, place=None, far_in={}, far_out=(), late=(), grant=48, pad=True):
    shapes = [
        jax.ShapeDtypeStruct(padded(shape) if pad and k in far_out else shape, F32)
        for k, shape in enumerate(outs)
    ]
    vmem = pl.BlockSpec(memory_space=pltpu.VMEM)
    hbm = pl.BlockSpec(memory_space=pltpu.HBM)
    specs = [hbm if k in far_in else vmem for k in range(len(args))]
    out_specs = [hbm if k in far_out else vmem for k in range(len(outs))]
    held = [pltpu.VMEM(shape, F32) for shape in far_in.values()]
    held += [pltpu.VMEM(outs[k], F32) for k in far_out]
    extra = len(far_in) + len(far_out)
    if extra:
        held.append(pltpu.SemaphoreType.DMA((extra,)))
    placed = place is not None
    count = len(args)

    def wrapped(*refs):
        refs = list(refs)
        head = [refs.pop(0)] if placed else []
        ins, results = refs[:count], refs[count : count + len(outs)]
        rest = refs[count + len(outs) :]
        mine, rest = rest[: len(scratch)], rest[len(scratch) :]
        copies_in, copies_out = {}, {}
        for j, k in enumerate(far_in):
            copies_in[k] = (ins[k].at[0 : far_in[k][0]], rest[j], rest[extra].at[j])
            ins[k] = rest[j]
        for j, k in enumerate(far_out, len(far_in)):
            copies_out[k] = (rest[j], results[k].at[0 : outs[k][0]], rest[extra].at[j])
            results[k] = rest[j]
        far = Far(copies_in, copies_out, late)
        body(far, *head, *ins, *results, *mine)
        far.finish()

    if placed:
        specs = [pl.BlockSpec(memory_space=pltpu.SMEM)] + specs
        args = (place,) + args
    return pl.pallas_call(
        wrapped,
        out_shape=shapes,
        in_specs=specs,
        out_specs=out_specs,
        scratch_shapes=[pltpu.VMEM(shape, F32) for shape in scratch] + held,
        compiler_params=pltpu.CompilerParams(vmem_limit_bytes=grant * MIB),
    )(*args)


class Item:
    def __init__(self, fields, planes, rows, rows_out, width, kind, trim=False, width_z=None, edge=0):
        self.n, self.z, self.x, self.xt, self.w, self.kind = fields, planes, rows, rows_out, width, kind
        self.wz = width if width_z is None else width_z
        self.zt = planes + 2 * self.wz
        self.edge = edge
        self.trim = trim
        self.tall = rows + 8 if trim else rows_out
        self.virtual = 2 * fields if kind == "pair" else fields
        self.own = LANES if kind == "full" else LANES // 2
        self.slots = LANES // width
        self.groups = -(-self.virtual * (self.zt - 2 * edge) // self.slots)
        self.rows_x = fields * planes * width
        self.rows_z = fields * self.wz * self.tall
        self.rows_y = self.groups * self.tall

    def narrow(self, plane):
        if not self.trim:
            return plane
        even, odd = plane[16:24], plane[40:48]
        rim = jnp.where(reached(even), even, roll(odd, 4, 0))
        return jnp.concatenate([plane[0:16], plane[24:40], rim], axis=0)

    def widen(self, plane):
        if not self.trim:
            return plane
        rim = plane[32:40]
        even = jnp.where(reached(rim), rim, 0.0)
        odd = jnp.where(reached(rim), roll(rim, 4, 0), 0.0)
        return jnp.concatenate([plane[0:16], even, plane[16:32], odd], axis=0)


def reached(rim):
    return (row_of(rim.shape) < 2) | (row_of(rim.shape) >= 6)


def every_other(first, count):
    return pl.ds(first, count, stride=2)


def total(counts):
    count = sum(counts)
    return -(-count // 8) * 8


def pack_x(items, refs, low, high):
    at = 0
    for item, ref in zip(items, refs):
        for n in range(item.n):
            for z in range(item.z):
                low[at : at + item.w, :] = ref[n, z, 0 : item.w, :]
                high[at : at + item.w, :] = ref[n, z, item.x - item.w : item.x, :]
                at += item.w


def unpack_x(items, refs, from_low, from_high, outs):
    at = 0
    for item, ref, out in zip(items, refs, outs):
        w = item.w
        if item.kind == "full":
            for first in (16, 40):
                out[:, :, first : first + 8, :] = jnp.zeros((item.n, item.z, 8, LANES), F32)
        else:
            out[:, :, item.x :, :] = jnp.zeros((item.n, item.z, item.xt - item.x, LANES), F32)
        for n in range(item.n):
            for z in range(item.z):
                if item.kind == "full":
                    more, less = (w + 1) // 2, w // 2
                    out[n, z, 0:16, :] = ref[n, z, every_other(0, 16), :]
                    out[n, z, 24:40, :] = ref[n, z, every_other(1, 16), :]
                    out[n, z, 16 : 16 + more, :] = from_high[every_other(at, more), :]
                    out[n, z, 40 : 40 + less, :] = from_high[every_other(at + 1, less), :]
                    out[n, z, 24 - less : 24, :] = from_low[every_other(at + w % 2, less), :]
                    out[n, z, 48 - more : 48, :] = from_low[every_other(at + 1 - w % 2, more), :]
                else:
                    out[n, z, 0 : item.x, :] = ref[n, z]
                    out[n, z, item.x : item.x + w, :] = from_high[at : at + w, :]
                    out[n, z, item.xt - w :, :] = from_low[at : at + w, :]
                at += w


def pack_z(items, refs, low, high):
    at = 0
    for item, ref in zip(items, refs):
        for n in range(item.n):
            for w in range(item.wz):
                low[at : at + item.tall, :] = item.narrow(ref[n, w])
                high[at : at + item.tall, :] = item.narrow(ref[n, item.z - item.wz + w])
                at += item.tall


class Planes:
    def __init__(self, item, ref, from_low, from_high, base):
        self.item, self.ref, self.low, self.high, self.base = item, ref, from_low, from_high, base

    def received(self, n, z):
        item = self.item
        if item.wz <= z < item.wz + item.z:
            return None
        message, w = (self.low, z) if z < item.wz else (self.high, z - item.wz - item.z)
        at = self.base + (n * item.wz + w) * item.tall
        return message[at : at + item.tall, :]

    def whole(self, n, z):
        plane = self.received(n, z)
        return self.ref[n, z - self.item.wz] if plane is None else self.item.widen(plane)

    def narrow(self, n, z):
        plane = self.received(n, z)
        return self.item.narrow(self.ref[n, z - self.item.wz]) if plane is None else plane


def planes_of(items, refs, from_low, from_high):
    planes, base = [], 0
    for item, ref in zip(items, refs):
        planes.append(Planes(item, ref, from_low, from_high, base))
        base += item.rows_z
    return planes


def pack_y(items, sources, low, high):
    at = 0
    for item, source in zip(items, sources):
        lane = lane_of((item.tall, LANES))
        pairs = [(v, z) for v in range(item.virtual) for z in range(item.edge, item.zt - item.edge)]
        for g in range(item.groups):
            lows = jnp.zeros((item.tall, LANES), F32)
            highs = lows
            for k, (v, z) in enumerate(pairs[g * item.slots : (g + 1) * item.slots]):
                n, first = (v // 2, (v % 2) * item.own) if item.kind == "pair" else (v, 0)
                plane = source.narrow(n, z)
                place = k * item.w
                mask = (lane >= place) & (lane < place + item.w)
                lows = jnp.where(mask, roll(plane, place - first, 1), lows)
                highs = jnp.where(mask, roll(plane, place - first - item.own + item.w, 1), highs)
            low[at : at + item.tall, :] = lows
            high[at : at + item.tall, :] = highs
            at += item.tall


def unpack_y(items, sources, from_low, from_high, outs):
    at = 0
    for item, source, fields in zip(items, sources, outs):
        lane = lane_of((item.tall, LANES))
        for v in range(item.virtual if item.edge else 0):
            for z in [*range(item.edge), *range(item.zt - item.edge, item.zt)]:
                fields[v][z, :, 0:LANES] = source.whole(v, z)
                fields[v][z, :, LANES:] = jnp.zeros((item.xt, LANES), F32)
        pairs = [(v, z) for v in range(item.virtual) for z in range(item.edge, item.zt - item.edge)]
        for g in range(item.groups):
            lows = from_low[at : at + item.tall, :]
            highs = from_high[at : at + item.tall, :]
            at += item.tall
            for k, (v, z) in enumerate(pairs[g * item.slots : (g + 1) * item.slots]):
                place = k * item.w
                start = item.own % LANES
                upper = roll(highs, start - place, 1)
                lower = roll(lows, LANES - item.w - place, 1)
                rim = jnp.where(
                    lane < start + item.w, upper, jnp.where(lane >= LANES - item.w, lower, 0.0)
                )
                if item.kind == "full":
                    fields[v][z, :, 0:LANES] = source.whole(v, z)
                    fields[v][z, :, LANES:] = item.widen(rim)
                else:
                    plane = source.whole(v // 2 if item.kind == "pair" else v, z)
                    if item.kind == "pair" and v % 2:
                        plane = roll(plane, item.own, 1)
                    fields[v][z] = jnp.where(lane < item.own, plane, rim)


def shift(low, high, axis):
    count = lax.axis_size(axis)
    forward = [(i, i + 1) for i in range(count - 1)]
    backward = [(target, source) for source, target in forward]
    return lax.ppermute(high, axis, forward), lax.ppermute(low, axis, backward)


def exchange(items, arrays, low, high):
    count = len(items)
    from_low, from_high = shift(low, high, "gx")
    shapes = [(item.n, item.z, item.xt, LANES) for item in items]
    message = (total(item.rows_z for item in items), LANES)

    def after_x(far, *refs):
        ins, (a, b), outs, (c, d) = refs[:count], refs[count : count + 2], refs[count + 2 : 2 * count + 2], refs[2 * count + 2 :]
        unpack_x(items, ins, a, b, outs)
        pack_z(items, outs, c, d)

    *arrays, low, high = call(after_x, shapes + [message] * 2, [], *arrays, from_low, from_high)
    z_low, z_high = shift(low, high, "gz")
    message = (total(item.rows_y for item in items), LANES)

    def after_z(far, *refs):
        pack_y(items, planes_of(items, refs[:count], *refs[count : count + 2]), *refs[count + 2 :])

    low, high = call(after_z, [message] * 2, [], *arrays, z_low, z_high)
    return (*arrays, z_low, z_high, *shift(low, high, "gy"))


STIFFNESS = Item(1, Z0, X0, XT0, W0, "full", True, edge=1)
INNER = Item(1, Z0, X0, XT0, W0 - 1, "full", True)
COARSE = Item(1, Z1, X1, XT1, S1, "pair", False, W1)
FORCING1 = Item(1, Z1, X1, XT1, F1, "half", False, G1)
POTENTIAL0 = Item(1, Z0, X0, XT0, W0, "full", False, 0)
FIRST, SECOND = (STIFFNESS, INNER, INNER, COARSE), (FORCING1, POTENTIAL0)


def x_message(items):
    return (total(item.rows_x for item in items), LANES)


def x_above(plane):
    if plane.shape[0] != XT0:
        return roll(plane, -1, 0)
    return jnp.concatenate([plane[EVEN:], roll(plane[:EVEN], -1, 0)], axis=0)


def x_below(plane):
    if plane.shape[0] != XT0:
        return roll(plane, 1, 0)
    return jnp.concatenate([roll(plane[EVEN:], 1, 0), plane[:EVEN]], axis=0)


def couple(s, m, r, cx, cy, cz, first, last, step, edges=False, start=None):
    planes, rows, lanes = s.shape

    def vertical(z):
        return 4.0 * jnp.minimum(s[z], s[z + 1])

    def one(z, below, above):
        here = s[z]
        x_face = jnp.minimum(here, x_above(here))
        y_face = jnp.minimum(here, roll(here, -1, 1))
        if edges:
            x_face = jnp.where(row_of(here.shape) < rows - 1, x_face, 0.0)
            y_face = jnp.where(lane_of(here.shape) < lanes - 1, y_face, 0.0)
        cx[z] = x_face
        cy[z] = y_face
        cz[z] = above
        d = m[z] + below + above + x_face + x_below(x_face) + y_face + roll(y_face, 1, 1)
        scale = DAMP / jnp.where(d > 0.0, d, 1.0)
        r[z] = scale
        if start:
            start[1][z] = scale * start[0][z]

    if edges:
        zero = jnp.zeros((rows, lanes), F32)
        one(0, zero, vertical(0))
        one(planes - 1, vertical(planes - 2), zero)
    else:
        cz[first - 1] = vertical(first - 1)
    loop(first + edges, last - edges, lambda z: one(z, vertical(z - 1), vertical(z)), step)


def gathered(v, f, cx, cy, cz, z, low=True, high=True):
    here = v[z]
    x_face, y_face = cx[z], cy[z]
    out = f[z]
    if high:
        out = out + cz[z] * v[z + 1]
    if low:
        out = out + cz[z - 1] * v[z - 1]
    out = out + x_face * x_above(here) + x_below(x_face * here)
    return here, out + y_face * roll(here, -1, 1) + roll(y_face * here, 1, 1)


def sweep(v, into, op, first, last, unroll, edges=False):
    r, f, cx, cy, cz = op

    def step(z, low=True, high=True):
        here, out = gathered(v, f, cx, cy, cz, z, low, high)
        into[z] = KEEP * here + r[z] * out

    if edges:
        step(first, low=False)
        step(last - 1, high=False)
        loop(first + 1, last - 1, step, unroll)
    else:
        loop(first, last, step, unroll)


def remain(v, op, z, low=True, high=True):
    r, f, cx, cy, cz = op
    here, out = gathered(v, f, cx, cy, cz, z, low, high)
    return out - here * (DAMP / r[z])


def first_sweep(v, op, first, last):
    r, f = op[:2]

    def step(z):
        v[z] = r[z] * f[z]

    loop(first, last, step, 4)


def prepare(far, place, stiffness, forcing, mass, coarse, low, high, packed2, tall):
    out = None
    for ref, scale, target in ((stiffness, 0.25, 0), (mass, 1.0, Y1)):
        for z in range(Z1):
            tall[z * X0 : (z + 1) * X0, :] = ref[0, 2 * z] + ref[0, 2 * z + 1]
        rows = tall[pl.ds(0, Z1 * X1, stride=2), :] + tall[pl.ds(1, Z1 * X1, stride=2), :]
        part = scale * fold_lanes(rows, 0, LANES, target)
        out = part if out is None else out + part
    for z in range(Z1):
        coarse[0, z] = out[z * X1 : (z + 1) * X1, :]
    pack_x(FIRST, (stiffness, forcing, mass, coarse), low, high)
    for part, scale in ((0, 0.25), (1, 1.0)):
        packed2[part * 8 : part * 8 + 8, :] = scale * pack_coarse(
            place, lambda z: coarse[0, z], part * Y1, tall
        )


def pack_coarse(place, plane, first, tall):
    for z in range(Z1 // 2):
        tall[z * X1 : (z + 1) * X1, :] = plane(2 * z) + plane(2 * z + 1)
    count = Z1 // 2 * X1 // 2
    rows = tall[pl.ds(0, count, stride=2), :] + tall[pl.ds(1, count, stride=2), :]
    out = jnp.zeros((X1 // 2, LANES), F32)
    for z in range(Z1 // 2):
        part = rows[z * X1 // 2 : (z + 1) * X1 // 2, :]
        out = out + fold_lanes(part, first, Y1, z * Y1 // 2)
    return pltpu.roll(out, place[2] * 32, 1)


def parts(ref, planes, count=5):
    return [ref.at[k * planes : (k + 1) * planes] for k in range(count)]


def presmooth0(
    far, x_s, x_f, x_m, x_coarse, z_low, z_high, from_low, from_high,
    v_own, g_own, op, s1, m1, low, high,
    s, m, va, vb, tall,
):
    r, f, cx, cy, cz = parts(op, ZT0)
    inner = slice(1, ZT0 - 1)
    unpack_y(
        FIRST, planes_of(FIRST, (x_s, x_f, x_m, x_coarse), z_low, z_high), from_low, from_high,
        ([s], [f.at[inner]], [m.at[inner]], [s1, m1]),
    )
    couple(s, m, r, cx, cy, cz, 1, ZT0 - 1, 8, start=(f, va))
    far.flush(2)
    op = (r, f, cx, cy, cz)
    sweep(va, vb, op, 2, ZT0 - 2, 11)
    sweep(vb, va, op, 3, ZT0 - 3, 10)
    sweep(va, vb, op, 4, ZT0 - 4, 9)
    rows = []
    for z in range(Z1):
        plane = remain(vb, op, W0 + 2 * z) + remain(vb, op, W0 + 2 * z + 1)
        rows.append(plane[0:X1, 0:Y0] + plane[EVEN : EVEN + X1, 0:Y0])
    out = fold_lanes(jnp.concatenate(rows, axis=0), 0, LANES, 0)
    for z in range(Z1):
        g_own[0, z] = out[z * X1 : (z + 1) * X1, :]
    for z in range(Z0):
        v_own[0, z, every_other(0, X1), :] = vb[W0 + z, 0:X1, 0:Y0]
        v_own[0, z, every_other(1, X1), :] = vb[W0 + z, EVEN : EVEN + X1, 0:Y0]
    pack_x(SECOND, (g_own, v_own), low, high)


def presmooth1(
    far, place, g_x, v0_x, z_low, z_high, from_low, from_high, s, m,
    v_own, v0, copies, op, low, high,
    va, vb, tall,
):
    r, g, cx, cy, cz = parts(op, ZT1)
    for k in range(W1 - G1):
        g[k] = jnp.zeros((XT1, LANES), F32)
        g[ZT1 - 1 - k] = jnp.zeros((XT1, LANES), F32)
    inner = g.at[W1 - G1 : ZT1 - (W1 - G1)]
    unpack_y(SECOND, planes_of(SECOND, (g_x, v0_x), z_low, z_high), from_low, from_high, ([inner], [v0]))
    couple(s, m, r, cx, cy, cz, 1, ZT1 - 1, 10, start=(g, va))
    far.flush(3)
    op = (r, g, cx, cy, cz)
    sweep(va, vb, op, 4, ZT1 - 4, 10)
    sweep(vb, va, op, 5, ZT1 - 5, 10)
    sweep(va, vb, op, 6, ZT1 - 6, 10)
    packed = pack_coarse(place, lambda z: remain(vb, op, W1 + z)[0:X1, :], 0, tall)
    for d in range(copies.shape[0]):
        copies[d] = packed
    for z in range(Z1):
        v_own[z] = vb[W1 + z]
    lane = lane_of((XT0, LANES))
    base = (W0 + 1) * XT0
    for message, first0, first1 in ((low, 0, 0), (high, Z0 - W0, Z1 - W1)):
        rims = jnp.zeros((XT0, LANES), F32)
        for w in range(W0):
            message[w * XT0 : (w + 1) * XT0, :] = v0[first0 + w, :, 0:LANES]
            here = (lane >= 2 * W0 * w) & (lane < 2 * W0 * (w + 1))
            rims = jnp.where(here, roll(v0[first0 + w, :, LANES:], W0 + 2 * W0 * w, 1), rims)
        message[W0 * XT0 : base, :] = rims
        for w in range(W1):
            message[base + w * XT1 : base + (w + 1) * XT1, :] = v_own[first1 + w]


def unpack_whole(blocks, first, out):
    group = lane_of((8, LANES)) // 32

    def body(step):
        gz, gx = step // 4, step % 4
        tiles = [blocks[step * 4 + gy, first : first + 8, :] for gy in range(4)]
        for z in range(4):
            plane = tiles[0]
            for gy in range(1, 4):
                plane = jnp.where(group == (z + gy) % 4, tiles[gy], plane)
            out[gz * 4 + z, pl.ds(pl.multiple_of(gx * 8, 8), 8), :] = roll(plane, -32 * z, 1)

    loop(0, 32, body, 4)


def fold_whole(plane, planes, rows, scale, tall, out):
    half = rows // 2
    for z in range(planes // 2):
        tall[z * rows : (z + 1) * rows, :] = plane(2 * z) + plane(2 * z + 1)
    count = planes // 2 * half
    folded = tall[pl.ds(0, count, stride=2), :] + tall[pl.ds(1, count, stride=2), :]
    folded = scale * fold_lanes(folded, 0, LANES, 0)
    for z in range(planes // 2):
        out[z] = folded[z * half : (z + 1) * half, :]


def spread_whole(v, planes, rows, tall, add):
    count = planes * rows
    flat = spread_lanes(jnp.concatenate([v[z] for z in range(planes)], axis=0))
    tall[pl.ds(0, count, stride=2), :] = flat
    tall[pl.ds(1, count, stride=2), :] = flat
    for z in range(planes):
        spread = tall[z * 2 * rows : (z + 1) * 2 * rows, :]
        add[2 * z] = add[2 * z] + spread
        add[2 * z + 1] = add[2 * z + 1] + spread


def coarsest(out, op):
    r, f, cx, cy, cz = op
    forced, upper, lower = [], [], []
    for z in range(8):
        scale = r[z]
        forced.append(scale * f[z])
        above = scale * cz[z]
        below = scale * cz[z - 1] if z else None
        upper.append((above, scale * cx[z], scale * cy[z]))
        lower.append((below, scale * roll(cx[z], 1, 0), scale * roll(cy[z], 1, 1)))

    def step(k, v):
        new = []
        for z in range(8):
            here = v[z]
            east = upper[z][2] * roll(here, -1, 1) + lower[z][2] * roll(here, 1, 1)
            north = upper[z][1] * roll(here, -1, 0) + lower[z][1] * roll(here, 1, 0)
            base = KEEP * here + forced[z]
            if z < 7:
                base = base + upper[z][0] * v[z + 1]
            if z:
                base = base + lower[z][0] * v[z - 1]
            new.append((base + north) + east)
        return tuple(new)

    v = lax.fori_loop(0, CSWEEPS - 1, step, tuple(forced), unroll=True)
    for z in range(8):
        out[z] = v[z]


def levels(stacked2, stacked34):
    level3 = [stacked34.at[16 * (k // 2) : 16 * (k // 2) + 16, 16 * (k % 2) : 16 * (k % 2) + 16, :] for k in range(4)]
    level4 = [stacked34.at[32:40, 8 * k : 8 * k + 8, :] for k in range(4)]
    return parts(stacked2, 32, 4), level3, level4


def coarse_operators(
    far, operators,
    stacked2, stacked34,
    s2, m2, s3, m3, s4, m4, tall,
):
    (r2, cx2, cy2, cz2), (r3, cx3, cy3, cz3), (r4, cx4, cy4, cz4) = levels(stacked2, stacked34)
    far.wait()
    unpack_whole(operators, 0, s2)
    unpack_whole(operators, 8, m2)
    couple(s2, m2, r2, cx2, cy2, cz2, 0, 32, 10, True)
    far.flush(0)
    fold_whole(lambda z: s2[z], 32, 32, 0.25, tall, s3)
    fold_whole(lambda z: m2[z], 32, 32, 1.0, tall, m3)
    couple(s3, m3, r3, cx3, cy3, cz3, 0, 16, 14, True)
    fold_whole(lambda z: s3[z], 16, 16, 0.25, tall, s4)
    fold_whole(lambda z: m3[z], 16, 16, 1.0, tall, m4)
    couple(s4, m4, r4, cx4, cy4, cz4, 0, 8, 6, True)


def coarse_cycle(
    far, forcing, stacked2, stacked34, out,
    f2, vb2, f3, va3, vb3, f4, vb4, tall, meanwhile,
):
    unpack_whole(forcing, 0, f2)
    far.wait(0, 3)
    far.start(1, 2)
    (r2, cx2, cy2, cz2), (r3, cx3, cy3, cz3), (r4, cx4, cy4, cz4) = levels(stacked2, stacked34)
    op2 = (r2, f2, cx2, cy2, cz2)
    op3 = (r3, f3, cx3, cy3, cz3)
    op4 = (r4, f4, cx4, cy4, cz4)
    va2 = out

    def four(va, vb, op, planes):
        sweep(va, vb, op, 0, planes, 30, True)
        sweep(vb, va, op, 0, planes, 30, True)

    def residue(v, op, planes):
        return lambda z: remain(v, op, z, z > 0, z < planes - 1)

    first_sweep(vb2, op2, 0, 32)
    sweep(vb2, va2, op2, 0, 32, 30, True)
    four(va2, vb2, op2, 32)
    fold_whole(residue(va2, op2, 32), 32, 32, 1.0, tall, f3)
    first_sweep(vb3, op3, 0, 16)
    sweep(vb3, va3, op3, 0, 16, 15, True)
    four(va3, vb3, op3, 16)
    fold_whole(residue(va3, op3, 16), 16, 16, 1.0, tall, f4)
    meanwhile()
    coarsest(vb4, op4)
    spread_whole(vb4, 8, 8, tall, va3)
    four(va3, vb3, op3, 16)
    four(va3, vb3, op3, 16)
    spread_whole(va3, 16, 16, tall, va2)
    four(va2, vb2, op2, 32)
    four(va2, vb2, op2, 32)


def finish(
    far, place, stacked2, stacked1, stacked0, stacked34, forcing, v1, v0_zx, from_low, from_high,
    potential, residual,
    va1, vb1, v0, vb0, correction, f2, vb2, f3, va3, vb3, f4, vb4, tall,
):
    def meanwhile():
        base = (W0 + 1) * XT0
        for message, first0, first1 in ((from_low, 0, 0), (from_high, W0 + Z0, W1 + Z1)):
            rims = message[W0 * XT0 : base, :]
            for w in range(W0):
                v0[first0 + w, :, 0:LANES] = message[w * XT0 : (w + 1) * XT0, :]
                v0[first0 + w, :, LANES:] = roll(rims, -W0 - 2 * W0 * w, 1)
            for w in range(W1):
                va1[first1 + w] = message[base + w * XT1 : base + (w + 1) * XT1, :]
        for z in range(Z0):
            v0[W0 + z] = v0_zx[z]
        for z in range(Z1):
            va1[W1 + z] = v1[z]

    coarse_cycle(far, forcing, stacked2, stacked34, correction, f2, vb2, f3, va3, vb3, f4, vb4, tall, meanwhile)
    gz, gx, gy = place[0], place[1], place[2]
    planes = []
    for k in range(12):
        plane = correction[(gz * 4 + 28 + k) % 32]
        plane = pltpu.roll(plane, (32 - gx * 8) % 32, 0)
        plane = pltpu.roll(plane, (LANES - gy * 32) % LANES, 1)
        planes += [plane[0:14], plane[26:32]]
    flat = jnp.concatenate(planes, axis=0)
    fine = lane_of(flat.shape)
    flat = pick(flat, fine // 2 + jnp.where(fine < 96, 0, 64))
    count = 12 * 20
    tall[pl.ds(0, count, stride=2), :] = flat
    tall[pl.ds(1, count, stride=2), :] = flat
    for z in range(ZT1):
        k = (z + 1) // 2
        va1[z] = va1[z] + tall[k * XT1 : (k + 1) * XT1, :]
    far.wait(1)
    op1 = parts(stacked1, ZT1)
    sweep(va1, vb1, op1, 1, ZT1 - 1, 20)
    sweep(vb1, va1, op1, 2, ZT1 - 2, 18)
    sweep(va1, vb1, op1, 3, ZT1 - 3, 16)
    sweep(vb1, va1, op1, 4, ZT1 - 4, 14)
    planes = []
    for k in range(14):
        planes += [va1[4 + k, 0:20, :], va1[4 + k, XT1 - 4 : XT1, :]]
    flat = jnp.concatenate(planes, axis=0)
    for half in range(2):
        part = spread_lanes(flat, 64 * half)
        at = slice(half * LANES, (half + 1) * LANES)
        for z in range(ZT0):
            k = (z + 1) // 2
            add = part[k * EVEN : (k + 1) * EVEN, :]
            v0[z, 0:EVEN, at] = v0[z, 0:EVEN, at] + add
            v0[z, EVEN:, at] = v0[z, EVEN:, at] + add
    far.wait(2)
    op0 = parts(stacked0, ZT0)
    sweep(v0, vb0, op0, 1, ZT0 - 1, 12)
    sweep(vb0, v0, op0, 2, ZT0 - 2, 11)
    sweep(v0, vb0, op0, 3, ZT0 - 3, 10)
    sweep(vb0, v0, op0, 4, ZT0 - 4, 9)
    for z in range(Z0):
        potential[z, every_other(0, X1), :] = v0[W0 + z, 0:X1, 0:Y0]
        potential[z, every_other(1, X1), :] = v0[W0 + z, EVEN : EVEN + X1, 0:Y0]
    far.flush(0)
    for z in range(Z0):
        plane = remain(v0, op0, W0 + z)
        residual[z, every_other(0, X1), :] = plane[0:X1, 0:Y0]
        residual[z, every_other(1, X1), :] = plane[EVEN : EVEN + X1, 0:Y0]


def shards(source, conductivity, cell_kind):
    own0, own1 = (1, Z0, X0, Y0), (1, Z1, X1, LANES)
    ext0, ext1 = (ZT0, XT0, 2 * LANES), (ZT1, XT1, LANES)
    everywhere = ("gz", "gx", "gy")
    devices = math.prod(lax.axis_size(axis) for axis in everywhere)
    place = jnp.stack([lax.axis_index(axis) for axis in everywhere]).astype(jnp.int32)
    wet = jnp.where(cell_kind > 0, 1.0, 0.0).astype(F32)
    surface = jnp.where(cell_kind == 2, 1.0, 0.0).astype(F32)
    stiffness = conductivity * wet
    mass = 0.005 * stiffness + 8.0 * stiffness * surface + 0.02 * (1.0 - wet)
    fields = [array.reshape(own0) for array in (stiffness, source * wet, mass)]
    coarse, low, high, packed2 = call(
        prepare,
        [own1] + [x_message(FIRST)] * 2 + [(16, LANES)],
        [(Z1 * X0, LANES)],
        *fields, place=place,
    )
    operators2 = lax.all_gather(packed2, everywhere, axis=0)
    received = exchange(FIRST, (*fields, coarse), low, high)
    v0, g1, op0, s1, m1, low, high = call(
        presmooth0,
        [own0, own1, (5 * ZT0, XT0, 2 * LANES)] + [ext1] * 2 + [x_message(SECOND)] * 2,
        [ext0] * 4 + [(Z1 * X0, LANES)],
        *received, far_out=(2,),
    )
    received = exchange(SECOND, (g1, v0), low, high)
    stack0, stack1 = (5 * ZT0, XT0, 2 * LANES), (5 * ZT1, XT1, LANES)
    stack2, stack34 = (128, 32, LANES), (40, 32, LANES)
    message = ((W0 + 1) * XT0 + W1 * XT1, LANES)
    v1, v0, copies, op1, low, high = call(
        presmooth1,
        [(Z1, XT1, LANES), (Z0, XT0, 2 * LANES), (devices, 8, LANES), stack1] + [message] * 2,
        [ext1] * 2 + [(Z1 // 2 * X1, LANES)],
        *received, s1, m1, place=place, far_out=(3,),
    )
    _, operators2 = lax.optimization_barrier((copies, operators2))
    forcing2 = lax.all_to_all(copies, everywhere, 0, 0)
    from_low, from_high = shift(low, high, "gz")
    level2, level3, level4 = (32, 32, LANES), (16, 16, LANES), (8, 8, LANES)
    operators, operators34 = call(
        coarse_operators,
        [stack2, stack34],
        [level2] * 2 + [level3] * 2 + [level4] * 2 + [(512, LANES)],
        operators2, far_in={0: operators2.shape}, far_out=(0, 1),
    )
    return call(
        finish,
        [(Z0, X0, Y0)] * 2,
        [ext1, ext1, ext0, ext0] + [level2] * 3 + [level3] * 3 + [level4] * 2 + [(14 * XT0, LANES)],
        operators, op1, op0, operators34, forcing2, v1, v0, from_low, from_high,
        place=place, far_in={0: stack2, 1: stack1, 2: stack0, 3: stack34}, late=(1, 2),
        far_out=(0, 1), pad=False,
    )


def solution(mesh):
    spec = P("gz", "gx", "gy")
    return jax.shard_map(
        shards, mesh=mesh, in_specs=(spec,) * 3, out_specs=(spec,) * 2, check_vma=False
    )
```

```python
import math

import jax
import jax.numpy as jnp
from jax import lax
from jax.experimental import pallas as pl
from jax.experimental.pallas import tpu as pltpu
from jax.sharding import PartitionSpec as P

CSWEEPS = 32
DAMP = 0.8
KEEP = 1.0 - DAMP
W0 = 5
W1 = 7
G1 = 6
S1, F1 = 11, 10
Z0, X0, Y0 = 16, 32, 128
Z1, X1, Y1 = 8, 16, 64
ZT0, XT0, EVEN = Z0 + 2 * W0, 48, 24
ZT1, XT1 = Z1 + 2 * W1, 40
LANES = 128
MIB = 1024 * 1024
F32 = jnp.float32


def lane_of(shape):
    return lax.broadcasted_iota(jnp.int32, shape, len(shape) - 1)


def row_of(shape):
    return lax.broadcasted_iota(jnp.int32, shape, len(shape) - 2)


def roll(x, shift, axis):
    size = x.shape[axis]
    shift = shift % size
    return x if shift == 0 else pltpu.roll(x, shift, axis)


def loop(first, last, body, step):
    chunks = (last - first) // step

    def chunk(c, carry):
        for k in range(step):
            body(first + c * step + k)
        return carry

    if chunks > 1:
        lax.fori_loop(0, chunks, chunk, 0)
    elif chunks:
        chunk(0, 0)
    for z in range(first + chunks * step, last):
        body(z)


def pick(x, index):
    return jnp.take_along_axis(x, index, axis=1)


def fold_lanes(x, first, count, target):
    to = lane_of(x.shape) - target
    index = (first + 2 * to) % LANES
    pairs = pick(x, index) + pick(x, (index + 1) % LANES)
    return jnp.where((to >= 0) & (to < count // 2), pairs, 0.0)


def spread_lanes(x, first=0):
    return pick(x, first + lane_of(x.shape) // 2)


class Far:
    def __init__(self, ins, outs, late):
        self.ins = {k: pltpu.make_async_copy(*pair) for k, pair in ins.items()}
        self.outs = {k: pltpu.make_async_copy(*pair) for k, pair in outs.items()}
        self.started = []
        self.start(*[k for k in self.ins if k not in late])

    def start(self, *keys):
        for k in keys:
            self.ins[k].start()

    def wait(self, *keys):
        for k in keys or tuple(self.ins):
            self.ins.pop(k).wait()

    def flush(self, *keys):
        for k in keys:
            self.outs[k].start()
            self.started.append(k)

    def finish(self):
        self.flush(*[k for k in self.outs if k not in self.started])
        for copy in self.outs.values():
            copy.wait()


def padded(shape):
    plane = 4 * math.prod(shape[1:])
    return (max(shape[0], -(-7 * MIB // plane)), *shape[1:])


def call(body, outs, scratch, *args, far_in={}, far_out=(), late=(), grant=48, pad=True):
    shapes = [
        jax.ShapeDtypeStruct(padded(shape) if pad and k in far_out else shape, F32)
        for k, shape in enumerate(outs)
    ]
    vmem = pl.BlockSpec(memory_space=pltpu.VMEM)
    hbm = pl.BlockSpec(memory_space=pltpu.HBM)
    specs = [hbm if k in far_in else vmem for k in range(len(args))]
    out_specs = [hbm if k in far_out else vmem for k in range(len(outs))]
    held = [pltpu.VMEM(shape, F32) for shape in far_in.values()]
    held += [pltpu.VMEM(outs[k], F32) for k in far_out]
    extra = len(far_in) + len(far_out)
    if extra:
        held.append(pltpu.SemaphoreType.DMA((extra,)))
    count = len(args)

    def wrapped(*refs):
        refs = list(refs)
        ins, results = refs[:count], refs[count : count + len(outs)]
        rest = refs[count + len(outs) :]
        mine, rest = rest[: len(scratch)], rest[len(scratch) :]
        copies_in, copies_out = {}, {}
        for j, k in enumerate(far_in):
            copies_in[k] = (ins[k].at[0 : far_in[k][0]], rest[j], rest[extra].at[j])
            ins[k] = rest[j]
        for j, k in enumerate(far_out, len(far_in)):
            copies_out[k] = (rest[j], results[k].at[0 : outs[k][0]], rest[extra].at[j])
            results[k] = rest[j]
        far = Far(copies_in, copies_out, late)
        body(far, *ins, *results, *mine)
        far.finish()

    return pl.pallas_call(
        wrapped,
        out_shape=shapes,
        in_specs=specs,
        out_specs=out_specs,
        scratch_shapes=[pltpu.VMEM(shape, F32) for shape in scratch] + held,
        compiler_params=pltpu.CompilerParams(vmem_limit_bytes=grant * MIB),
    )(*args)


class Item:
    def __init__(self, fields, planes, rows, rows_out, width, kind, trim=False, width_z=None, edge=0):
        self.n, self.z, self.x, self.xt, self.w, self.kind = fields, planes, rows, rows_out, width, kind
        self.wz = width if width_z is None else width_z
        self.zt = planes + 2 * self.wz
        self.edge = edge
        self.trim = trim
        self.tall = rows + 8 if trim else rows_out
        self.virtual = 2 * fields if kind == "pair" else fields
        self.own = LANES if kind == "full" else LANES // 2
        self.slots = LANES // width
        self.groups = -(-self.virtual * (self.zt - 2 * edge) // self.slots)
        self.rows_x = fields * planes * width
        self.rows_z = fields * self.wz * self.tall
        self.rows_y = self.groups * self.tall

    def narrow(self, plane):
        if not self.trim:
            return plane
        even, odd = plane[16:24], plane[40:48]
        rim = jnp.where(reached(even), even, roll(odd, 4, 0))
        return jnp.concatenate([plane[0:16], plane[24:40], rim], axis=0)

    def widen(self, plane):
        if not self.trim:
            return plane
        rim = plane[32:40]
        even = jnp.where(reached(rim), rim, 0.0)
        odd = jnp.where(reached(rim), roll(rim, 4, 0), 0.0)
        return jnp.concatenate([plane[0:16], even, plane[16:32], odd], axis=0)


def reached(rim):
    return (row_of(rim.shape) < 2) | (row_of(rim.shape) >= 6)


def every_other(first, count):
    return pl.ds(first, count, stride=2)


def total(counts):
    count = sum(counts)
    return -(-count // 8) * 8


def pack_x(items, refs, low, high):
    at = 0
    for item, ref in zip(items, refs):
        for n in range(item.n):
            for z in range(item.z):
                low[at : at + item.w, :] = ref[n, z, 0 : item.w, :]
                high[at : at + item.w, :] = ref[n, z, item.x - item.w : item.x, :]
                at += item.w


def unpack_x(items, refs, from_low, from_high, outs):
    at = 0
    for item, ref, out in zip(items, refs, outs):
        w = item.w
        if item.kind == "full":
            for first in (16, 40):
                out[:, :, first : first + 8, :] = jnp.zeros((item.n, item.z, 8, LANES), F32)
        else:
            out[:, :, item.x :, :] = jnp.zeros((item.n, item.z, item.xt - item.x, LANES), F32)
        for n in range(item.n):
            for z in range(item.z):
                if item.kind == "full":
                    more, less = (w + 1) // 2, w // 2
                    out[n, z, 0:16, :] = ref[n, z, every_other(0, 16), :]
                    out[n, z, 24:40, :] = ref[n, z, every_other(1, 16), :]
                    out[n, z, 16 : 16 + more, :] = from_high[every_other(at, more), :]
                    out[n, z, 40 : 40 + less, :] = from_high[every_other(at + 1, less), :]
                    out[n, z, 24 - less : 24, :] = from_low[every_other(at + w % 2, less), :]
                    out[n, z, 48 - more : 48, :] = from_low[every_other(at + 1 - w % 2, more), :]
                else:
                    out[n, z, 0 : item.x, :] = ref[n, z]
                    out[n, z, item.x : item.x + w, :] = from_high[at : at + w, :]
                    out[n, z, item.xt - w :, :] = from_low[at : at + w, :]
                at += w


def pack_z(items, refs, low, high):
    at = 0
    for item, ref in zip(items, refs):
        for n in range(item.n):
            for w in range(item.wz):
                low[at : at + item.tall, :] = item.narrow(ref[n, w])
                high[at : at + item.tall, :] = item.narrow(ref[n, item.z - item.wz + w])
                at += item.tall


class Planes:
    def __init__(self, item, ref, from_low, from_high, base):
        self.item, self.ref, self.low, self.high, self.base = item, ref, from_low, from_high, base

    def received(self, n, z):
        item = self.item
        if item.wz <= z < item.wz + item.z:
            return None
        message, w = (self.low, z) if z < item.wz else (self.high, z - item.wz - item.z)
        at = self.base + (n * item.wz + w) * item.tall
        return message[at : at + item.tall, :]

    def whole(self, n, z):
        plane = self.received(n, z)
        return self.ref[n, z - self.item.wz] if plane is None else self.item.widen(plane)

    def narrow(self, n, z):
        plane = self.received(n, z)
        return self.item.narrow(self.ref[n, z - self.item.wz]) if plane is None else plane


def planes_of(items, refs, from_low, from_high):
    planes, base = [], 0
    for item, ref in zip(items, refs):
        planes.append(Planes(item, ref, from_low, from_high, base))
        base += item.rows_z
    return planes


def pack_y(items, sources, low, high):
    at = 0
    for item, source in zip(items, sources):
        lane = lane_of((item.tall, LANES))
        pairs = [(v, z) for v in range(item.virtual) for z in range(item.edge, item.zt - item.edge)]
        for g in range(item.groups):
            lows = jnp.zeros((item.tall, LANES), F32)
            highs = lows
            for k, (v, z) in enumerate(pairs[g * item.slots : (g + 1) * item.slots]):
                n, first = (v // 2, (v % 2) * item.own) if item.kind == "pair" else (v, 0)
                plane = source.narrow(n, z)
                place = k * item.w
                mask = (lane >= place) & (lane < place + item.w)
                lows = jnp.where(mask, roll(plane, place - first, 1), lows)
                highs = jnp.where(mask, roll(plane, place - first - item.own + item.w, 1), highs)
            low[at : at + item.tall, :] = lows
            high[at : at + item.tall, :] = highs
            at += item.tall


def unpack_y(items, sources, from_low, from_high, outs):
    at = 0
    for item, source, fields in zip(items, sources, outs):
        lane = lane_of((item.tall, LANES))
        for v in range(item.virtual if item.edge else 0):
            for z in [*range(item.edge), *range(item.zt - item.edge, item.zt)]:
                fields[v][z, :, 0:LANES] = source.whole(v, z)
                fields[v][z, :, LANES:] = jnp.zeros((item.xt, LANES), F32)
        pairs = [(v, z) for v in range(item.virtual) for z in range(item.edge, item.zt - item.edge)]
        for g in range(item.groups):
            lows = from_low[at : at + item.tall, :]
            highs = from_high[at : at + item.tall, :]
            at += item.tall
            for k, (v, z) in enumerate(pairs[g * item.slots : (g + 1) * item.slots]):
                place = k * item.w
                start = item.own % LANES
                upper = roll(highs, start - place, 1)
                lower = roll(lows, LANES - item.w - place, 1)
                rim = jnp.where(
                    lane < start + item.w, upper, jnp.where(lane >= LANES - item.w, lower, 0.0)
                )
                if item.kind == "full":
                    fields[v][z, :, 0:LANES] = source.whole(v, z)
                    fields[v][z, :, LANES:] = item.widen(rim)
                else:
                    plane = source.whole(v // 2 if item.kind == "pair" else v, z)
                    if item.kind == "pair" and v % 2:
                        plane = roll(plane, item.own, 1)
                    fields[v][z] = jnp.where(lane < item.own, plane, rim)


def shift(low, high, axis):
    count = lax.axis_size(axis)
    forward = [(i, i + 1) for i in range(count - 1)]
    backward = [(target, source) for source, target in forward]
    return lax.ppermute(high, axis, forward), lax.ppermute(low, axis, backward)


def exchange(items, arrays, low, high, beside=None):
    count = len(items)
    from_low, from_high = shift(low, high, "gx")
    shapes = [(item.n, item.z, item.xt, LANES) for item in items]
    message = (total(item.rows_z for item in items), LANES)

    def after_x(far, *refs):
        ins, (a, b), outs, (c, d) = refs[:count], refs[count : count + 2], refs[count + 2 : 2 * count + 2], refs[2 * count + 2 :]
        unpack_x(items, ins, a, b, outs)
        pack_z(items, outs, c, d)

    *arrays, low, high = call(after_x, shapes + [message] * 2, [], *arrays, from_low, from_high)
    extra = beside(low) if beside else None
    z_low, z_high = shift(low, high, "gz")
    message = (total(item.rows_y for item in items), LANES)

    def after_z(far, *refs):
        pack_y(items, planes_of(items, refs[:count], *refs[count : count + 2]), *refs[count + 2 :])

    low, high = call(after_z, [message] * 2, [], *arrays, z_low, z_high)
    received = (*arrays, z_low, z_high, *shift(low, high, "gy"))
    return (received, extra) if beside else received


STIFFNESS = Item(1, Z0, X0, XT0, W0, "full", True, edge=1)
INNER = Item(1, Z0, X0, XT0, W0 - 1, "full", True)
COARSE = Item(1, Z1, X1, XT1, S1, "pair", False, W1)
FORCING1 = Item(1, Z1, X1, XT1, F1, "half", False, G1)
POTENTIAL0 = Item(1, Z0, X0, XT0, W0, "full", False, 0)
FIRST, SECOND = (STIFFNESS, INNER, INNER, COARSE), (FORCING1, POTENTIAL0)


def x_message(items):
    return (total(item.rows_x for item in items), LANES)


def x_above(plane):
    if plane.shape[0] != XT0:
        return roll(plane, -1, 0)
    return jnp.concatenate([plane[EVEN:], roll(plane[:EVEN], -1, 0)], axis=0)


def x_below(plane):
    if plane.shape[0] != XT0:
        return roll(plane, 1, 0)
    return jnp.concatenate([roll(plane[EVEN:], 1, 0), plane[:EVEN]], axis=0)


def couple(s, m, r, cx, cy, cz, first, last, step, edges=False, start=None):
    planes, rows, lanes = s.shape

    def vertical(z):
        return 4.0 * jnp.minimum(s[z], s[z + 1])

    def one(z, below, above):
        here = s[z]
        x_face = jnp.minimum(here, x_above(here))
        y_face = jnp.minimum(here, roll(here, -1, 1))
        if edges:
            x_face = jnp.where(row_of(here.shape) < rows - 1, x_face, 0.0)
            y_face = jnp.where(lane_of(here.shape) < lanes - 1, y_face, 0.0)
        cx[z] = x_face
        cy[z] = y_face
        cz[z] = above
        d = m[z] + below + above + x_face + x_below(x_face) + y_face + roll(y_face, 1, 1)
        scale = DAMP / jnp.where(d > 0.0, d, 1.0)
        r[z] = scale
        if start:
            start[1][z] = scale * start[0][z]

    if edges:
        zero = jnp.zeros((rows, lanes), F32)
        one(0, zero, vertical(0))
        one(planes - 1, vertical(planes - 2), zero)
    else:
        cz[first - 1] = vertical(first - 1)
    loop(first + edges, last - edges, lambda z: one(z, vertical(z - 1), vertical(z)), step)


def gathered(v, f, cx, cy, cz, z, low=True, high=True):
    here = v[z]
    x_face, y_face = cx[z], cy[z]
    out = f[z]
    if high:
        out = out + cz[z] * v[z + 1]
    if low:
        out = out + cz[z - 1] * v[z - 1]
    out = out + x_face * x_above(here) + x_below(x_face * here)
    return here, out + y_face * roll(here, -1, 1) + roll(y_face * here, 1, 1)


def sweep(v, into, op, first, last, unroll, edges=False):
    r, f, cx, cy, cz = op

    def step(z, low=True, high=True):
        here, out = gathered(v, f, cx, cy, cz, z, low, high)
        into[z] = KEEP * here + r[z] * out

    if edges:
        step(first, low=False)
        step(last - 1, high=False)
        loop(first + 1, last - 1, step, unroll)
    else:
        loop(first, last, step, unroll)


def remain(v, op, z, low=True, high=True):
    r, f, cx, cy, cz = op
    here, out = gathered(v, f, cx, cy, cz, z, low, high)
    return out - here * (DAMP / r[z])


def first_sweep(v, op, first, last):
    r, f = op[:2]

    def step(z):
        v[z] = r[z] * f[z]

    loop(first, last, step, 4)


def prepare(far, stiffness, forcing, mass, coarse, low, high, tall):
    out = None
    for ref, scale, target in ((stiffness, 0.25, 0), (mass, 1.0, Y1)):
        for z in range(Z1):
            tall[z * X0 : (z + 1) * X0, :] = ref[0, 2 * z] + ref[0, 2 * z + 1]
        rows = tall[pl.ds(0, Z1 * X1, stride=2), :] + tall[pl.ds(1, Z1 * X1, stride=2), :]
        part = scale * fold_lanes(rows, 0, LANES, target)
        out = part if out is None else out + part
    for z in range(Z1):
        coarse[0, z] = out[z * X1 : (z + 1) * X1, :]
    pack_x(FIRST, (stiffness, forcing, mass, coarse), low, high)


def prepare_coarse(far, coarse, packed2, tall):
    for part, scale in ((0, 0.25), (1, 1.0)):
        packed2[part * 8 : part * 8 + 8, :] = scale * pack_coarse(
            lambda z: coarse[0, z], part * Y1, tall
        )


def pack_coarse(plane, first, tall):
    for z in range(Z1 // 2):
        tall[z * X1 : (z + 1) * X1, :] = plane(2 * z) + plane(2 * z + 1)
    count = Z1 // 2 * X1 // 2
    rows = tall[pl.ds(0, count, stride=2), :] + tall[pl.ds(1, count, stride=2), :]
    out = jnp.zeros((X1 // 2, LANES), F32)
    for z in range(Z1 // 2):
        part = rows[z * X1 // 2 : (z + 1) * X1 // 2, :]
        out = out + fold_lanes(part, first, Y1, z * Y1 // 2)
    return pltpu.roll(out, lax.axis_index("gy") * 32, 1)


def parts(ref, planes, count=5):
    return [ref.at[k * planes : (k + 1) * planes] for k in range(count)]


def presmooth0(
    far, x_s, x_f, x_m, x_coarse, z_low, z_high, from_low, from_high,
    v_own, g_own, op, s1, m1, low, high,
    s, m, va, vb, tall,
):
    r, f, cx, cy, cz = parts(op, ZT0)
    inner = slice(1, ZT0 - 1)
    unpack_y(
        FIRST, planes_of(FIRST, (x_s, x_f, x_m, x_coarse), z_low, z_high), from_low, from_high,
        ([s], [f.at[inner]], [m.at[inner]], [s1, m1]),
    )
    couple(s, m, r, cx, cy, cz, 1, ZT0 - 1, 8, start=(f, va))
    far.flush(2)
    op = (r, f, cx, cy, cz)
    sweep(va, vb, op, 2, ZT0 - 2, 11)
    sweep(vb, va, op, 3, ZT0 - 3, 10)
    sweep(va, vb, op, 4, ZT0 - 4, 9)
    rows = []
    for z in range(Z1):
        plane = remain(vb, op, W0 + 2 * z) + remain(vb, op, W0 + 2 * z + 1)
        rows.append(plane[0:X1, 0:Y0] + plane[EVEN : EVEN + X1, 0:Y0])
    out = fold_lanes(jnp.concatenate(rows, axis=0), 0, LANES, 0)
    for z in range(Z1):
        g_own[0, z] = out[z * X1 : (z + 1) * X1, :]
    for z in range(Z0):
        v_own[0, z, every_other(0, X1), :] = vb[W0 + z, 0:X1, 0:Y0]
        v_own[0, z, every_other(1, X1), :] = vb[W0 + z, EVEN : EVEN + X1, 0:Y0]
    pack_x(SECOND, (g_own, v_own), low, high)


def presmooth1(
    far, g_x, v0_x, z_low, z_high, from_low, from_high, s, m,
    v_own, v0, copies, op, low, high,
    va, vb, tall,
):
    r, g, cx, cy, cz = parts(op, ZT1)
    for k in range(W1 - G1):
        g[k] = jnp.zeros((XT1, LANES), F32)
        g[ZT1 - 1 - k] = jnp.zeros((XT1, LANES), F32)
    inner = g.at[W1 - G1 : ZT1 - (W1 - G1)]
    unpack_y(SECOND, planes_of(SECOND, (g_x, v0_x), z_low, z_high), from_low, from_high, ([inner], [v0]))
    couple(s, m, r, cx, cy, cz, 1, ZT1 - 1, 10, start=(g, va))
    far.flush(3)
    op = (r, g, cx, cy, cz)
    sweep(va, vb, op, 4, ZT1 - 4, 10)
    sweep(vb, va, op, 5, ZT1 - 5, 10)
    sweep(va, vb, op, 6, ZT1 - 6, 10)
    packed = pack_coarse(lambda z: remain(vb, op, W1 + z)[0:X1, :], 0, tall)
    for d in range(copies.shape[0]):
        copies[d] = packed
    for z in range(Z1):
        v_own[z] = vb[W1 + z]
    lane = lane_of((XT0, LANES))
    base = (W0 + 1) * XT0
    for message, first0, first1 in ((low, 0, 0), (high, Z0 - W0, Z1 - W1)):
        rims = jnp.zeros((XT0, LANES), F32)
        for w in range(W0):
            message[w * XT0 : (w + 1) * XT0, :] = v0[first0 + w, :, 0:LANES]
            here = (lane >= 2 * W0 * w) & (lane < 2 * W0 * (w + 1))
            rims = jnp.where(here, roll(v0[first0 + w, :, LANES:], W0 + 2 * W0 * w, 1), rims)
        message[W0 * XT0 : base, :] = rims
        for w in range(W1):
            message[base + w * XT1 : base + (w + 1) * XT1, :] = v_own[first1 + w]


def unpack_whole(blocks, first, out):
    group = lane_of((8, LANES)) // 32

    def body(step):
        gz, gx = step // 4, step % 4
        tiles = [blocks[step * 4 + gy, first : first + 8, :] for gy in range(4)]
        for z in range(4):
            plane = tiles[0]
            for gy in range(1, 4):
                plane = jnp.where(group == (z + gy) % 4, tiles[gy], plane)
            out[gz * 4 + z, pl.ds(pl.multiple_of(gx * 8, 8), 8), :] = roll(plane, -32 * z, 1)

    loop(0, 32, body, 4)


def fold_whole(plane, planes, rows, scale, tall, out):
    half = rows // 2
    for z in range(planes // 2):
        tall[z * rows : (z + 1) * rows, :] = plane(2 * z) + plane(2 * z + 1)
    count = planes // 2 * half
    folded = tall[pl.ds(0, count, stride=2), :] + tall[pl.ds(1, count, stride=2), :]
    folded = scale * fold_lanes(folded, 0, LANES, 0)
    for z in range(planes // 2):
        out[z] = folded[z * half : (z + 1) * half, :]


def spread_whole(v, planes, rows, tall, add):
    count = planes * rows
    flat = spread_lanes(jnp.concatenate([v[z] for z in range(planes)], axis=0))
    tall[pl.ds(0, count, stride=2), :] = flat
    tall[pl.ds(1, count, stride=2), :] = flat
    for z in range(planes):
        spread = tall[z * 2 * rows : (z + 1) * 2 * rows, :]
        add[2 * z] = add[2 * z] + spread
        add[2 * z + 1] = add[2 * z + 1] + spread


def coarsest(out, op):
    r, f, cx, cy, cz = op
    forced, upper, lower = [], [], []
    for z in range(8):
        scale = r[z]
        forced.append(scale * f[z])
        above = scale * cz[z]
        below = scale * cz[z - 1] if z else None
        upper.append((above, scale * cx[z], scale * cy[z]))
        lower.append((below, scale * roll(cx[z], 1, 0), scale * roll(cy[z], 1, 1)))

    def step(k, v):
        new = []
        for z in range(8):
            here = v[z]
            east = upper[z][2] * roll(here, -1, 1) + lower[z][2] * roll(here, 1, 1)
            north = upper[z][1] * roll(here, -1, 0) + lower[z][1] * roll(here, 1, 0)
            base = KEEP * here + forced[z]
            if z < 7:
                base = base + upper[z][0] * v[z + 1]
            if z:
                base = base + lower[z][0] * v[z - 1]
            new.append((base + north) + east)
        return tuple(new)

    v = lax.fori_loop(0, CSWEEPS - 1, step, tuple(forced), unroll=True)
    for z in range(8):
        out[z] = v[z]


def levels(stacked2, stacked34):
    level3 = [stacked34.at[16 * (k // 2) : 16 * (k // 2) + 16, 16 * (k % 2) : 16 * (k % 2) + 16, :] for k in range(4)]
    level4 = [stacked34.at[32:40, 8 * k : 8 * k + 8, :] for k in range(4)]
    return parts(stacked2, 32, 4), level3, level4


def coarse_operators(
    far, operators,
    stacked2, stacked34,
    s2, m2, s3, m3, s4, m4, tall,
):
    (r2, cx2, cy2, cz2), (r3, cx3, cy3, cz3), (r4, cx4, cy4, cz4) = levels(stacked2, stacked34)
    far.wait()
    unpack_whole(operators, 0, s2)
    unpack_whole(operators, 8, m2)
    couple(s2, m2, r2, cx2, cy2, cz2, 0, 32, 10, True)
    far.flush(0)
    fold_whole(lambda z: s2[z], 32, 32, 0.25, tall, s3)
    fold_whole(lambda z: m2[z], 32, 32, 1.0, tall, m3)
    couple(s3, m3, r3, cx3, cy3, cz3, 0, 16, 14, True)
    fold_whole(lambda z: s3[z], 16, 16, 0.25, tall, s4)
    fold_whole(lambda z: m3[z], 16, 16, 1.0, tall, m4)
    couple(s4, m4, r4, cx4, cy4, cz4, 0, 8, 6, True)


def coarse_cycle(
    far, forcing, stacked2, stacked34, out,
    f2, vb2, f3, va3, vb3, f4, vb4, tall, meanwhile,
):
    unpack_whole(forcing, 0, f2)
    far.wait(0, 3)
    far.start(1, 2)
    (r2, cx2, cy2, cz2), (r3, cx3, cy3, cz3), (r4, cx4, cy4, cz4) = levels(stacked2, stacked34)
    op2 = (r2, f2, cx2, cy2, cz2)
    op3 = (r3, f3, cx3, cy3, cz3)
    op4 = (r4, f4, cx4, cy4, cz4)
    va2 = out

    def four(va, vb, op, planes):
        sweep(va, vb, op, 0, planes, 30, True)
        sweep(vb, va, op, 0, planes, 30, True)

    def residue(v, op, planes):
        return lambda z: remain(v, op, z, z > 0, z < planes - 1)

    first_sweep(vb2, op2, 0, 32)
    sweep(vb2, va2, op2, 0, 32, 30, True)
    four(va2, vb2, op2, 32)
    fold_whole(residue(va2, op2, 32), 32, 32, 1.0, tall, f3)
    first_sweep(vb3, op3, 0, 16)
    sweep(vb3, va3, op3, 0, 16, 15, True)
    four(va3, vb3, op3, 16)
    fold_whole(residue(va3, op3, 16), 16, 16, 1.0, tall, f4)
    meanwhile()
    coarsest(vb4, op4)
    spread_whole(vb4, 8, 8, tall, va3)
    four(va3, vb3, op3, 16)
    four(va3, vb3, op3, 16)
    spread_whole(va3, 16, 16, tall, va2)
    four(va2, vb2, op2, 32)
    four(va2, vb2, op2, 32)


def finish(
    far, stacked2, stacked1, stacked0, stacked34, forcing, v1, v0_zx, from_low, from_high,
    potential, residual,
    va1, vb1, v0, vb0, correction, f2, vb2, f3, va3, vb3, f4, vb4, tall,
):
    def meanwhile():
        base = (W0 + 1) * XT0
        for message, first0, first1 in ((from_low, 0, 0), (from_high, W0 + Z0, W1 + Z1)):
            rims = message[W0 * XT0 : base, :]
            for w in range(W0):
                v0[first0 + w, :, 0:LANES] = message[w * XT0 : (w + 1) * XT0, :]
                v0[first0 + w, :, LANES:] = roll(rims, -W0 - 2 * W0 * w, 1)
            for w in range(W1):
                va1[first1 + w] = message[base + w * XT1 : base + (w + 1) * XT1, :]
        for z in range(Z0):
            v0[W0 + z] = v0_zx[z]
        for z in range(Z1):
            va1[W1 + z] = v1[z]

    coarse_cycle(far, forcing, stacked2, stacked34, correction, f2, vb2, f3, va3, vb3, f4, vb4, tall, meanwhile)
    gz, gx, gy = (lax.axis_index(axis) for axis in ("gz", "gx", "gy"))
    planes = []
    for k in range(12):
        plane = correction[(gz * 4 + 28 + k) % 32]
        plane = pltpu.roll(plane, (32 - gx * 8) % 32, 0)
        plane = pltpu.roll(plane, (LANES - gy * 32) % LANES, 1)
        planes += [plane[0:14], plane[26:32]]
    flat = jnp.concatenate(planes, axis=0)
    fine = lane_of(flat.shape)
    flat = pick(flat, fine // 2 + jnp.where(fine < 96, 0, 64))
    count = 12 * 20
    tall[pl.ds(0, count, stride=2), :] = flat
    tall[pl.ds(1, count, stride=2), :] = flat
    for z in range(ZT1):
        k = (z + 1) // 2
        va1[z] = va1[z] + tall[k * XT1 : (k + 1) * XT1, :]
    far.wait(1)
    op1 = parts(stacked1, ZT1)
    sweep(va1, vb1, op1, 1, ZT1 - 1, 20)
    sweep(vb1, va1, op1, 2, ZT1 - 2, 18)
    sweep(va1, vb1, op1, 3, ZT1 - 3, 16)
    sweep(vb1, va1, op1, 4, ZT1 - 4, 14)
    planes = []
    for k in range(14):
        planes += [va1[4 + k, 0:20, :], va1[4 + k, XT1 - 4 : XT1, :]]
    flat = jnp.concatenate(planes, axis=0)
    for half in range(2):
        part = spread_lanes(flat, 64 * half)
        at = slice(half * LANES, (half + 1) * LANES)
        for z in range(ZT0):
            k = (z + 1) // 2
            add = part[k * EVEN : (k + 1) * EVEN, :]
            v0[z, 0:EVEN, at] = v0[z, 0:EVEN, at] + add
            v0[z, EVEN:, at] = v0[z, EVEN:, at] + add
    far.wait(2)
    op0 = parts(stacked0, ZT0)
    sweep(v0, vb0, op0, 1, ZT0 - 1, 12)
    sweep(vb0, v0, op0, 2, ZT0 - 2, 11)
    sweep(v0, vb0, op0, 3, ZT0 - 3, 10)
    sweep(vb0, v0, op0, 4, ZT0 - 4, 9)
    for z in range(Z0):
        potential[z, every_other(0, X1), :] = v0[W0 + z, 0:X1, 0:Y0]
        potential[z, every_other(1, X1), :] = v0[W0 + z, EVEN : EVEN + X1, 0:Y0]
    far.flush(0)
    for z in range(Z0):
        plane = remain(v0, op0, W0 + z)
        residual[z, every_other(0, X1), :] = plane[0:X1, 0:Y0]
        residual[z, every_other(1, X1), :] = plane[EVEN : EVEN + X1, 0:Y0]


def shards(source, conductivity, cell_kind):
    own0, own1 = (1, Z0, X0, Y0), (1, Z1, X1, LANES)
    ext0, ext1 = (ZT0, XT0, 2 * LANES), (ZT1, XT1, LANES)
    everywhere = ("gz", "gx", "gy")
    devices = math.prod(lax.axis_size(axis) for axis in everywhere)
    wet = jnp.where(cell_kind > 0, 1.0, 0.0).astype(F32)
    surface = jnp.where(cell_kind == 2, 1.0, 0.0).astype(F32)
    stiffness = conductivity * wet
    mass = 0.005 * stiffness + 8.0 * stiffness * surface + 0.02 * (1.0 - wet)
    fields = [array.reshape(own0) for array in (stiffness, source * wet, mass)]
    coarse, low, high = call(
        prepare, [own1] + [x_message(FIRST)] * 2, [(Z1 * X0, LANES)], *fields
    )

    def gather_coarse(message):
        block, _ = lax.optimization_barrier((coarse, message))
        (packed2,) = call(prepare_coarse, [(16, LANES)], [(Z1 // 2 * X1, LANES)], block)
        return lax.all_gather(packed2, everywhere, axis=0)

    received, operators2 = exchange(FIRST, (*fields, coarse), low, high, gather_coarse)
    v0, g1, op0, s1, m1, low, high = call(
        presmooth0,
        [own0, own1, (5 * ZT0, XT0, 2 * LANES)] + [ext1] * 2 + [x_message(SECOND)] * 2,
        [ext0] * 4 + [(Z1 * X0, LANES)],
        *received, far_out=(2,),
    )
    received = exchange(SECOND, (g1, v0), low, high)
    stack0, stack1 = (5 * ZT0, XT0, 2 * LANES), (5 * ZT1, XT1, LANES)
    stack2, stack34 = (128, 32, LANES), (40, 32, LANES)
    message = ((W0 + 1) * XT0 + W1 * XT1, LANES)
    v1, v0, copies, op1, low, high = call(
        presmooth1,
        [(Z1, XT1, LANES), (Z0, XT0, 2 * LANES), (devices, 8, LANES), stack1] + [message] * 2,
        [ext1] * 2 + [(Z1 // 2 * X1, LANES)],
        *received, s1, m1, far_out=(3,),
    )
    _, operators2 = lax.optimization_barrier((copies, operators2))
    forcing2 = lax.all_to_all(copies, everywhere, 0, 0)
    from_low, from_high = shift(low, high, "gz")
    level2, level3, level4 = (32, 32, LANES), (16, 16, LANES), (8, 8, LANES)
    operators, operators34 = call(
        coarse_operators,
        [stack2, stack34],
        [level2] * 2 + [level3] * 2 + [level4] * 2 + [(512, LANES)],
        operators2, far_in={0: operators2.shape}, far_out=(0, 1),
    )
    return call(
        finish,
        [(Z0, X0, Y0)] * 2,
        [ext1, ext1, ext0, ext0] + [level2] * 3 + [level3] * 3 + [level4] * 2 + [(14 * XT0, LANES)],
        operators, op1, op0, operators34, forcing2, v1, v0, from_low, from_high,
        far_in={0: stack2, 1: stack1, 2: stack0, 3: stack34}, late=(1, 2),
        far_out=(0, 1), pad=False,
    )


def solution(mesh):
    spec = P("gz", "gx", "gy")
    return jax.shard_map(
        shards, mesh=mesh, in_specs=(spec,) * 3, out_specs=(spec,) * 2, check_vma=False
    )
```

```python
import math

import jax
import jax.numpy as jnp
from jax import lax
from jax.experimental import pallas as pl
from jax.experimental.pallas import tpu as pltpu
from jax.sharding import PartitionSpec as P

CSWEEPS = 32
DAMP = 0.8
KEEP = 1.0 - DAMP
W0 = 5
W1 = 7
G1 = 6
S1, F1 = 11, 10
Z0, X0, Y0 = 16, 32, 128
Z1, X1, Y1 = 8, 16, 64
ZT0, XT0, EVEN = Z0 + 2 * W0, 48, 24
ZT1, XT1 = Z1 + 2 * W1, 40
LANES = 128
MIB = 1024 * 1024
F32 = jnp.float32


def lane_of(shape):
    return lax.broadcasted_iota(jnp.int32, shape, len(shape) - 1)


def row_of(shape):
    return lax.broadcasted_iota(jnp.int32, shape, len(shape) - 2)


def roll(x, shift, axis):
    size = x.shape[axis]
    shift = shift % size
    return x if shift == 0 else pltpu.roll(x, shift, axis)


def loop(first, last, body, step):
    chunks = (last - first) // step

    def chunk(c, carry):
        for k in range(step):
            body(first + c * step + k)
        return carry

    if chunks > 1:
        lax.fori_loop(0, chunks, chunk, 0)
    elif chunks:
        chunk(0, 0)
    for z in range(first + chunks * step, last):
        body(z)


def pick(x, index):
    return jnp.take_along_axis(x, index, axis=1)


def fold_lanes(x, first, count, target):
    to = lane_of(x.shape) - target
    index = (first + 2 * to) % LANES
    pairs = pick(x, index) + pick(x, (index + 1) % LANES)
    return jnp.where((to >= 0) & (to < count // 2), pairs, 0.0)


def spread_lanes(x, first=0):
    return pick(x, first + lane_of(x.shape) // 2)


class Far:
    def __init__(self, ins, outs, late):
        self.ins = {k: pltpu.make_async_copy(*pair) for k, pair in ins.items()}
        self.outs = {k: pltpu.make_async_copy(*pair) for k, pair in outs.items()}
        self.started = []
        self.start(*[k for k in self.ins if k not in late])

    def start(self, *keys):
        for k in keys:
            self.ins[k].start()

    def wait(self, *keys):
        for k in keys or tuple(self.ins):
            self.ins.pop(k).wait()

    def flush(self, *keys):
        for k in keys:
            self.outs[k].start()
            self.started.append(k)

    def finish(self):
        self.flush(*[k for k in self.outs if k not in self.started])
        for copy in self.outs.values():
            copy.wait()


def padded(shape):
    plane = 4 * math.prod(shape[1:])
    return (max(shape[0], -(-7 * MIB // plane)), *shape[1:])


def call(body, outs, scratch, *args, far_in={}, far_out=(), late=(), grant=48, pad=True):
    shapes = [
        jax.ShapeDtypeStruct(padded(shape) if pad and k in far_out else shape, F32)
        for k, shape in enumerate(outs)
    ]
    vmem = pl.BlockSpec(memory_space=pltpu.VMEM)
    hbm = pl.BlockSpec(memory_space=pltpu.HBM)
    specs = [hbm if k in far_in else vmem for k in range(len(args))]
    out_specs = [hbm if k in far_out else vmem for k in range(len(outs))]
    held = [pltpu.VMEM(shape, F32) for shape in far_in.values()]
    held += [pltpu.VMEM(outs[k], F32) for k in far_out]
    extra = len(far_in) + len(far_out)
    if extra:
        held.append(pltpu.SemaphoreType.DMA((extra,)))
    count = len(args)

    def wrapped(*refs):
        refs = list(refs)
        ins, results = refs[:count], refs[count : count + len(outs)]
        rest = refs[count + len(outs) :]
        mine, rest = rest[: len(scratch)], rest[len(scratch) :]
        copies_in, copies_out = {}, {}
        for j, k in enumerate(far_in):
            copies_in[k] = (ins[k].at[0 : far_in[k][0]], rest[j], rest[extra].at[j])
            ins[k] = rest[j]
        for j, k in enumerate(far_out, len(far_in)):
            copies_out[k] = (rest[j], results[k].at[0 : outs[k][0]], rest[extra].at[j])
            results[k] = rest[j]
        far = Far(copies_in, copies_out, late)
        body(far, *ins, *results, *mine)
        far.finish()

    return pl.pallas_call(
        wrapped,
        out_shape=shapes,
        in_specs=specs,
        out_specs=out_specs,
        scratch_shapes=[pltpu.VMEM(shape, F32) for shape in scratch] + held,
        compiler_params=pltpu.CompilerParams(vmem_limit_bytes=grant * MIB),
    )(*args)


class Item:
    def __init__(self, fields, planes, rows, rows_out, width, kind, trim=False, width_z=None, edge=0):
        self.n, self.z, self.x, self.xt, self.w, self.kind = fields, planes, rows, rows_out, width, kind
        self.wz = width if width_z is None else width_z
        self.zt = planes + 2 * self.wz
        self.edge = edge
        self.trim = trim
        self.tall = rows + 8 if trim else rows_out
        self.virtual = 2 * fields if kind == "pair" else fields
        self.own = LANES if kind == "full" else LANES // 2
        self.slots = LANES // width
        self.groups = -(-self.virtual * (self.zt - 2 * edge) // self.slots)
        self.rows_x = fields * planes * width
        self.rows_z = fields * self.wz * self.tall
        self.rows_y = self.groups * self.tall

    def narrow(self, plane):
        if not self.trim:
            return plane
        even, odd = plane[16:24], plane[40:48]
        rim = jnp.where(reached(even), even, roll(odd, 4, 0))
        return jnp.concatenate([plane[0:16], plane[24:40], rim], axis=0)

    def widen(self, plane):
        if not self.trim:
            return plane
        rim = plane[32:40]
        even = jnp.where(reached(rim), rim, 0.0)
        odd = jnp.where(reached(rim), roll(rim, 4, 0), 0.0)
        return jnp.concatenate([plane[0:16], even, plane[16:32], odd], axis=0)


def reached(rim):
    return (row_of(rim.shape) < 2) | (row_of(rim.shape) >= 6)


def every_other(first, count):
    return pl.ds(first, count, stride=2)


def total(counts):
    count = sum(counts)
    return -(-count // 8) * 8


def pack_x(items, refs, low, high):
    at = 0
    for item, ref in zip(items, refs):
        for n in range(item.n):
            for z in range(item.z):
                low[at : at + item.w, :] = ref[n, z, 0 : item.w, :]
                high[at : at + item.w, :] = ref[n, z, item.x - item.w : item.x, :]
                at += item.w


def unpack_x(items, refs, from_low, from_high, outs):
    at = 0
    for item, ref, out in zip(items, refs, outs):
        w = item.w
        if item.kind == "full":
            for first in (16, 40):
                out[:, :, first : first + 8, :] = jnp.zeros((item.n, item.z, 8, LANES), F32)
        else:
            out[:, :, item.x :, :] = jnp.zeros((item.n, item.z, item.xt - item.x, LANES), F32)
        for n in range(item.n):
            for z in range(item.z):
                if item.kind == "full":
                    more, less = (w + 1) // 2, w // 2
                    out[n, z, 0:16, :] = ref[n, z, every_other(0, 16), :]
                    out[n, z, 24:40, :] = ref[n, z, every_other(1, 16), :]
                    out[n, z, 16 : 16 + more, :] = from_high[every_other(at, more), :]
                    out[n, z, 40 : 40 + less, :] = from_high[every_other(at + 1, less), :]
                    out[n, z, 24 - less : 24, :] = from_low[every_other(at + w % 2, less), :]
                    out[n, z, 48 - more : 48, :] = from_low[every_other(at + 1 - w % 2, more), :]
                else:
                    out[n, z, 0 : item.x, :] = ref[n, z]
                    out[n, z, item.x : item.x + w, :] = from_high[at : at + w, :]
                    out[n, z, item.xt - w :, :] = from_low[at : at + w, :]
                at += w


def pack_z(items, refs, low, high):
    at = 0
    for item, ref in zip(items, refs):
        for n in range(item.n):
            for w in range(item.wz):
                low[at : at + item.tall, :] = item.narrow(ref[n, w])
                high[at : at + item.tall, :] = item.narrow(ref[n, item.z - item.wz + w])
                at += item.tall


class Planes:
    def __init__(self, item, ref, from_low, from_high, base):
        self.item, self.ref, self.low, self.high, self.base = item, ref, from_low, from_high, base

    def received(self, n, z):
        item = self.item
        if item.wz <= z < item.wz + item.z:
            return None
        message, w = (self.low, z) if z < item.wz else (self.high, z - item.wz - item.z)
        at = self.base + (n * item.wz + w) * item.tall
        return message[at : at + item.tall, :]

    def whole(self, n, z):
        plane = self.received(n, z)
        return self.ref[n, z - self.item.wz] if plane is None else self.item.widen(plane)

    def narrow(self, n, z):
        plane = self.received(n, z)
        return self.item.narrow(self.ref[n, z - self.item.wz]) if plane is None else plane


def planes_of(items, refs, from_low, from_high):
    planes, base = [], 0
    for item, ref in zip(items, refs):
        planes.append(Planes(item, ref, from_low, from_high, base))
        base += item.rows_z
    return planes


def pack_y(items, sources, low, high):
    at = 0
    for item, source in zip(items, sources):
        lane = lane_of((item.tall, LANES))
        pairs = [(v, z) for v in range(item.virtual) for z in range(item.edge, item.zt - item.edge)]
        for g in range(item.groups):
            lows = jnp.zeros((item.tall, LANES), F32)
            highs = lows
            for k, (v, z) in enumerate(pairs[g * item.slots : (g + 1) * item.slots]):
                n, first = (v // 2, (v % 2) * item.own) if item.kind == "pair" else (v, 0)
                plane = source.narrow(n, z)
                place = k * item.w
                mask = (lane >= place) & (lane < place + item.w)
                lows = jnp.where(mask, roll(plane, place - first, 1), lows)
                highs = jnp.where(mask, roll(plane, place - first - item.own + item.w, 1), highs)
            low[at : at + item.tall, :] = lows
            high[at : at + item.tall, :] = highs
            at += item.tall


def unpack_y(items, sources, from_low, from_high, outs):
    at = 0
    for item, source, fields in zip(items, sources, outs):
        lane = lane_of((item.tall, LANES))
        for v in range(item.virtual if item.edge else 0):
            for z in [*range(item.edge), *range(item.zt - item.edge, item.zt)]:
                fields[v][z, :, 0:LANES] = source.whole(v, z)
                fields[v][z, :, LANES:] = jnp.zeros((item.xt, LANES), F32)
        pairs = [(v, z) for v in range(item.virtual) for z in range(item.edge, item.zt - item.edge)]
        for g in range(item.groups):
            lows = from_low[at : at + item.tall, :]
            highs = from_high[at : at + item.tall, :]
            at += item.tall
            for k, (v, z) in enumerate(pairs[g * item.slots : (g + 1) * item.slots]):
                place = k * item.w
                start = item.own % LANES
                upper = roll(highs, start - place, 1)
                lower = roll(lows, LANES - item.w - place, 1)
                rim = jnp.where(
                    lane < start + item.w, upper, jnp.where(lane >= LANES - item.w, lower, 0.0)
                )
                if item.kind == "full":
                    fields[v][z, :, 0:LANES] = source.whole(v, z)
                    fields[v][z, :, LANES:] = item.widen(rim)
                else:
                    plane = source.whole(v // 2 if item.kind == "pair" else v, z)
                    if item.kind == "pair" and v % 2:
                        plane = roll(plane, item.own, 1)
                    fields[v][z] = jnp.where(lane < item.own, plane, rim)


def shift(low, high, axis):
    count = lax.axis_size(axis)
    forward = [(i, i + 1) for i in range(count - 1)]
    backward = [(target, source) for source, target in forward]
    return lax.ppermute(high, axis, forward), lax.ppermute(low, axis, backward)


def exchange(items, arrays, low, high, beside=None):
    count = len(items)
    from_low, from_high = shift(low, high, "gx")
    shapes = [(item.n, item.z, item.xt, LANES) for item in items]
    message = (total(item.rows_z for item in items), LANES)

    def after_x(far, *refs):
        ins, (a, b), outs, (c, d) = refs[:count], refs[count : count + 2], refs[count + 2 : 2 * count + 2], refs[2 * count + 2 :]
        unpack_x(items, ins, a, b, outs)
        pack_z(items, outs, c, d)

    *arrays, low, high = call(after_x, shapes + [message] * 2, [], *arrays, from_low, from_high)
    extra = beside(low) if beside else None
    z_low, z_high = shift(low, high, "gz")
    message = (total(item.rows_y for item in items), LANES)

    def after_z(far, *refs):
        pack_y(items, planes_of(items, refs[:count], *refs[count : count + 2]), *refs[count + 2 :])

    low, high = call(after_z, [message] * 2, [], *arrays, z_low, z_high)
    received = (*arrays, z_low, z_high, *shift(low, high, "gy"))
    return (received, extra) if beside else received


STIFFNESS = Item(1, Z0, X0, XT0, W0, "full", True, edge=1)
INNER = Item(1, Z0, X0, XT0, W0 - 1, "full", True)
COARSE = Item(1, Z1, X1, XT1, S1, "pair", False, W1)
FORCING1 = Item(1, Z1, X1, XT1, F1, "half", False, G1)
POTENTIAL0 = Item(1, Z0, X0, XT0, W0, "full", False, 0)
FIRST, SECOND = (STIFFNESS, INNER, INNER, COARSE), (FORCING1, POTENTIAL0)


def x_message(items):
    return (total(item.rows_x for item in items), LANES)


def x_above(plane):
    if plane.shape[0] != XT0:
        return roll(plane, -1, 0)
    return jnp.concatenate([plane[EVEN:], roll(plane[:EVEN], -1, 0)], axis=0)


def x_below(plane):
    if plane.shape[0] != XT0:
        return roll(plane, 1, 0)
    return jnp.concatenate([roll(plane[EVEN:], 1, 0), plane[:EVEN]], axis=0)


def couple(s, m, r, cx, cy, cz, first, last, step, edges=False, start=None):
    planes, rows, lanes = s.shape

    def vertical(z):
        return 4.0 * jnp.minimum(s[z], s[z + 1])

    def one(z, below, above):
        here = s[z]
        x_face = jnp.minimum(here, x_above(here))
        y_face = jnp.minimum(here, roll(here, -1, 1))
        if edges:
            x_face = jnp.where(row_of(here.shape) < rows - 1, x_face, 0.0)
            y_face = jnp.where(lane_of(here.shape) < lanes - 1, y_face, 0.0)
        cx[z] = x_face
        cy[z] = y_face
        cz[z] = above
        d = m[z] + below + above + x_face + x_below(x_face) + y_face + roll(y_face, 1, 1)
        scale = DAMP / jnp.where(d > 0.0, d, 1.0)
        r[z] = scale
        if start:
            start[1][z] = scale * start[0][z]

    if edges:
        zero = jnp.zeros((rows, lanes), F32)
        one(0, zero, vertical(0))
        one(planes - 1, vertical(planes - 2), zero)
    else:
        cz[first - 1] = vertical(first - 1)
    loop(first + edges, last - edges, lambda z: one(z, vertical(z - 1), vertical(z)), step)


def gathered(v, f, cx, cy, cz, z, low=True, high=True):
    here = v[z]
    x_face, y_face = cx[z], cy[z]
    out = f[z]
    if high:
        out = out + cz[z] * v[z + 1]
    if low:
        out = out + cz[z - 1] * v[z - 1]
    out = out + x_face * x_above(here) + x_below(x_face * here)
    return here, out + y_face * roll(here, -1, 1) + roll(y_face * here, 1, 1)


def sweep(v, into, op, first, last, unroll, edges=False):
    r, f, cx, cy, cz = op

    def step(z, low=True, high=True):
        here, out = gathered(v, f, cx, cy, cz, z, low, high)
        into[z] = KEEP * here + r[z] * out

    if edges:
        step(first, low=False)
        step(last - 1, high=False)
        loop(first + 1, last - 1, step, unroll)
    else:
        loop(first, last, step, unroll)


def remain(v, op, z, low=True, high=True):
    r, f, cx, cy, cz = op
    here, out = gathered(v, f, cx, cy, cz, z, low, high)
    return out - here * (DAMP / r[z])


def first_sweep(v, op, first, last):
    r, f = op[:2]

    def step(z):
        v[z] = r[z] * f[z]

    loop(first, last, step, 4)


def prepare(far, stiffness, forcing, mass, coarse, low, high, tall):
    out = None
    for ref, scale, target in ((stiffness, 0.25, 0), (mass, 1.0, Y1)):
        for z in range(Z1):
            tall[z * X0 : (z + 1) * X0, :] = ref[0, 2 * z] + ref[0, 2 * z + 1]
        rows = tall[pl.ds(0, Z1 * X1, stride=2), :] + tall[pl.ds(1, Z1 * X1, stride=2), :]
        part = scale * fold_lanes(rows, 0, LANES, target)
        out = part if out is None else out + part
    for z in range(Z1):
        coarse[0, z] = out[z * X1 : (z + 1) * X1, :]
    pack_x(FIRST, (stiffness, forcing, mass, coarse), low, high)


def prepare_coarse(far, coarse, packed2, tall):
    for part, scale in ((0, 0.25), (1, 1.0)):
        packed2[part * 8 : part * 8 + 8, :] = scale * pack_coarse(
            lambda z: coarse[0, z], part * Y1, tall
        )


def pack_coarse(plane, first, tall):
    for z in range(Z1 // 2):
        tall[z * X1 : (z + 1) * X1, :] = plane(2 * z) + plane(2 * z + 1)
    count = Z1 // 2 * X1 // 2
    rows = tall[pl.ds(0, count, stride=2), :] + tall[pl.ds(1, count, stride=2), :]
    out = jnp.zeros((X1 // 2, LANES), F32)
    for z in range(Z1 // 2):
        part = rows[z * X1 // 2 : (z + 1) * X1 // 2, :]
        out = out + fold_lanes(part, first, Y1, z * Y1 // 2)
    return out


def parts(ref, planes, count=5):
    return [ref.at[k * planes : (k + 1) * planes] for k in range(count)]


def presmooth0(
    far, x_s, x_f, x_m, x_coarse, z_low, z_high, from_low, from_high,
    v_own, g_own, op, s1, m1, low, high,
    s, m, va, vb, tall,
):
    r, f, cx, cy, cz = parts(op, ZT0)
    inner = slice(1, ZT0 - 1)
    unpack_y(
        FIRST, planes_of(FIRST, (x_s, x_f, x_m, x_coarse), z_low, z_high), from_low, from_high,
        ([s], [f.at[inner]], [m.at[inner]], [s1, m1]),
    )
    couple(s, m, r, cx, cy, cz, 1, ZT0 - 1, 8, start=(f, va))
    far.flush(2)
    op = (r, f, cx, cy, cz)
    sweep(va, vb, op, 2, ZT0 - 2, 11)
    sweep(vb, va, op, 3, ZT0 - 3, 10)
    sweep(va, vb, op, 4, ZT0 - 4, 9)
    rows = []
    for z in range(Z1):
        plane = remain(vb, op, W0 + 2 * z) + remain(vb, op, W0 + 2 * z + 1)
        rows.append(plane[0:X1, 0:Y0] + plane[EVEN : EVEN + X1, 0:Y0])
    out = fold_lanes(jnp.concatenate(rows, axis=0), 0, LANES, 0)
    for z in range(Z1):
        g_own[0, z] = out[z * X1 : (z + 1) * X1, :]
    for z in range(Z0):
        v_own[0, z, every_other(0, X1), :] = vb[W0 + z, 0:X1, 0:Y0]
        v_own[0, z, every_other(1, X1), :] = vb[W0 + z, EVEN : EVEN + X1, 0:Y0]
    pack_x(SECOND, (g_own, v_own), low, high)


def presmooth1(
    far, g_x, v0_x, z_low, z_high, from_low, from_high, s, m,
    v_own, v0, copies, op, low, high,
    va, vb, tall,
):
    r, g, cx, cy, cz = parts(op, ZT1)
    for k in range(W1 - G1):
        g[k] = jnp.zeros((XT1, LANES), F32)
        g[ZT1 - 1 - k] = jnp.zeros((XT1, LANES), F32)
    inner = g.at[W1 - G1 : ZT1 - (W1 - G1)]
    unpack_y(SECOND, planes_of(SECOND, (g_x, v0_x), z_low, z_high), from_low, from_high, ([inner], [v0]))
    couple(s, m, r, cx, cy, cz, 1, ZT1 - 1, 10, start=(g, va))
    far.flush(3)
    op = (r, g, cx, cy, cz)
    sweep(va, vb, op, 4, ZT1 - 4, 10)
    sweep(vb, va, op, 5, ZT1 - 5, 10)
    sweep(va, vb, op, 6, ZT1 - 6, 10)
    packed = pack_coarse(lambda z: remain(vb, op, W1 + z)[0:X1, :], 0, tall)
    for d in range(copies.shape[0]):
        copies[d] = packed
    for z in range(Z1):
        v_own[z] = vb[W1 + z]
    lane = lane_of((XT0, LANES))
    base = (W0 + 1) * XT0
    for message, first0, first1 in ((low, 0, 0), (high, Z0 - W0, Z1 - W1)):
        rims = jnp.zeros((XT0, LANES), F32)
        for w in range(W0):
            message[w * XT0 : (w + 1) * XT0, :] = v0[first0 + w, :, 0:LANES]
            here = (lane >= 2 * W0 * w) & (lane < 2 * W0 * (w + 1))
            rims = jnp.where(here, roll(v0[first0 + w, :, LANES:], W0 + 2 * W0 * w, 1), rims)
        message[W0 * XT0 : base, :] = rims
        for w in range(W1):
            message[base + w * XT1 : base + (w + 1) * XT1, :] = v_own[first1 + w]


def unpack_whole(blocks, first, out):
    group = lane_of((8, LANES)) // 32

    def body(step):
        gz, gx = step // 4, step % 4
        for z in range(4):
            plane = None
            for gy in range(4):
                block = blocks[step * 4 + gy, first : first + 8, :]
                moved = roll(block, (gy - z) * 32, 1)
                plane = moved if plane is None else jnp.where(group == gy, moved, plane)
            out[gz * 4 + z, pl.ds(pl.multiple_of(gx * 8, 8), 8), :] = plane

    loop(0, 32, body, 4)


def fold_whole(plane, planes, rows, scale, tall, out):
    half = rows // 2
    for z in range(planes // 2):
        tall[z * rows : (z + 1) * rows, :] = plane(2 * z) + plane(2 * z + 1)
    count = planes // 2 * half
    folded = tall[pl.ds(0, count, stride=2), :] + tall[pl.ds(1, count, stride=2), :]
    folded = scale * fold_lanes(folded, 0, LANES, 0)
    for z in range(planes // 2):
        out[z] = folded[z * half : (z + 1) * half, :]


def spread_whole(v, planes, rows, tall, add):
    count = planes * rows
    flat = spread_lanes(jnp.concatenate([v[z] for z in range(planes)], axis=0))
    tall[pl.ds(0, count, stride=2), :] = flat
    tall[pl.ds(1, count, stride=2), :] = flat
    for z in range(planes):
        spread = tall[z * 2 * rows : (z + 1) * 2 * rows, :]
        add[2 * z] = add[2 * z] + spread
        add[2 * z + 1] = add[2 * z + 1] + spread


def coarsest(out, op):
    r, f, cx, cy, cz = op
    forced, upper, lower = [], [], []
    for z in range(8):
        scale = r[z]
        forced.append(scale * f[z])
        above = scale * cz[z]
        below = scale * cz[z - 1] if z else None
        upper.append((above, scale * cx[z], scale * cy[z]))
        lower.append((below, scale * roll(cx[z], 1, 0), scale * roll(cy[z], 1, 1)))

    def step(k, v):
        new = []
        for z in range(8):
            here = v[z]
            east = upper[z][2] * roll(here, -1, 1) + lower[z][2] * roll(here, 1, 1)
            north = upper[z][1] * roll(here, -1, 0) + lower[z][1] * roll(here, 1, 0)
            base = KEEP * here + forced[z]
            if z < 7:
                base = base + upper[z][0] * v[z + 1]
            if z:
                base = base + lower[z][0] * v[z - 1]
            new.append((base + north) + east)
        return tuple(new)

    v = lax.fori_loop(0, CSWEEPS - 1, step, tuple(forced), unroll=True)
    for z in range(8):
        out[z] = v[z]


def levels(stacked2, stacked34):
    level3 = [stacked34.at[16 * (k // 2) : 16 * (k // 2) + 16, 16 * (k % 2) : 16 * (k % 2) + 16, :] for k in range(4)]
    level4 = [stacked34.at[32:40, 8 * k : 8 * k + 8, :] for k in range(4)]
    return parts(stacked2, 32, 4), level3, level4


def coarse_operators(
    far, operators,
    stacked2, stacked34,
    s2, m2, s3, m3, s4, m4, tall,
):
    (r2, cx2, cy2, cz2), (r3, cx3, cy3, cz3), (r4, cx4, cy4, cz4) = levels(stacked2, stacked34)
    far.wait()
    unpack_whole(operators, 0, s2)
    unpack_whole(operators, 8, m2)
    couple(s2, m2, r2, cx2, cy2, cz2, 0, 32, 10, True)
    far.flush(0)
    fold_whole(lambda z: s2[z], 32, 32, 0.25, tall, s3)
    fold_whole(lambda z: m2[z], 32, 32, 1.0, tall, m3)
    couple(s3, m3, r3, cx3, cy3, cz3, 0, 16, 14, True)
    fold_whole(lambda z: s3[z], 16, 16, 0.25, tall, s4)
    fold_whole(lambda z: m3[z], 16, 16, 1.0, tall, m4)
    couple(s4, m4, r4, cx4, cy4, cz4, 0, 8, 6, True)


def coarse_cycle(
    far, forcing, stacked2, stacked34, out,
    f2, vb2, f3, va3, vb3, f4, vb4, tall, meanwhile,
):
    unpack_whole(forcing, 0, f2)
    far.wait(0, 3)
    far.start(1, 2)
    (r2, cx2, cy2, cz2), (r3, cx3, cy3, cz3), (r4, cx4, cy4, cz4) = levels(stacked2, stacked34)
    op2 = (r2, f2, cx2, cy2, cz2)
    op3 = (r3, f3, cx3, cy3, cz3)
    op4 = (r4, f4, cx4, cy4, cz4)
    va2 = out

    def four(va, vb, op, planes):
        sweep(va, vb, op, 0, planes, 30, True)
        sweep(vb, va, op, 0, planes, 30, True)

    def residue(v, op, planes):
        return lambda z: remain(v, op, z, z > 0, z < planes - 1)

    first_sweep(vb2, op2, 0, 32)
    sweep(vb2, va2, op2, 0, 32, 30, True)
    four(va2, vb2, op2, 32)
    fold_whole(residue(va2, op2, 32), 32, 32, 1.0, tall, f3)
    first_sweep(vb3, op3, 0, 16)
    sweep(vb3, va3, op3, 0, 16, 15, True)
    four(va3, vb3, op3, 16)
    fold_whole(residue(va3, op3, 16), 16, 16, 1.0, tall, f4)
    meanwhile()
    coarsest(vb4, op4)
    spread_whole(vb4, 8, 8, tall, va3)
    four(va3, vb3, op3, 16)
    four(va3, vb3, op3, 16)
    spread_whole(va3, 16, 16, tall, va2)
    four(va2, vb2, op2, 32)
    four(va2, vb2, op2, 32)


def finish(
    far, stacked2, stacked1, stacked0, stacked34, forcing, v1, v0_zx, from_low, from_high,
    potential, residual,
    va1, vb1, v0, vb0, correction, f2, vb2, f3, va3, vb3, f4, vb4, tall,
):
    def meanwhile():
        base = (W0 + 1) * XT0
        for message, first0, first1 in ((from_low, 0, 0), (from_high, W0 + Z0, W1 + Z1)):
            rims = message[W0 * XT0 : base, :]
            for w in range(W0):
                v0[first0 + w, :, 0:LANES] = message[w * XT0 : (w + 1) * XT0, :]
                v0[first0 + w, :, LANES:] = roll(rims, -W0 - 2 * W0 * w, 1)
            for w in range(W1):
                va1[first1 + w] = message[base + w * XT1 : base + (w + 1) * XT1, :]
        for z in range(Z0):
            v0[W0 + z] = v0_zx[z]
        for z in range(Z1):
            va1[W1 + z] = v1[z]

    coarse_cycle(far, forcing, stacked2, stacked34, correction, f2, vb2, f3, va3, vb3, f4, vb4, tall, meanwhile)
    gz, gx, gy = (lax.axis_index(axis) for axis in ("gz", "gx", "gy"))
    planes = []
    for k in range(12):
        plane = correction[(gz * 4 + 28 + k) % 32]
        plane = pltpu.roll(plane, (32 - gx * 8) % 32, 0)
        plane = pltpu.roll(plane, (LANES - gy * 32) % LANES, 1)
        planes += [plane[0:14], plane[26:32]]
    flat = jnp.concatenate(planes, axis=0)
    fine = lane_of(flat.shape)
    flat = pick(flat, fine // 2 + jnp.where(fine < 96, 0, 64))
    count = 12 * 20
    tall[pl.ds(0, count, stride=2), :] = flat
    tall[pl.ds(1, count, stride=2), :] = flat
    for z in range(ZT1):
        k = (z + 1) // 2
        va1[z] = va1[z] + tall[k * XT1 : (k + 1) * XT1, :]
    far.wait(1)
    op1 = parts(stacked1, ZT1)
    sweep(va1, vb1, op1, 1, ZT1 - 1, 20)
    sweep(vb1, va1, op1, 2, ZT1 - 2, 18)
    sweep(va1, vb1, op1, 3, ZT1 - 3, 16)
    sweep(vb1, va1, op1, 4, ZT1 - 4, 14)
    planes = []
    for k in range(14):
        planes += [va1[4 + k, 0:20, :], va1[4 + k, XT1 - 4 : XT1, :]]
    flat = jnp.concatenate(planes, axis=0)
    for half in range(2):
        part = spread_lanes(flat, 64 * half)
        at = slice(half * LANES, (half + 1) * LANES)
        for z in range(ZT0):
            k = (z + 1) // 2
            add = part[k * EVEN : (k + 1) * EVEN, :]
            v0[z, 0:EVEN, at] = v0[z, 0:EVEN, at] + add
            v0[z, EVEN:, at] = v0[z, EVEN:, at] + add
    far.wait(2)
    op0 = parts(stacked0, ZT0)
    sweep(v0, vb0, op0, 1, ZT0 - 1, 12)
    sweep(vb0, v0, op0, 2, ZT0 - 2, 11)
    sweep(v0, vb0, op0, 3, ZT0 - 3, 10)
    sweep(vb0, v0, op0, 4, ZT0 - 4, 9)
    for z in range(Z0):
        potential[z, every_other(0, X1), :] = v0[W0 + z, 0:X1, 0:Y0]
        potential[z, every_other(1, X1), :] = v0[W0 + z, EVEN : EVEN + X1, 0:Y0]
    far.flush(0)
    for z in range(Z0):
        plane = remain(v0, op0, W0 + z)
        residual[z, every_other(0, X1), :] = plane[0:X1, 0:Y0]
        residual[z, every_other(1, X1), :] = plane[EVEN : EVEN + X1, 0:Y0]


def shards(source, conductivity, cell_kind):
    own0, own1 = (1, Z0, X0, Y0), (1, Z1, X1, LANES)
    ext0, ext1 = (ZT0, XT0, 2 * LANES), (ZT1, XT1, LANES)
    everywhere = ("gz", "gx", "gy")
    devices = math.prod(lax.axis_size(axis) for axis in everywhere)
    wet = jnp.where(cell_kind > 0, 1.0, 0.0).astype(F32)
    surface = jnp.where(cell_kind == 2, 1.0, 0.0).astype(F32)
    stiffness = conductivity * wet
    mass = 0.005 * stiffness + 8.0 * stiffness * surface + 0.02 * (1.0 - wet)
    fields = [array.reshape(own0) for array in (stiffness, source * wet, mass)]
    coarse, low, high = call(
        prepare, [own1] + [x_message(FIRST)] * 2, [(Z1 * X0, LANES)], *fields
    )

    def gather_coarse(message):
        block, _ = lax.optimization_barrier((coarse, message))
        (packed2,) = call(prepare_coarse, [(16, LANES)], [(Z1 // 2 * X1, LANES)], block)
        return lax.all_gather(packed2, everywhere, axis=0)

    received, operators2 = exchange(FIRST, (*fields, coarse), low, high, gather_coarse)
    v0, g1, op0, s1, m1, low, high = call(
        presmooth0,
        [own0, own1, (5 * ZT0, XT0, 2 * LANES)] + [ext1] * 2 + [x_message(SECOND)] * 2,
        [ext0] * 4 + [(Z1 * X0, LANES)],
        *received, far_out=(2,),
    )
    received = exchange(SECOND, (g1, v0), low, high)
    stack0, stack1 = (5 * ZT0, XT0, 2 * LANES), (5 * ZT1, XT1, LANES)
    stack2, stack34 = (128, 32, LANES), (40, 32, LANES)
    message = ((W0 + 1) * XT0 + W1 * XT1, LANES)
    v1, v0, copies, op1, low, high = call(
        presmooth1,
        [(Z1, XT1, LANES), (Z0, XT0, 2 * LANES), (devices, 8, LANES), stack1] + [message] * 2,
        [ext1] * 2 + [(Z1 // 2 * X1, LANES)],
        *received, s1, m1, far_out=(3,),
    )
    _, operators2 = lax.optimization_barrier((copies, operators2))
    forcing2 = lax.all_to_all(copies, everywhere, 0, 0)
    from_low, from_high = shift(low, high, "gz")
    level2, level3, level4 = (32, 32, LANES), (16, 16, LANES), (8, 8, LANES)
    operators, operators34 = call(
        coarse_operators,
        [stack2, stack34],
        [level2] * 2 + [level3] * 2 + [level4] * 2 + [(512, LANES)],
        operators2, far_in={0: operators2.shape}, far_out=(0, 1),
    )
    return call(
        finish,
        [(Z0, X0, Y0)] * 2,
        [ext1, ext1, ext0, ext0] + [level2] * 3 + [level3] * 3 + [level4] * 2 + [(14 * XT0, LANES)],
        operators, op1, op0, operators34, forcing2, v1, v0, from_low, from_high,
        far_in={0: stack2, 1: stack1, 2: stack0, 3: stack34}, late=(1, 2),
        far_out=(0, 1), pad=False,
    )


def solution(mesh):
    spec = P("gz", "gx", "gy")
    return jax.shard_map(
        shards, mesh=mesh, in_specs=(spec,) * 3, out_specs=(spec,) * 2, check_vma=False
    )
```
